32 devices in a mesh: dp: 8 (over z, y), mp: 4 (over x, core).
Axes of the slice: x: 2, y: 2, z: 4, core: 2. Of those that a mesh axis runs over, the one named last changes fastest.
Arguments:
- inputs: bfloat16 [4096, 1024], P('dp'), may hold values from -6 to 6
- lengths: int32 [8, 4], P('dp'), may hold values from 0 to 512, as said below
- out_grad: bfloat16 [4096, 1024], P('dp'), may hold values from -6 to 6
- first_norm: float32 [1024], P('dp'), may hold values from 0.5 to 1.5
- first_up: float32 [1024, 4096], P('dp', 'mp'), may hold values from -0.1875 to 0.1875
- first_down: float32 [1024, 4096], P('dp', 'mp'), may hold values from -0.1875 to 0.1875
- attention_norm: float32 [1024], P('dp'), may hold values from 0.5 to 1.5
- query_weight: float32 [1024, 1024], P('dp', 'mp'), may hold values from -0.1875 to 0.1875
- key_weight: float32 [1024, 1024], P('dp', 'mp'), may hold values from -0.1875 to 0.1875
- value_weight: float32 [1024, 1024], P('dp', 'mp'), may hold values from -0.1875 to 0.1875
- position_weight: float32 [1024, 1024], P('dp', 'mp'), may hold values from -0.1875 to 0.1875
- output_weight: float32 [1024, 1024], P('dp', 'mp'), may hold values from -0.75 to 0.75
- content_bias: float32 [128, 8], P('dp', 'mp'), may hold values from -3 to 3
- position_bias: float32 [128, 8], P('dp', 'mp'), may hold values from -3 to 3
- convolution_norm: float32 [1024], P('dp'), may hold values from 0.5 to 1.5
- pointwise_in: float32 [1024, 2, 1024], P('dp', None, 'mp'), may hold values from -0.1875 to 0.1875
- depthwise_kernel: float32 [1024, 5], P(('mp', 'dp')), may hold values from -2.5 to 2.5
- batch_gain: float32 [1024], P(('mp', 'dp')), may hold values from 0.5 to 1.5
- batch_shift: float32 [1024], P(('mp', 'dp')), may hold values from -3 to 3
- pointwise_out: float32 [1024, 1024], P('dp', 'mp'), may hold values from -0.375 to 0.375
- second_norm: float32 [1024], P('dp'), may hold values from 0.5 to 1.5
- second_up: float32 [1024, 4096], P('dp', 'mp'), may hold values from -0.1875 to 0.1875
- second_down: float32 [1024, 4096], P('dp', 'mp'), may hold values from -0.1875 to 0.1875
- final_norm: float32 [1024], P('dp'), may hold values from 0.5 to 1.5
Outputs:
- result: bfloat16 [4096, 1024], P('dp')
- inputs_grad: float32 [4096, 1024], P('dp')
- first_norm_grad: float32 [1024], P('dp')
- first_up_grad: float32 [1024, 4096], P('dp', 'mp')
- first_down_grad: float32 [1024, 4096], P('dp', 'mp')
- attention_norm_grad: float32 [1024], P('dp')
- query_weight_grad: float32 [1024, 1024], P('dp', 'mp')
- key_weight_grad: float32 [1024, 1024], P('dp', 'mp')
- value_weight_grad: float32 [1024, 1024], P('dp', 'mp')
- position_weight_grad: float32 [1024, 1024], P('dp', 'mp')
- output_weight_grad: float32 [1024, 1024], P('dp', 'mp')
- content_bias_grad: float32 [128, 8], P('dp', 'mp')
- position_bias_grad: float32 [128, 8], P('dp', 'mp')
- convolution_norm_grad: float32 [1024], P('dp')
- pointwise_in_grad: float32 [1024, 2, 1024], P('dp', None, 'mp')
- depthwise_kernel_grad: float32 [1024, 5], P(('mp', 'dp'))
- batch_gain_gradient: float32 [1024], P(('mp', 'dp'))
- batch_shift_grad: float32 [1024], P(('mp', 'dp'))
- pointwise_out_grad: float32 [1024, 1024], P('dp', 'mp')
- second_norm_grad: float32 [1024], P('dp')
- second_up_grad: float32 [1024, 4096], P('dp', 'mp')
- second_down_grad: float32 [1024, 4096], P('dp', 'mp')
- final_norm_grad: float32 [1024], P('dp')
The draws below stay inside these ranges and needn't reach their ends.
Inputs may be any that keep to these rules, and one draw needn't show every extreme that they name: Lengths are whole numbers; the lengths of one group add up to at most 512; one group holds a single utterance of 512 frames and zero lengths in its other slots; a group's rows past its total are padding.
All inputs are finite; a program needn't handle non-finite values.
Results may differ from the reference program's by a relative error of at most 0.04.
Values may be sent and summed in bfloat16 or wider, within the bound.
No kernel may reach another device: no remote copies, remote signals or barrier semaphores. Data moves between devices by JAX's collectives and lax.ppermute only.
A program may use at most 128 MiB of HBM per device.

```python
import math
import jax
import jax.numpy as jnp
from jax import lax

D = 1024
FF = 4096
H = 8
DH = 128
KERNEL = 5
ROWS = 512
SEQS = 4
GROUPS = 8
TOKENS = 4096


def draw_lengths(key, part):
    key = jax.random.fold_in(key, 7)
    fill_key, full_key, cut_key = jax.random.split(key, 3)
    filled = jax.random.randint(fill_key, (GROUPS,), ROWS // 4, ROWS + 1)
    busiest = jax.random.randint(full_key, (), 0, GROUPS)
    cut_points = jnp.sort(jax.random.randint(cut_key, (GROUPS, SEQS - 1), 0, ROWS + 1), axis=1)
    cut_points = jnp.minimum(cut_points, filled[:, None])
    bounds = jnp.concatenate([jnp.zeros((GROUPS, 1), jnp.int32), cut_points, filled[:, None]], axis=1)
    spans = (bounds[:, 1:] - bounds[:, :-1]).astype(jnp.int32)
    whole = jnp.where(jnp.arange(SEQS) == 0, ROWS, 0).astype(jnp.int32)
    chosen = (jnp.arange(GROUPS) == busiest)[:, None]
    return jnp.where(chosen, whole[None, :], spans).astype(jnp.int32)


def block_levels(rng, shape, cuts, smallest, high):
    factor_of, own = 1.0, jax.random.fold_in(rng, 6)
    for axis_at, shards_of in cuts:
        heights = jnp.exp(jax.random.uniform(jax.random.fold_in(own, axis_at), (shards_of,), jnp.float32, smallest / len(cuts), high / len(cuts)))
        factor_of = factor_of * jnp.repeat(heights, shape[axis_at] // shards_of).reshape([-1 if axis == axis_at else 1 for axis in range(len(shape))])
    return factor_of


def normal_values(own_key, shape, scale, limit, cuts=(), kind=jnp.bfloat16):
    array = scale * jax.random.normal(own_key, shape, jnp.float32)
    if cuts:
        array = array * block_levels(own_key, shape, cuts, -0.22, 0.18)
    return jnp.clip(array, -limit, limit).astype(kind)


def setup_inputs(seed: int = 0) -> dict:
    seeds = jax.random.split(jax.random.key(seed), 25)
    inputs = normal_values(seeds[0], (TOKENS, D), 1.0, 6.0, ((0, 8),))
    lengths = draw_lengths(jax.random.fold_in(seeds[24], 71), 0)
    out_grad = normal_values(seeds[2], (TOKENS, D), 1.0, 6.0, ((0, 8),))
    first_norm = jnp.clip(1.0 + 0.1 * jax.random.normal(seeds[3], (D,), jnp.float32), 0.5, 1.5)
    first_up = normal_values(seeds[4], (D, FF), D ** -0.5, 0.1875, ((0, 8), (1, 4)), jnp.float32)
    first_down = normal_values(seeds[5], (D, FF), (FF // 4) ** -0.5, 0.1875, ((0, 8), (1, 4)), jnp.float32)
    attention_norm = jnp.clip(1.0 + 0.1 * jax.random.normal(seeds[6], (D,), jnp.float32), 0.5, 1.5)
    query_weight = normal_values(seeds[7], (D, H * DH), D ** -0.5, 0.1875, ((0, 8), (1, 4)), jnp.float32)
    key_weight = normal_values(seeds[8], (D, H * DH), D ** -0.5, 0.1875, ((0, 8), (1, 4)), jnp.float32)
    value_weight = normal_values(seeds[9], (D, H * DH), D ** -0.5, 0.1875, ((0, 8), (1, 4)), jnp.float32)
    position_weight = normal_values(seeds[10], (D, H * DH), D ** -0.5, 0.1875, ((0, 8), (1, 4)), jnp.float32)
    output_weight = normal_values(seeds[11], (D, H * DH), (H * DH // 16) ** -0.5, 0.75, ((0, 8), (1, 4)), jnp.float32)
    content_bias = normal_values(seeds[12], (DH, H), 0.5, 3.0, ((0, 8), (1, 4)), jnp.float32)
    position_bias = normal_values(seeds[13], (DH, H), 0.5, 3.0, ((0, 8), (1, 4)), jnp.float32)
    convolution_norm = jnp.clip(1.0 + 0.1 * jax.random.normal(seeds[14], (D,), jnp.float32), 0.5, 1.5)
    pointwise_in = normal_values(seeds[15], (D, 2, D), D ** -0.5, 0.1875, ((0, 8), (2, 4)), jnp.float32)
    depthwise_kernel = normal_values(seeds[16], (D, KERNEL), KERNEL ** -0.5, 2.5, ((0, 32),), jnp.float32)
    batch_gain = jnp.clip(1.0 + 0.1 * jax.random.normal(seeds[17], (D,), jnp.float32), 0.5, 1.5)
    batch_shift = normal_values(seeds[18], (D,), 0.5, 3.0, ((0, 32),), jnp.float32)
    pointwise_out = normal_values(seeds[19], (D, D), (D // 4) ** -0.5, 0.375, ((0, 8), (1, 4)), jnp.float32)
    second_norm = jnp.clip(1.0 + 0.1 * jax.random.normal(seeds[20], (D,), jnp.float32), 0.5, 1.5)
    second_up = normal_values(seeds[21], (D, FF), D ** -0.5, 0.1875, ((0, 8), (1, 4)), jnp.float32)
    second_down = normal_values(seeds[22], (D, FF), (FF // 4) ** -0.5, 0.1875, ((0, 8), (1, 4)), jnp.float32)
    final_norm = jnp.clip(1.0 + 0.1 * jax.random.normal(seeds[23], (D,), jnp.float32), 0.5, 1.5)
    return dict(inputs=inputs, lengths=lengths, out_grad=out_grad, first_norm=first_norm, first_up=first_up, first_down=first_down, attention_norm=attention_norm, query_weight=query_weight, key_weight=key_weight, value_weight=value_weight, position_weight=position_weight, output_weight=output_weight, content_bias=content_bias, position_bias=position_bias, convolution_norm=convolution_norm, pointwise_in=pointwise_in, depthwise_kernel=depthwise_kernel, batch_gain=batch_gain, batch_shift=batch_shift, pointwise_out=pointwise_out, second_norm=second_norm, second_up=second_up, second_down=second_down, final_norm=final_norm)


EPSILON = 1e-05
FINEST_PRECISION = lax.Precision.HIGHEST

@jax.custom_vjp
def low(v):
    return lax.optimization_barrier(v.astype(jnp.bfloat16)).astype(jnp.float32)

@jax.custom_vjp
def low_back(v):
    return v

def low_keep(v):
    return (low(v), None)

def low_pass(kept, grad):
    return (grad,)

def back_keep(v):
    return (v, None)

def back_low(kept, grad):
    return (low(grad),)
low.defvjp(low_keep, low_pass)
low_back.defvjp(back_keep, back_low)

def matmul(left_side, right_side):
    return jnp.dot(left_side, right_side, precision=FINEST_PRECISION, preferred_element_type=jnp.float32)

def times_transposed(left_side, right_side):
    return lax.dot_general(left_side, right_side, (((1,), (1,)), ((), ())), precision=FINEST_PRECISION, preferred_element_type=jnp.float32)

def layer_norm(values, norm_gain):
    average = lax.optimization_barrier(jnp.mean(values, axis=-1, keepdims=True))
    centred = values - average
    spread = lax.optimization_barrier(jnp.mean(centred * centred, axis=-1, keepdims=True))
    return centred * lax.rsqrt(spread + EPSILON) * norm_gain

def segment_ids(utterances, row_count):
    bounds = jnp.cumsum(utterances).astype(jnp.int32)
    places = jnp.arange(row_count, dtype=jnp.int32)
    return lax.optimization_barrier(jnp.sum((places[:, None] >= bounds[None, :]).astype(jnp.int32), axis=1)).astype(jnp.int32)

def position_table(row_count, feature_count):
    offsets = (row_count - 1 - jnp.arange(2 * row_count - 1)).astype(jnp.float32)
    rates = jnp.exp(jnp.arange(0, feature_count, 2).astype(jnp.float32) * (-math.log(10000.0) / feature_count))
    angles = offsets[:, None] * rates[None, :]
    return jnp.concatenate([jnp.sin(angles), jnp.cos(angles)], axis=1)

def shear_rows(broad_score_rows):
    head_count, row_count, span_count = broad_score_rows.shape
    flattened = broad_score_rows.reshape(head_count, row_count * span_count)
    flattened = flattened[:, row_count - 1:row_count - 1 + row_count * (span_count - 1)]
    return flattened.reshape(head_count, row_count, span_count - 1)[:, :, :row_count]

def shift_rows(values, offset):
    row_count = values.shape[0]
    if offset > 0:
        return jnp.concatenate([values[offset:], jnp.zeros((offset,) + values.shape[1:], values.dtype)], axis=0)
    if offset < 0:
        return jnp.concatenate([jnp.zeros((-offset,) + values.shape[1:], values.dtype), values[:row_count + offset]], axis=0)
    return values

def depthwise(gated_rows, kernel, segment):
    tap_count = kernel.shape[1]
    marker = segment + 1
    output = jnp.zeros_like(gated_rows)
    for tap_index in range(tap_count):
        offset = tap_index - tap_count // 2
        matching = (shift_rows(marker, offset) == marker).astype(gated_rows.dtype)
        output = output + kernel[:, tap_index][None, :] * matching[:, None] * shift_rows(gated_rows, offset)
    return output

def feed_forward(residual, norm_gain, up_weight, down_weight):
    normed = low(layer_norm(residual, low(norm_gain)))
    before = low_back(matmul(normed, low(up_weight)))
    active = low(before * jax.nn.sigmoid(before))
    return residual + 0.5 * low_back(times_transposed(active, low(down_weight)))

def attention(residual, segment, weights):
    norm_gain, query_weight, key_weight, value_weight, position_weight, output_weight, content_bias, position_bias = weights
    row_count, feature_count = residual.shape
    head_size, head_count = content_bias.shape
    normed = low(layer_norm(residual, low(norm_gain)))
    query_rows = low_back(matmul(normed, low(query_weight))).reshape(row_count, head_count, head_size)
    with_content = low(query_rows + low(content_bias).T[None])
    plus_position_term = low(query_rows + low(position_bias).T[None])
    key_rows = low(low_back(matmul(normed, low(key_weight)))).reshape(row_count, head_count, head_size)
    value_rows = low(low_back(matmul(normed, low(value_weight)))).reshape(row_count, head_count, head_size)
    sin_table = low(position_table(row_count, feature_count))
    relative_offset = low(low_back(matmul(sin_table, low(position_weight)))).reshape(2 * row_count - 1, head_count, head_size)
    direct = jnp.einsum('ihd,jhd->hij', with_content, key_rows, precision=FINEST_PRECISION)
    broad_score_rows = jnp.einsum('tkn,ukn->ktu', plus_position_term, relative_offset, precision=FINEST_PRECISION)
    scores = low_back((direct + shear_rows(broad_score_rows)) * head_size ** (-0.5))
    matching = segment[:, None] == segment[None, :]
    masked = jnp.where(matching[None], scores, -1e+30)
    row_peak = lax.optimization_barrier(jnp.max(masked, axis=-1, keepdims=True))
    exponent = jnp.exp(masked - row_peak)
    prob_low = low(exponent / lax.optimization_barrier(jnp.sum(exponent, axis=-1, keepdims=True)))
    mixed_rows = low(low_back(jnp.einsum('hij,jhd->ihd', prob_low, value_rows, precision=FINEST_PRECISION)))
    mixed_rows = mixed_rows.reshape(row_count, head_count * head_size)
    return residual + low_back(times_transposed(mixed_rows, low(output_weight)))

def forward(residual_all, params, segment, valid_rows):
    first_norm, first_up, first_down, attention_norm, query_weight, key_weight, value_weight, position_weight, output_weight, content_bias, position_bias, convolution_norm, pointwise_in, depthwise_kernel, batch_gain, batch_shift, pointwise_out, second_norm, second_up, second_down, final_norm = params

    def section_one(group_data):
        residual, group_segment, group_valid = group_data
        residual = feed_forward(residual, first_norm, first_up, first_down)
        residual = attention(residual, group_segment, (attention_norm, query_weight, key_weight, value_weight, position_weight, output_weight, content_bias, position_bias))
        normed = low(layer_norm(residual, low(convolution_norm)))
        lifted = low_back(jnp.einsum('rd,dgc->rgc', normed, low(pointwise_in), precision=FINEST_PRECISION))
        gated_rows = lifted[:, 0] * jax.nn.sigmoid(lifted[:, 1]) * group_valid[:, None]
        return (residual, depthwise(gated_rows, low(depthwise_kernel), group_segment))
    middle, convolved = lax.map(jax.checkpoint(section_one), (residual_all, segment, valid_rows))
    frame_count = jnp.sum(valid_rows)
    average = lax.optimization_barrier(jnp.sum(convolved * valid_rows[..., None], axis=(0, 1))) / frame_count
    squares = lax.optimization_barrier(jnp.sum(convolved * convolved * valid_rows[..., None], axis=(0, 1))) / frame_count
    inverse = lax.rsqrt(squares - average * average + EPSILON)

    def section_two(group_data):
        residual, conv_group, group_valid = group_data
        normalized = (conv_group - average) * inverse * low(batch_gain) + low(batch_shift)
        swished = low(normalized * jax.nn.sigmoid(normalized) * group_valid[:, None])
        residual = residual + low_back(times_transposed(swished, low(pointwise_out)))
        residual = feed_forward(residual, second_norm, second_up, second_down)
        return layer_norm(residual, low(final_norm))
    return lax.map(jax.checkpoint(section_two), (middle, convolved, valid_rows))

def reference(inputs, lengths, out_grad, first_norm, first_up, first_down, attention_norm, query_weight, key_weight, value_weight, position_weight, output_weight, content_bias, position_bias, convolution_norm, pointwise_in, depthwise_kernel, batch_gain, batch_shift, pointwise_out, second_norm, second_up, second_down, final_norm):
    segment = jax.vmap(lambda utterances: segment_ids(utterances, ROWS))(lengths)
    valid_rows = (segment < SEQS).astype(jnp.float32)
    residual_all = inputs.astype(jnp.float32).reshape(GROUPS, ROWS, D)
    params = (first_norm, first_up, first_down, attention_norm, query_weight, key_weight, value_weight, position_weight, output_weight, content_bias, position_bias, convolution_norm, pointwise_in, depthwise_kernel, batch_gain, batch_shift, pointwise_out, second_norm, second_up, second_down, final_norm)
    result, pullback = jax.vjp(lambda residual_in, weights: forward(residual_in, weights, segment, valid_rows), residual_all, params)
    residual_grad, grads = pullback(out_grad.astype(jnp.float32).reshape(GROUPS, ROWS, D))
    return (result.reshape(TOKENS, D).astype(jnp.bfloat16), residual_grad.reshape(TOKENS, D), grads[0], grads[1], grads[2], grads[3], grads[4], grads[5], grads[6], grads[7], grads[8], grads[9], grads[10], grads[11], grads[12], grads[13], grads[14], grads[15], grads[16], grads[17], grads[18], grads[19], grads[20])
```

```python
import math

import jax
import jax.numpy as jnp
from jax import lax
from jax.sharding import PartitionSpec as P

EPSILON = 1e-05
LOW = jnp.bfloat16
FLOAT = jnp.float32


def matmul(left_side, right_side):
    return jnp.dot(left_side, right_side, preferred_element_type=FLOAT)


def times_transposed(left_side, right_side):
    return lax.dot_general(
        left_side, right_side, (((1,), (1,)), ((), ())), preferred_element_type=FLOAT
    )


def outer_sum(left_side, right_side):
    return lax.dot_general(
        left_side, right_side, (((0,), (0,)), ((), ())), preferred_element_type=FLOAT
    )


def reversed_bits(places, size):
    outcome = places * 0
    mask, back = size // 2, 1
    while mask:
        outcome = outcome + ((places // back) % 2) * mask
        mask, back = mask // 2, back * 2
    return outcome


def swap(values, axis, mask):
    size = lax.axis_size(axis)
    return lax.ppermute(values, axis, [(i, i ^ mask) for i in range(size)])


def spread(values, axis):
    mask = lax.axis_size(axis) // 2
    while mask:
        values = jnp.concatenate([values, swap(values, axis, mask)], axis=0)
        mask //= 2
    return values


def collect(values, axis, wire, mask=1):
    while mask < lax.axis_size(axis):
        half = values.shape[0] // 2
        values = values[:half] + swap(values[half:].astype(wire), axis, mask).astype(FLOAT)
        mask *= 2
    return values


def total_over(values, axis):
    mask = 1
    while mask < lax.axis_size(axis):
        values = values + swap(values, axis, mask)
        mask *= 2
    return values


def reduce_rows(left_side, right_side):
    half = left_side.shape[0] // 2
    sent = swap(times_transposed(left_side[half:], right_side).astype(LOW), "mp", 1)
    kept = times_transposed(left_side[:half], right_side) + sent.astype(FLOAT)
    return collect(kept, "mp", LOW, 2)


def reduce_weight(left_side, right_side):
    half = left_side.shape[1] // 2
    sent = swap(outer_sum(left_side[:, half:], right_side).astype(LOW), "dp", 1)
    kept = outer_sum(left_side[:, :half], right_side) + sent.astype(FLOAT)
    return collect(kept, "dp", LOW, 2)


def standardize(values):
    average = jnp.mean(values, axis=-1, keepdims=True)
    centred = values - average
    spread_of = jnp.mean(centred * centred, axis=-1, keepdims=True)
    scale = lax.rsqrt(spread_of + EPSILON)
    return centred * scale, scale


def layer_norm(values, norm_gain):
    return standardize(values)[0] * norm_gain


def norm_back(values, norm_gain, normed_grad):
    hat, scale = standardize(values)
    gained = normed_grad * norm_gain
    first = jnp.mean(gained, axis=-1, keepdims=True)
    second = jnp.mean(gained * hat, axis=-1, keepdims=True)
    return (gained - first - hat * second) * scale, jnp.sum(normed_grad * hat, axis=0)


def segment_ids(utterances, row_count):
    bounds = jnp.cumsum(utterances)
    places = jnp.arange(row_count, dtype=jnp.int32)
    return jnp.sum((places[:, None] >= bounds[None, :]).astype(jnp.int32), axis=1)


def position_table(row_count, feature_count):
    offsets = (row_count - 1 - jnp.arange(2 * row_count - 1)).astype(FLOAT)
    rates = jnp.exp(
        jnp.arange(0, feature_count, 2).astype(FLOAT) * (-math.log(10000.0) / feature_count)
    )
    angles = offsets[:, None] * rates[None, :]
    return jnp.concatenate([jnp.sin(angles), jnp.cos(angles)], axis=1)


def shear_rows(broad_score_rows):
    head_count, row_count, span_count = broad_score_rows.shape
    flattened = broad_score_rows.reshape(head_count, row_count * span_count)
    flattened = flattened[:, row_count - 1 : row_count - 1 + row_count * (span_count - 1)]
    return flattened.reshape(head_count, row_count, span_count - 1)[:, :, :row_count]


def unshear_rows(narrow):
    head_count, row_count = (narrow.shape[0], narrow.shape[1])
    padded = jnp.pad(narrow, ((0, 0), (0, 0), (0, row_count - 2)))
    flattened = jnp.pad(
        padded.reshape(head_count, row_count * (2 * row_count - 2)), ((0, 0), (row_count - 1, 1))
    )
    return flattened.reshape(head_count, row_count, 2 * row_count - 1)


def shift_rows(values, offset):
    row_count = values.shape[0]
    if offset > 0:
        return jnp.concatenate(
            [values[offset:], jnp.zeros((offset,) + values.shape[1:], values.dtype)], axis=0
        )
    if offset < 0:
        return jnp.concatenate(
            [jnp.zeros((-offset,) + values.shape[1:], values.dtype), values[: row_count + offset]],
            axis=0,
        )
    return values


def depthwise(gated_rows, kernel, segment):
    tap_count = kernel.shape[1]
    marker = segment + 1
    output = jnp.zeros_like(gated_rows)
    for tap_index in range(tap_count):
        offset = tap_index - tap_count // 2
        matching = (shift_rows(marker, offset) == marker).astype(gated_rows.dtype)
        output = output + kernel[:, tap_index][None, :] * matching[:, None] * shift_rows(
            gated_rows, offset
        )
    return output


def gated_conv(lifted, kernel, segment, valid_rows):
    half = lifted.shape[1] // 2
    gated_rows = lifted[:, :half] * jax.nn.sigmoid(lifted[:, half:]) * valid_rows[:, None]
    return depthwise(gated_rows, kernel, segment)


def attention_scores(with_content, with_position, key_rows, relative_offset, segment):
    head_size = key_rows.shape[2]
    direct = jnp.einsum("ihd,jhd->hij", with_content, key_rows, preferred_element_type=FLOAT)
    broad_score_rows = jnp.einsum(
        "tkn,ukn->ktu", with_position, relative_offset, preferred_element_type=FLOAT
    )
    scores = (direct + shear_rows(broad_score_rows)) * head_size ** (-0.5)
    matching = segment[:, None] == segment[None, :]
    return jnp.where(matching[None], scores, -1e30)


def ffn_forward(residual, normed, up_weight, down_weight):
    before = matmul(normed, up_weight)
    active = (before * jax.nn.sigmoid(before)).astype(LOW)
    return residual + 0.5 * reduce_rows(active, down_weight), (before, active)


def ffn_backward(residual_grad, residual, norm_gain, normed, up_weight, down_weight, stored):
    before, active = stored
    branch_grad = spread((0.5 * residual_grad).astype(LOW), "mp")
    squashed = jax.nn.sigmoid(before)
    before_grad = (
        matmul(branch_grad, down_weight) * squashed * (1.0 + before * (1.0 - squashed))
    ).astype(LOW)
    normed_grad = reduce_rows(before_grad, up_weight)
    down_grad = reduce_weight(branch_grad, active)
    up_grad = reduce_weight(normed, before_grad)
    input_grad, gain_grad = norm_back(residual, norm_gain, normed_grad)
    return residual_grad + input_grad, gain_grad, up_grad, down_grad


def per_device(
    inputs,
    lengths,
    out_grad,
    first_norm,
    first_up,
    first_down,
    attention_norm,
    query_weight,
    key_weight,
    value_weight,
    position_weight,
    output_weight,
    content_bias,
    position_bias,
    convolution_norm,
    pointwise_in,
    depthwise_kernel,
    batch_gain,
    batch_shift,
    pointwise_out,
    second_norm,
    second_up,
    second_down,
    final_norm,
):
    row_count, feature_count = inputs.shape
    dp_size, mp_size = lax.axis_size("dp"), lax.axis_size("mp")
    dp_at, mp_at = lax.axis_index("dp"), lax.axis_index("mp")
    block = first_up.shape[0]
    row_block = row_count // mp_size
    bias_rows, head_count = content_bias.shape
    head_size = bias_rows * dp_size
    local_channels, tap_count = depthwise_kernel.shape
    channels = local_channels * dp_size
    score_scale = head_size ** (-0.5)

    places = jnp.arange(feature_count, dtype=jnp.int32)
    owners = dp_at ^ reversed_bits(places // block, dp_size)
    source = owners * block + places % block
    selection = (places[:, None] == source[None, :]).astype(LOW)
    block_places = jnp.arange(dp_size, dtype=jnp.int32)
    block_owners = dp_at ^ reversed_bits(block_places, dp_size)
    block_selection = (block_places[:, None] == block_owners[None, :]).astype(FLOAT)
    mp_back = reversed_bits(mp_at, mp_size)

    def own_rows(values):
        pieces = [
            lax.dynamic_slice_in_dim(
                values, (mp_at ^ reversed_bits(p, mp_size)) * row_block, row_block, axis=0
            )
            for p in range(mp_size)
        ]
        return jnp.concatenate(pieces, axis=0)

    def plain_rows(values):
        pieces = [
            lax.dynamic_slice_in_dim(
                values, (mp_back ^ reversed_bits(p, mp_size)) * row_block, row_block, axis=0
            )
            for p in range(mp_size)
        ]
        return jnp.concatenate(pieces, axis=0)

    first_up_all = spread(first_up.astype(LOW), "dp")
    small_parts = [
        first_norm, attention_norm, convolution_norm, second_norm, final_norm,
        content_bias.reshape(-1), position_bias.reshape(-1), depthwise_kernel.reshape(-1),
        batch_gain, batch_shift,
    ]
    small_own = jnp.concatenate([part.astype(LOW).astype(FLOAT) for part in small_parts])
    small_all = spread(small_own[None], "dp")
    first_down_all = spread(first_down.astype(LOW), "dp")
    attention_own = jnp.concatenate(
        [query_weight, key_weight, value_weight, position_weight, output_weight], axis=1
    ).astype(LOW)
    attention_all = spread(attention_own, "dp")
    convolution_own = jnp.concatenate(
        [pointwise_in.reshape(block, 2 * channels), pointwise_out], axis=1
    ).astype(LOW)
    convolution_all = spread(convolution_own, "dp")
    second_up_all = spread(second_up.astype(LOW), "dp")
    second_down_all = spread(second_down.astype(LOW), "dp")

    norms = small_all[:, : 5 * block].reshape(dp_size, 5, block)
    norms = norms.transpose(1, 0, 2).reshape(5, feature_count)
    first_gain, attention_gain, convolution_gain, second_gain, final_gain = norms
    plain_small = jnp.dot(
        block_selection, small_all[:, 5 * block :], preferred_element_type=FLOAT
    )
    cut = bias_rows * head_count
    content_all = plain_small[:, :cut].reshape(head_size, head_count)
    position_all = plain_small[:, cut : 2 * cut].reshape(head_size, head_count)
    at = 2 * cut + local_channels * tap_count
    taps = plain_small[:, 2 * cut : at].reshape(channels, tap_count)
    gain_all = plain_small[:, at : at + local_channels].reshape(channels)
    shift_all = plain_small[:, at + local_channels :].reshape(channels)

    segment = segment_ids(lengths[0], row_count)
    valid_rows = (segment < lengths.shape[1]).astype(FLOAT)
    arranged = matmul(own_rows(inputs), selection)
    own_out_grad = matmul(
        lax.dynamic_slice_in_dim(out_grad, mp_at * row_block, row_block, axis=0), selection
    )
    sin_table = position_table(row_count, feature_count).astype(LOW)
    sin_table = matmul(sin_table, selection).astype(LOW)
    frame_count = jnp.sum(valid_rows)

    residual_zero = arranged[:row_block]
    normed_a = layer_norm(arranged, first_gain).astype(LOW)
    residual_one, first_stored = ffn_forward(residual_zero, normed_a, first_up_all, first_down_all)

    heads = head_count * head_size
    normed_b = spread(layer_norm(residual_one, attention_gain).astype(LOW), "mp")
    qkv_weight = attention_all[:, : 3 * heads]
    position_weight_all = attention_all[:, 3 * heads : 4 * heads]
    output_weight_all = attention_all[:, 4 * heads :]
    qkv = plain_rows(matmul(normed_b, qkv_weight))
    query_rows = qkv[:, :heads].reshape(row_count, head_count, head_size)
    with_content = (query_rows + content_all.T[None]).astype(LOW)
    with_position = (query_rows + position_all.T[None]).astype(LOW)
    key_rows = qkv[:, heads : 2 * heads].astype(LOW).reshape(row_count, head_count, head_size)
    value_rows = qkv[:, 2 * heads :].astype(LOW).reshape(row_count, head_count, head_size)
    relative_offset = (
        matmul(sin_table, position_weight_all)
        .astype(LOW)
        .reshape(2 * row_count - 1, head_count, head_size)
    )
    masked = attention_scores(with_content, with_position, key_rows, relative_offset, segment)
    row_peak = jnp.max(masked, axis=-1, keepdims=True)
    exponent = jnp.exp(masked - row_peak)
    prob_low = (exponent / jnp.sum(exponent, axis=-1, keepdims=True)).astype(LOW)
    mixed_rows = jnp.einsum("hij,jhd->ihd", prob_low, value_rows, preferred_element_type=FLOAT)
    mixed_rows = own_rows(mixed_rows.astype(LOW).reshape(row_count, heads))
    residual_two = residual_one + reduce_rows(mixed_rows, output_weight_all)

    normed_c = spread(layer_norm(residual_two, convolution_gain).astype(LOW), "mp")
    pointwise_in_all = convolution_all[:, : 2 * channels]
    pointwise_out_all = convolution_all[:, 2 * channels :]
    lifted = plain_rows(matmul(normed_c, pointwise_in_all))
    convolved = gated_conv(lifted, taps, segment, valid_rows)
    masked_conv = convolved * valid_rows[:, None]
    sums = jnp.stack(
        [
            jnp.sum(masked_conv, axis=0),
            jnp.sum(masked_conv * convolved, axis=0),
            jnp.broadcast_to(frame_count, (channels,)),
        ]
    )
    sums = total_over(sums, "dp")
    frame_total = sums[2]
    average = sums[0] / frame_total
    inverse = lax.rsqrt(sums[1] / frame_total - average * average + EPSILON)
    hatted = (convolved - average) * inverse
    normalized = hatted * gain_all + shift_all
    swished = own_rows(
        (normalized * jax.nn.sigmoid(normalized) * valid_rows[:, None]).astype(LOW)
    )
    residual_three = residual_two + reduce_rows(swished, pointwise_out_all)

    normed_d = spread(layer_norm(residual_three, second_gain).astype(LOW), "mp")
    residual_four, second_stored = ffn_forward(
        residual_three, normed_d, second_up_all, second_down_all
    )
    own_result = layer_norm(residual_four, final_gain).astype(LOW)
    result = plain_rows(spread(times_transposed(own_result, selection).astype(LOW), "mp"))

    residual_grad, final_gain_grad = norm_back(residual_four, final_gain, own_out_grad)
    residual_grad, second_gain_grad, second_up_grad, second_down_grad = ffn_backward(
        residual_grad, residual_three, second_gain, normed_d, second_up_all, second_down_all,
        second_stored,
    )

    branch_grad = spread(residual_grad.astype(LOW), "mp")
    squashed = jax.nn.sigmoid(normalized)
    normal_grad = (
        plain_rows(matmul(branch_grad, pointwise_out_all))
        * valid_rows[:, None]
        * squashed
        * (1.0 + normalized * (1.0 - squashed))
    )
    back_sums = total_over(
        jnp.stack([jnp.sum(normal_grad, axis=0), jnp.sum(normal_grad * hatted, axis=0)]), "dp"
    )
    shift_total, gain_total = back_sums[0], back_sums[1]
    conv_grad = inverse * (
        normal_grad * gain_all
        - valid_rows[:, None] * gain_all * (shift_total + hatted * gain_total) / frame_total
    )
    _, pullback = jax.vjp(
        lambda lifted_in, kernel_in: gated_conv(lifted_in, kernel_in, segment, valid_rows),
        lifted,
        taps,
    )
    lifted_grad, taps_grad = pullback(conv_grad)
    lifted_low = own_rows(lifted_grad.astype(LOW))
    normed_grad = reduce_rows(lifted_low, pointwise_in_all)
    pointwise_out_grad = reduce_weight(branch_grad, swished)
    pointwise_in_grad = reduce_weight(normed_c, lifted_low)
    input_grad, convolution_gain_grad = norm_back(residual_two, convolution_gain, normed_grad)
    residual_grad = residual_grad + input_grad
    first_row = dp_at * local_channels
    gain_piece = lax.dynamic_slice_in_dim(gain_total, first_row, local_channels)
    shift_piece = lax.dynamic_slice_in_dim(shift_total, first_row, local_channels)

    branch_grad = spread(residual_grad.astype(LOW), "mp")
    mixed_grad = plain_rows(matmul(branch_grad, output_weight_all).astype(LOW)).reshape(
        row_count, head_count, head_size
    )
    prob_rows = prob_low.astype(FLOAT)
    value_grad = jnp.einsum("hij,ihd->jhd", prob_low, mixed_grad, preferred_element_type=FLOAT)
    prob_grad = jnp.einsum("ihd,jhd->hij", mixed_grad, value_rows, preferred_element_type=FLOAT)
    inner_term = jnp.sum(prob_grad * prob_rows, axis=-1, keepdims=True)
    score_grad = (prob_rows * (prob_grad - inner_term)).astype(LOW)
    content_part = score_scale * jnp.einsum(
        "hij,jhd->ihd", score_grad, key_rows, preferred_element_type=FLOAT
    )
    key_grad = score_scale * jnp.einsum(
        "hij,ihd->jhd", score_grad, with_content, preferred_element_type=FLOAT
    )
    broad = unshear_rows(score_grad)
    position_part = score_scale * jnp.einsum(
        "yfa,ayt->fyt", broad, relative_offset, preferred_element_type=FLOAT
    )
    position_grad = score_scale * jnp.einsum(
        "nsq,snr->qnr", broad, with_position, preferred_element_type=FLOAT
    )
    position_grad = position_grad.astype(LOW).reshape(2 * row_count - 1, heads)
    qkv_grad = jnp.concatenate(
        [
            (content_part + position_part).astype(LOW).reshape(row_count, heads),
            key_grad.astype(LOW).reshape(row_count, heads),
            value_grad.astype(LOW).reshape(row_count, heads),
        ],
        axis=1,
    )
    qkv_grad = own_rows(qkv_grad)
    content_bias_grad = jnp.sum(content_part, axis=0).T
    position_bias_grad = jnp.sum(position_part, axis=0).T
    normed_grad = reduce_rows(qkv_grad, qkv_weight)
    output_weight_grad = reduce_weight(branch_grad, mixed_rows)
    qkv_weight_grad = reduce_weight(normed_b, qkv_grad)
    position_weight_grad = reduce_weight(sin_table, position_grad)
    input_grad, attention_gain_grad = norm_back(residual_one, attention_gain, normed_grad)
    residual_grad = residual_grad + input_grad

    residual_grad, first_gain_grad, first_up_grad, first_down_grad = ffn_backward(
        residual_grad, residual_zero, first_gain, normed_a, first_up_all, first_down_all,
        first_stored,
    )
    own_inputs_grad = times_transposed(residual_grad.astype(LOW), selection).astype(LOW)
    inputs_grad = plain_rows(spread(own_inputs_grad, "mp").astype(FLOAT))

    plain_grads = jnp.concatenate(
        [
            content_bias_grad.reshape(dp_size, cut),
            position_bias_grad.reshape(dp_size, cut),
            taps_grad.reshape(dp_size, local_channels * tap_count),
        ],
        axis=1,
    )
    plain_grads = lax.dot_general(
        block_selection, plain_grads, (((0,), (0,)), ((), ())),
        precision=lax.Precision.HIGHEST, preferred_element_type=FLOAT,
    )
    gain_grads = jnp.stack(
        [
            first_gain_grad, attention_gain_grad, convolution_gain_grad, second_gain_grad,
            final_gain_grad,
        ]
    )
    gain_grads = gain_grads.reshape(5, dp_size, block).transpose(1, 0, 2)
    small_grads = jnp.concatenate([gain_grads.reshape(dp_size, 5 * block), plain_grads], axis=1)
    small_grads = collect(small_grads, "dp", FLOAT)[0]
    gain_grads = total_over(small_grads[: 5 * block].reshape(5, block), "mp")
    plain_grads = small_grads[5 * block :]

    return (
        result,
        inputs_grad,
        gain_grads[0],
        first_up_grad,
        first_down_grad,
        gain_grads[1],
        qkv_weight_grad[:, :heads],
        qkv_weight_grad[:, heads : 2 * heads],
        qkv_weight_grad[:, 2 * heads :],
        position_weight_grad,
        output_weight_grad,
        plain_grads[:cut].reshape(bias_rows, head_count),
        plain_grads[cut : 2 * cut].reshape(bias_rows, head_count),
        gain_grads[2],
        pointwise_in_grad.reshape(block, 2, channels),
        plain_grads[2 * cut :].reshape(local_channels, tap_count),
        gain_piece,
        shift_piece,
        pointwise_out_grad,
        gain_grads[3],
        second_up_grad,
        second_down_grad,
        gain_grads[4],
    )


def solution(mesh):
    return jax.shard_map(
        per_device,
        mesh=mesh,
        in_specs=(
            P("dp", None),
            P("dp", None),
            P("dp", None),
            P("dp"),
            P("dp", "mp"),
            P("dp", "mp"),
            P("dp"),
            P("dp", "mp"),
            P("dp", "mp"),
            P("dp", "mp"),
            P("dp", "mp"),
            P("dp", "mp"),
            P("dp", "mp"),
            P("dp", "mp"),
            P("dp"),
            P("dp", None, "mp"),
            P(("mp", "dp"), None),
            P(("mp", "dp")),
            P(("mp", "dp")),
            P("dp", "mp"),
            P("dp"),
            P("dp", "mp"),
            P("dp", "mp"),
            P("dp"),
        ),
        out_specs=(
            P("dp", None),
            P("dp", None),
            P("dp"),
            P("dp", "mp"),
            P("dp", "mp"),
            P("dp"),
            P("dp", "mp"),
            P("dp", "mp"),
            P("dp", "mp"),
            P("dp", "mp"),
            P("dp", "mp"),
            P("dp", "mp"),
            P("dp", "mp"),
            P("dp"),
            P("dp", None, "mp"),
            P(("mp", "dp"), None),
            P(("mp", "dp")),
            P(("mp", "dp")),
            P("dp", "mp"),
            P("dp"),
            P("dp", "mp"),
            P("dp", "mp"),
            P("dp"),
        ),
        check_vma=False,
    )
```

```python
import functools
import math

import jax
import jax.numpy as jnp
from jax import lax
from jax.experimental import pallas as pl
from jax.experimental.pallas import tpu as pltpu
from jax.sharding import PartitionSpec as P

EPSILON = 1e-05
LOW = jnp.bfloat16
FLOAT = jnp.float32


def matmul(left_side, right_side):
    return jnp.dot(left_side, right_side, preferred_element_type=FLOAT)


def times_transposed(left_side, right_side):
    return lax.dot_general(
        left_side, right_side, (((1,), (1,)), ((), ())), preferred_element_type=FLOAT
    )


def outer_sum(left_side, right_side):
    return lax.dot_general(
        left_side, right_side, (((0,), (0,)), ((), ())), preferred_element_type=FLOAT
    )


def reversed_bits(places, size):
    outcome = places * 0
    mask, back = size // 2, 1
    while mask:
        outcome = outcome + ((places // back) % 2) * mask
        mask, back = mask // 2, back * 2
    return outcome


def swap(values, axis, mask):
    size = lax.axis_size(axis)
    return lax.ppermute(values, axis, [(i, i ^ mask) for i in range(size)])


def after(values, *tokens):
    return lax.optimization_barrier((values, tokens))[0] if tokens else values


class Links:
    def __init__(self, depth, apart=False):
        self.depth, self.apart, self.queues = depth, apart, {}

    def swap(self, values, mask):
        queue, depth = self.queues.setdefault(self.apart and mask == 1, []), self.depth
        if len(queue) >= depth:
            values = after(values, *queue[-2 * depth : len(queue) + 1 - depth])
        queue.append(swap(values, "dp", mask))
        return queue[-1]


ORDER = (4, 1, 2, 3, 5, 6, 7)


class Spread:
    def __init__(self, links, own):
        self.links, self.mask = links, lax.axis_size("dp") // 2
        while self.mask > 4:
            own = jnp.concatenate([own, links.swap(own, self.mask)], axis=0)
            self.mask //= 2
        self.blocks = [own] + [None] * (2 * self.mask - 1)

    def go(self, places, *tokens):
        for p in places:
            if p < len(self.blocks):
                top = 1 << (p.bit_length() - 1)
                self.blocks[p] = self.links.swap(
                    after(self.blocks[p - top], *tokens), self.mask // top
                )


def spread(values, axis):
    mask = lax.axis_size(axis) // 2
    while mask:
        values = jnp.concatenate([values, swap(values, axis, mask)], axis=0)
        mask //= 2
    return values


def collect(values, axis, wire, mask=1):
    while mask < lax.axis_size(axis):
        half = values.shape[0] // 2
        values = values[:half] + swap(values[half:].astype(wire), axis, mask).astype(FLOAT)
        mask *= 2
    return values


def total_over(values, axis):
    mask = 1
    while mask < lax.axis_size(axis):
        values = values + swap(values, axis, mask)
        mask *= 2
    return values


def total_hops(values, axis):
    arrivals, mask = [], lax.axis_size(axis) // 2
    while mask:
        arrivals.append(swap(values, axis, mask))
        values = values + arrivals[-1]
        mask //= 2
    return values, arrivals


class WeightSum:
    def __init__(self, *pairs):
        self.pairs, self.mask = pairs, 0

    def advance(self, *tokens, links=None):
        if not self.mask:
            half = self.pairs[0][0].shape[1] // 2
            upper = [outer_sum(left[:, half:], right).astype(LOW) for left, right in self.pairs]
            lower = [outer_sum(left[:, :half], right) for left, right in self.pairs]
            self.upper, self.kept = jnp.concatenate(upper, axis=1), jnp.concatenate(lower, axis=1)
            self.upper, self.mask = after(self.upper, *tokens), 1
        else:
            total = self.kept + after(self.sent, *tokens).astype(FLOAT)
            half = total.shape[0] // 2
            self.upper, self.kept = total[half:].astype(LOW), total[:half]
        if links is None:
            self.sent = swap(self.upper, "dp", self.mask)
        else:
            self.sent = links.swap(self.upper, self.mask)
        self.mask *= 2

    def rest(self, *tokens):
        while self.mask < lax.axis_size("dp"):
            self.advance(*tokens)


def position_table(places, row_count, feature_count):
    rates = jnp.exp(
        jnp.arange(0, feature_count, 2).astype(FLOAT) * (-math.log(10000.0) / feature_count)
    )
    stride = 32
    count = places.shape[0] // stride
    coarse = (row_count - 1 - stride * places[:count]).astype(FLOAT)[:, None] * rates[None, :]
    fine = -places[:stride].astype(FLOAT)[:, None] * rates[None, :]
    coarse_sin, coarse_cos = jnp.sin(coarse)[:, None], jnp.cos(coarse)[:, None]
    fine_sin, fine_cos = jnp.sin(fine)[None], jnp.cos(fine)[None]
    sines = coarse_sin * fine_cos + coarse_cos * fine_sin
    cosines = coarse_cos * fine_cos - coarse_sin * fine_sin
    table = jnp.concatenate([sines, cosines], axis=2).astype(LOW)
    return table.reshape(places.shape[0], feature_count)


def fixed_reversed(place, size):
    outcome, mask = 0, size // 2
    while mask:
        outcome, place, mask = outcome + (place % 2) * mask, place // 2, mask // 2
    return outcome


def relative_window(position_ref, first, row_block, columns):
    row_count = position_ref.shape[0] // 2
    start = pl.multiple_of(row_count - row_block - first, row_block)
    return position_ref.at[pl.ds(start, row_count + row_block), columns]


def in_smem():
    return pl.BlockSpec(memory_space=pltpu.SMEM)


def in_vmem():
    return pl.BlockSpec(memory_space=pltpu.VMEM)


def anywhere():
    return pl.BlockSpec(memory_space=pl.ANY)


def call(kernel, outs, scratch, flops, *operands):
    places = dict(smem=in_smem, vmem=in_vmem, any=anywhere)
    moved = sum(array.size * array.dtype.itemsize for _, array in operands)
    moved += sum(math.prod(shape) * jnp.dtype(kind).itemsize for shape, kind in outs)
    return pl.pallas_call(
        kernel,
        out_shape=tuple(jax.ShapeDtypeStruct(shape, kind) for shape, kind in outs),
        in_specs=[places[place]() for place, _ in operands],
        out_specs=(in_vmem(),) * len(outs),
        scratch_shapes=scratch,
        compiler_params=pltpu.CompilerParams(vmem_limit_bytes=(50 if scratch else 6) * 2**20),
        cost_estimate=pl.CostEstimate(flops=flops, bytes_accessed=0, transcendentals=0),
    )(*[array for _, array in operands])


class Copies:
    def __init__(self, semaphores):
        self.semaphores, self.count = semaphores, 0

    def start(self, source, target):
        copy = pltpu.make_async_copy(source, target, self.semaphores.at[self.count])
        copy.start()
        self.count += 1
        return copy

    def stack(self, sources, target, columns=None):
        copies, block = [], target.shape[0] // len(sources)
        for p, source in enumerate(sources):
            if columns is not None:
                source = source.at[:, columns]
            copies.append(self.start(source, target.at[pl.ds(p * block, block)]))
        return copies

    def weight(self, sources, owners_ref, target, columns):
        if len(sources) > 1:
            return self.stack(sources, target, columns)
        copies, blocks = [], owners_ref.shape[0]
        block = target.shape[0] // blocks
        for p in range(blocks):
            first = pl.multiple_of(owners_ref[p] * block, block)
            copies.append(
                self.start(
                    sources[0].at[pl.ds(first, block), columns],
                    target.at[pl.ds(p * block, block)],
                )
            )
        return copies


def wait(copies):
    for copy in copies:
        copy.wait()


def weight_copies(sources, owners):
    return len(sources) if len(sources) > 1 else owners.shape[0]


TILE = 256


def write_parts(hi_ref, next_ref, own_ref, columns, product):
    half, own = hi_ref.shape[0], own_ref.shape[0]
    hi_ref[:, columns] = product[half:].astype(LOW)
    next_ref[:, columns] = product[own:half].astype(LOW)
    own_ref[:, columns] = product[:own]


def tiles(count):
    def loop(body):
        @pl.loop(0, count // TILE)
        def _(t):
            body(pl.ds(pl.multiple_of(t * TILE, TILE), TILE))

    return loop


def ffn_forward_kernel(*refs, pieces, weights, up_columns, down_columns):
    owners_ref, refs = refs[0], refs[1:]
    row_refs, refs = refs[:pieces], refs[pieces:]
    up_refs, refs = refs[:weights], refs[weights:]
    down_refs, refs = refs[:weights], refs[weights:]
    rows_ref, before_ref, active_ref, hi_ref, next_ref, own_ref, up, down, semaphores = refs
    copies = Copies(semaphores)
    rows_copies = copies.stack(row_refs, rows_ref)
    up_copies = copies.weight(up_refs, owners_ref, up, up_columns)
    down_copies = copies.weight(down_refs, owners_ref, down, down_columns)
    wait(rows_copies + up_copies)

    @tiles(up.shape[1])
    def _(columns):
        before = matmul(rows_ref[...], up[:, columns])
        before_ref[:, columns] = before.astype(LOW)
        active_ref[:, columns] = (before * jax.nn.sigmoid(before)).astype(LOW)

    wait(down_copies)

    @tiles(down.shape[0])
    def _(features):
        write_parts(
            hi_ref, next_ref, own_ref, features, times_transposed(active_ref[...], down[features, :])
        )


def ffn_backward_kernel(*refs, pieces, weights, up_columns, down_columns, gains):
    owners_ref, refs = refs[0], refs[1:]
    if gains:
        hat_ref, gain_grad_ref, refs = refs[-10], refs[-4], refs[:-10] + refs[-9:-4] + refs[-3:]
    row_refs, refs = refs[:pieces], refs[pieces:]
    up_refs, refs = refs[:weights], refs[weights:]
    down_refs, refs = refs[:weights], refs[weights:]
    before_ref, rows_ref, grad_ref, hi_ref, next_ref, own_ref, up, down, semaphores = refs
    copies = Copies(semaphores)
    rows_copies = copies.stack(row_refs, rows_ref)
    down_copies = copies.weight(down_refs, owners_ref, down, down_columns)
    up_copies = copies.weight(up_refs, owners_ref, up, up_columns)
    wait(rows_copies + down_copies)

    @tiles(down.shape[1])
    def _(columns):
        before = before_ref[:, columns].astype(FLOAT)
        squashed = jax.nn.sigmoid(before)
        grad = matmul(rows_ref[...], down[:, columns])
        grad_ref[:, columns] = (grad * squashed * (1.0 + before * (1.0 - squashed))).astype(LOW)

    wait(up_copies)

    @tiles(up.shape[0])
    def _(features):
        product = times_transposed(grad_ref[...], up[features, :])
        write_parts(hi_ref, next_ref, own_ref, features, product)
        if gains:
            gain_grad_ref[:, features] = jnp.sum(
                product * hat_ref[:, features].astype(FLOAT), axis=0, keepdims=True
            )


def row_parts(rows, features):
    return [
        ((rows // 2, features), LOW), ((rows // 4, features), LOW), ((rows // 4, features), FLOAT)
    ]


def ffn_call(
    kernel, owners, rows, ups, downs, up_columns, down_columns, before=None, hat=None
):
    row_count = len(rows) * rows[0].shape[0]
    features = rows[0].shape[1]
    hidden = up_columns.stop - up_columns.start
    outs = [((row_count, features), LOW)]
    outs += [((row_count, hidden), LOW)] * (2 if before is None else 1)
    count = len(rows) + 2 * weight_copies(ups, owners)
    operands = [("smem", owners)]
    operands += [("any", array) for array in list(rows) + list(ups) + list(downs)]
    if before is not None:
        operands.append(("vmem", before))
        kernel = functools.partial(kernel, gains=hat is not None)
    outs += row_parts(row_count, features)
    if hat is not None:
        operands.append(("vmem", hat))
        outs.append(((1, features), FLOAT))
    return call(
        functools.partial(
            kernel, pieces=len(rows), weights=len(ups), up_columns=up_columns,
            down_columns=down_columns,
        ),
        outs,
        [
            pltpu.VMEM((features, hidden), LOW),
            pltpu.VMEM((features, hidden), LOW),
            pltpu.SemaphoreType.DMA((count,)),
        ],
        4 * row_count * features * hidden,
        *operands,
    )


def segment_of(lengths_ref, places):
    bound, segment = 0, jnp.zeros(places.shape, jnp.int32)
    for s in range(lengths_ref.shape[1]):
        bound = bound + lengths_ref[0, s]
        segment = segment + (places >= bound).astype(jnp.int32)
    return segment


def block_firsts(place_ref, blocks, row_block):
    place = place_ref[0]
    return [
        pl.multiple_of((place ^ fixed_reversed(q, blocks)) * row_block, row_block)
        for q in range(blocks)
    ]


def attention_forward_kernel(*refs, pieces, weights):
    place_ref, lengths_ref, owners_ref, content_ref, shift_ref = refs[:5]
    refs = refs[5:]
    row_refs, refs = refs[:pieces], refs[pieces:]
    weight_refs, refs = refs[:weights], refs[weights:]
    (
        table_ref,
        rows_ref, mixed_ref, prob_ref, content_rows_ref, position_rows_ref, key_ref, value_ref,
        position_ref, hi_ref, next_ref, own_ref,
        weight, table, qkv, semaphores,
    ) = refs
    row_count, heads = mixed_ref.shape
    head_count, head_size = content_ref.shape
    row_block = row_count // pieces
    window = row_count + row_block
    copies = Copies(semaphores)
    rows_copies = copies.stack(row_refs, rows_ref)
    everything = slice(0, weight.shape[1])
    weight_copies_ = copies.weight(weight_refs, owners_ref, weight, everything)
    table_copy = copies.start(table_ref, table)
    firsts = block_firsts(place_ref, pieces, row_block)
    wait(rows_copies + weight_copies_)

    @tiles(3 * heads)
    def _(columns):
        qkv[:, columns] = matmul(rows_ref[...], weight[:, columns])

    table_copy.wait()

    @tiles(table.shape[0])
    def _(places):
        position_ref[places, :] = matmul(
            table[places, :], weight[:, 3 * heads : 4 * heads]
        ).astype(LOW)

    for q in range(pieces):
        rows = pl.ds(q * row_block, row_block)
        key_ref[pl.ds(firsts[q], row_block), :] = qkv[rows, heads : 2 * heads].astype(LOW)
        value_ref[pl.ds(firsts[q], row_block), :] = qkv[rows, 2 * heads :].astype(LOW)

    along = lax.broadcasted_iota(jnp.int32, (1, row_count), 1)
    column_segment = segment_of(lengths_ref, along)
    for q in range(pieces):
        rows = pl.ds(q * row_block, row_block)
        down = lax.broadcasted_iota(jnp.int32, (row_block, 1), 0) + firsts[q]
        matching = segment_of(lengths_ref, down) == column_segment
        for h in range(head_count):
            columns = slice(h * head_size, (h + 1) * head_size)
            query = qkv[rows, columns]
            with_content = (query + content_ref[h : h + 1, :]).astype(LOW)
            with_position = (query + shift_ref[h : h + 1, :]).astype(LOW)
            content_rows_ref[rows, columns] = with_content
            position_rows_ref[rows, columns] = with_position
            direct = times_transposed(with_content, key_ref[:, columns])
            relative = relative_window(position_ref, firsts[q], row_block, columns)[...]
            broad = times_transposed(with_position, relative)
            broad = pltpu.roll(
                broad, window - (row_block - 1), axis=1, stride=1, stride_axis=0
            )
            scores = (direct + broad[:, :row_count]) * head_size ** (-0.5)
            scores = jnp.where(matching, scores, -1e30)
            exponent = jnp.exp(scores - jnp.max(scores, axis=1, keepdims=True))
            prob = (exponent / jnp.sum(exponent, axis=1, keepdims=True)).astype(LOW)
            prob_ref[h, rows, :] = prob
            mixed_ref[rows, columns] = matmul(prob, value_ref[:, columns]).astype(LOW)

    @tiles(weight.shape[0])
    def _(features):
        write_parts(
            hi_ref, next_ref, own_ref, features,
            times_transposed(mixed_ref[...], weight[features, 4 * heads : 5 * heads]),
        )


def attention_forward(place, lengths, owners, rows, weights, table, content_bias, position_bias):
    row_count, features = len(rows) * rows[0].shape[0], rows[0].shape[1]
    head_count, head_size = content_bias.shape
    heads = head_count * head_size
    row_array = ((row_count, heads), LOW)
    return call(
        functools.partial(attention_forward_kernel, pieces=len(rows), weights=len(weights)),
        [
            ((row_count, features), LOW), row_array,
            ((head_count, row_count, row_count), LOW),
            row_array, row_array, row_array, row_array,
            ((2 * row_count, heads), LOW),
        ]
        + row_parts(row_count, features),
        [
            pltpu.VMEM((features, 5 * heads), LOW),
            pltpu.VMEM(table.shape, LOW),
            pltpu.VMEM((row_count, 3 * heads), FLOAT),
            pltpu.SemaphoreType.DMA((len(rows) + weight_copies(weights, owners) + 1,)),
        ],
        12 * row_count * features * heads + 9 * heads * row_count**2,
        ("smem", place), ("smem", lengths), ("smem", owners),
        ("vmem", content_bias), ("vmem", position_bias),
        *[("any", array) for array in list(rows) + list(weights) + [table]],
    )


def attention_backward_kernel(*refs, pieces, weights, head_count):
    place_ref, owners_ref, refs = refs[0], refs[1], refs[2:]
    row_refs, refs = refs[:pieces], refs[pieces:]
    weight_refs, refs = refs[:weights], refs[weights:]
    (
        position_ref, prob_ref, content_rows_ref, position_rows_ref, key_ref, value_ref,
        rows_ref, qkv_grad_ref, position_grad_ref, bias_grad_ref, hi_ref, next_ref, own_ref,
        weight, mixed_grad_ref, key_sum, value_sum, position_sum, semaphores,
    ) = refs
    row_count, heads = mixed_grad_ref.shape
    head_size = heads // head_count
    row_block = row_count // pieces
    scale = head_size ** (-0.5)
    copies = Copies(semaphores)
    rows_copies = copies.stack(row_refs, rows_ref)
    everything = slice(0, weight.shape[1])
    weight_copies_ = copies.weight(weight_refs, owners_ref, weight, everything)
    firsts = block_firsts(place_ref, pieces, row_block)
    key_sum[...] = jnp.zeros_like(key_sum)
    value_sum[...] = jnp.zeros_like(value_sum)
    position_sum[...] = jnp.zeros_like(position_sum)
    turn = (
        lax.broadcasted_iota(jnp.int32, (row_block, row_block), 0)
        + lax.broadcasted_iota(jnp.int32, (row_block, row_block), 1)
        == row_block - 1
    ).astype(LOW)
    wait(rows_copies + weight_copies_)
    mixed_grad_ref[...] = matmul(rows_ref[...], weight[:, 4 * heads : 5 * heads]).astype(LOW)
    for h in range(head_count):
        columns = slice(h * head_size, (h + 1) * head_size)
        content_total = jnp.zeros((1, head_size), FLOAT)
        position_total = jnp.zeros((1, head_size), FLOAT)
        for q in range(pieces):
            rows = pl.ds(q * row_block, row_block)
            mixed_grad = mixed_grad_ref[rows, columns]
            prob = prob_ref[h, rows, :]
            prob_float = prob.astype(FLOAT)
            prob_grad = times_transposed(mixed_grad, value_ref[:, columns])
            inner = jnp.sum(prob_grad * prob_float, axis=1, keepdims=True)
            score_grad = (prob_float * (prob_grad - inner)).astype(LOW)
            value_sum[:, columns] += outer_sum(prob, mixed_grad)
            key_sum[:, columns] += outer_sum(score_grad, content_rows_ref[rows, columns])
            turned = matmul(turn, score_grad).astype(LOW)
            content_part = matmul(turned, key_ref[:, columns]) * scale
            broad = jnp.concatenate([turned, jnp.zeros((row_block, row_block), LOW)], axis=1)
            broad = pltpu.roll(broad, 0, axis=1, stride=1, stride_axis=0)
            relative = relative_window(position_ref, firsts[q], row_block, columns)[...]
            position_part = matmul(broad, relative) * scale
            turned_rows = matmul(turn, position_rows_ref[rows, columns]).astype(LOW)
            total_ref = relative_window(position_sum, firsts[q], row_block, columns)
            total_ref[...] += outer_sum(broad, turned_rows)
            query_grad = (content_part + position_part).astype(LOW)
            qkv_grad_ref[rows, columns] = matmul(turn, query_grad).astype(LOW)
            content_total += jnp.sum(content_part, axis=0, keepdims=True)
            position_total += jnp.sum(position_part, axis=0, keepdims=True)
        bias_grad_ref[h : h + 1, :] = content_total
        bias_grad_ref[head_count + h : head_count + h + 1, :] = position_total
    for q in range(pieces):
        rows, plain = pl.ds(q * row_block, row_block), pl.ds(firsts[q], row_block)
        qkv_grad_ref[rows, heads : 2 * heads] = (key_sum[plain, :] * scale).astype(LOW)
        qkv_grad_ref[rows, 2 * heads :] = value_sum[plain, :].astype(LOW)
    position_grad_ref[...] = (position_sum[...] * scale).astype(LOW)

    @tiles(weight.shape[0])
    def _(features):
        write_parts(
            hi_ref, next_ref, own_ref, features,
            times_transposed(qkv_grad_ref[...], weight[features, : 3 * heads]),
        )


def attention_backward(place, owners, rows, weights, stored, head_count):
    row_count, features = len(rows) * rows[0].shape[0], rows[0].shape[1]
    position = stored[0]
    heads = position.shape[1]
    return call(
        functools.partial(
            attention_backward_kernel, pieces=len(rows), weights=len(weights),
            head_count=head_count,
        ),
        [
            ((row_count, features), LOW),
            ((row_count, 3 * heads), LOW),
            (position.shape, LOW),
            ((2 * head_count, heads // head_count), FLOAT),
        ]
        + row_parts(row_count, features),
        [
            pltpu.VMEM((features, 5 * heads), LOW),
            pltpu.VMEM((row_count, heads), LOW),
            pltpu.VMEM((row_count, heads), FLOAT),
            pltpu.VMEM((row_count, heads), FLOAT),
            pltpu.VMEM(position.shape, FLOAT),
            pltpu.SemaphoreType.DMA((len(rows) + weight_copies(weights, owners),)),
        ],
        8 * row_count * features * heads + 16 * heads * row_count**2,
        ("smem", place), ("smem", owners),
        *[("any", array) for array in list(rows) + list(weights)],
        *[("vmem", array) for array in stored],
    )


MARGIN = 8


def conv_matches(lengths_ref, row_count, taps):
    places = lax.broadcasted_iota(jnp.int32, (row_count, 1), 0)
    segment = segment_of(lengths_ref, places)
    valid = (segment < lengths_ref.shape[1]).astype(FLOAT)
    matches = []
    for t in range(taps):
        other = segment_of(lengths_ref, places + (t - taps // 2))
        matches.append((other == segment).astype(FLOAT))
    return valid, matches


def conv_lift_kernel(*refs, pieces, weights):
    place_ref, lengths_ref, owners_ref, taps_ref = refs[:4]
    refs = refs[4:]
    row_refs, refs = refs[:pieces], refs[pieces:]
    weight_refs, refs = refs[:weights], refs[weights:]
    rows_ref, lifted_ref, convolved_ref, sums_ref, weight, padded, semaphores = refs
    row_count, channels = convolved_ref.shape
    taps = taps_ref.shape[0]
    row_block = row_count // pieces
    copies = Copies(semaphores)
    rows_copies = copies.stack(row_refs, rows_ref)
    weight_copies_ = copies.weight(weight_refs, owners_ref, weight, slice(0, 2 * channels))
    firsts = block_firsts(place_ref, pieces, row_block)
    valid, matches = conv_matches(lengths_ref, row_count, taps)
    padded[:MARGIN, :] = jnp.zeros((MARGIN, channels), FLOAT)
    padded[MARGIN + row_count :, :] = jnp.zeros((MARGIN, channels), FLOAT)
    wait(rows_copies + weight_copies_)
    lifted = matmul(rows_ref[...], weight[...])
    for q in range(pieces):
        lifted_ref[pl.ds(firsts[q], row_block), :] = lifted[q * row_block : (q + 1) * row_block]
    gated = lifted_ref[:, :channels] * jax.nn.sigmoid(lifted_ref[:, channels:]) * valid
    padded[MARGIN : MARGIN + row_count, :] = gated
    convolved = jnp.zeros((row_count, channels), FLOAT)
    for t in range(taps):
        first = MARGIN + t - taps // 2
        convolved += taps_ref[t : t + 1, :] * matches[t] * padded[first : first + row_count, :]
    convolved_ref[...] = convolved
    masked = convolved * valid
    sums_ref[...] = jnp.zeros_like(sums_ref)
    sums_ref[0:1, :] = jnp.sum(masked, axis=0, keepdims=True)
    sums_ref[1:2, :] = jnp.sum(masked * convolved, axis=0, keepdims=True)
    sums_ref[2:3, :] = jnp.zeros((1, channels), FLOAT) + jnp.sum(valid, axis=0, keepdims=True)


def conv_lift(place, lengths, owners, taps, rows, weights):
    row_count, features = len(rows) * rows[0].shape[0], rows[0].shape[1]
    channels = taps.shape[1]
    return call(
        functools.partial(conv_lift_kernel, pieces=len(rows), weights=len(weights)),
        [
            ((row_count, features), LOW),
            ((row_count, 2 * channels), FLOAT),
            ((row_count, channels), FLOAT),
            ((8, channels), FLOAT),
        ],
        [
            pltpu.VMEM((features, 2 * channels), LOW),
            pltpu.VMEM((row_count + 2 * MARGIN, channels), FLOAT),
            pltpu.SemaphoreType.DMA((len(rows) + weight_copies(weights, owners),)),
        ],
        4 * row_count * features * channels,
        ("smem", place), ("smem", lengths), ("smem", owners), ("vmem", taps),
        *[("any", array) for array in list(rows) + list(weights)],
    )


def batch_scales(sums_ref):
    count = sums_ref[2:3, :]
    average = sums_ref[0:1, :] / count
    return count, average, lax.rsqrt(sums_ref[1:2, :] / count - average * average + EPSILON)


def conv_out_kernel(*refs, pieces, weights):
    place_ref, lengths_ref, owners_ref, affine_ref, sums_ref, convolved_ref = refs[:6]
    refs = refs[6:]
    weight_refs, refs = refs[:weights], refs[weights:]
    swished_ref, hi_ref, next_ref, own_ref, weight, plain, semaphores = refs
    row_count, channels = convolved_ref.shape
    row_block = row_count // pieces
    copies = Copies(semaphores)
    weight_copies_ = copies.weight(
        weight_refs, owners_ref, weight, slice(2 * channels, 3 * channels)
    )
    firsts = block_firsts(place_ref, pieces, row_block)
    places = lax.broadcasted_iota(jnp.int32, (row_count, 1), 0)
    valid = (segment_of(lengths_ref, places) < lengths_ref.shape[1]).astype(FLOAT)
    _, average, inverse = batch_scales(sums_ref)
    hatted = (convolved_ref[...] - average) * inverse
    normalized = hatted * affine_ref[0:1, :] + affine_ref[1:2, :]
    plain[...] = (normalized * jax.nn.sigmoid(normalized) * valid).astype(LOW)
    for q in range(pieces):
        swished_ref[q * row_block : (q + 1) * row_block, :] = plain[
            pl.ds(firsts[q], row_block), :
        ]
    wait(weight_copies_)

    @tiles(weight.shape[0])
    def _(features):
        write_parts(
            hi_ref, next_ref, own_ref, features, times_transposed(swished_ref[...], weight[features, :])
        )


def conv_out(place, lengths, owners, affine, sums, convolved, weights, pieces, features):
    row_count, channels = convolved.shape
    return call(
        functools.partial(conv_out_kernel, pieces=pieces, weights=len(weights)),
        [((row_count, channels), LOW)] + row_parts(row_count, features),
        [
            pltpu.VMEM((features, channels), LOW),
            pltpu.VMEM((row_count, channels), LOW),
            pltpu.SemaphoreType.DMA((weight_copies(weights, owners),)),
        ],
        2 * row_count * features * channels,
        ("smem", place), ("smem", lengths), ("smem", owners),
        ("vmem", affine), ("vmem", sums), ("vmem", convolved),
        *[("any", array) for array in weights],
    )


def conv_back_sums_kernel(*refs, pieces, weights):
    place_ref, lengths_ref, owners_ref, affine_ref, sums_ref, convolved_ref = refs[:6]
    refs = refs[6:]
    row_refs, refs = refs[:pieces], refs[pieces:]
    weight_refs, refs = refs[:weights], refs[weights:]
    rows_ref, normal_ref, back_ref, weight, plain, semaphores = refs
    row_count, channels = convolved_ref.shape
    row_block = row_count // pieces
    copies = Copies(semaphores)
    rows_copies = copies.stack(row_refs, rows_ref)
    weight_copies_ = copies.weight(
        weight_refs, owners_ref, weight, slice(2 * channels, 3 * channels)
    )
    firsts = block_firsts(place_ref, pieces, row_block)
    places = lax.broadcasted_iota(jnp.int32, (row_count, 1), 0)
    valid = (segment_of(lengths_ref, places) < lengths_ref.shape[1]).astype(FLOAT)
    _, average, inverse = batch_scales(sums_ref)
    hatted = (convolved_ref[...] - average) * inverse
    normalized = hatted * affine_ref[0:1, :] + affine_ref[1:2, :]
    squashed = jax.nn.sigmoid(normalized)
    wait(rows_copies + weight_copies_)
    product = matmul(rows_ref[...], weight[...])
    for q in range(pieces):
        plain[pl.ds(firsts[q], row_block), :] = product[q * row_block : (q + 1) * row_block]
    normal = plain[...] * valid * squashed * (1.0 + normalized * (1.0 - squashed))
    normal_ref[...] = normal
    back_ref[...] = jnp.zeros_like(back_ref)
    back_ref[0:1, :] = jnp.sum(normal, axis=0, keepdims=True)
    back_ref[1:2, :] = jnp.sum(normal * hatted, axis=0, keepdims=True)


def conv_back_sums(place, lengths, owners, affine, sums, convolved, rows, weights):
    row_count, channels = convolved.shape
    features = rows[0].shape[1]
    return call(
        functools.partial(conv_back_sums_kernel, pieces=len(rows), weights=len(weights)),
        [
            ((row_count, features), LOW), ((row_count, channels), FLOAT), ((8, channels), FLOAT)
        ],
        [
            pltpu.VMEM((features, channels), LOW),
            pltpu.VMEM((row_count, channels), FLOAT),
            pltpu.SemaphoreType.DMA((len(rows) + weight_copies(weights, owners),)),
        ],
        2 * row_count * features * channels,
        ("smem", place), ("smem", lengths), ("smem", owners),
        ("vmem", affine), ("vmem", sums), ("vmem", convolved),
        *[("any", array) for array in list(rows) + list(weights)],
    )


def conv_back_kernel(*refs, pieces, weights):
    (
        place_ref, lengths_ref, owners_ref, taps_ref, affine_ref, sums_ref, back_ref,
        convolved_ref, normal_ref, lifted_ref,
    ) = refs[:10]
    refs = refs[10:]
    weight_refs, refs = refs[:weights], refs[weights:]
    lifted_grad_ref, taps_grad_ref, hi_ref, next_ref, own_ref, weight, padded, padded_grad, plain, semaphores = refs
    row_count, channels = convolved_ref.shape
    taps = taps_ref.shape[0]
    row_block = row_count // pieces
    copies = Copies(semaphores)
    weight_copies_ = copies.weight(weight_refs, owners_ref, weight, slice(0, 2 * channels))
    firsts = block_firsts(place_ref, pieces, row_block)
    valid, matches = conv_matches(lengths_ref, row_count, taps)
    count, average, inverse = batch_scales(sums_ref)
    gain = affine_ref[0:1, :]
    hatted = (convolved_ref[...] - average) * inverse
    conv_grad = inverse * (
        normal_ref[...] * gain
        - valid * gain * (back_ref[0:1, :] + hatted * back_ref[1:2, :]) / count
    )
    value = lifted_ref[:, :channels]
    gate = jax.nn.sigmoid(lifted_ref[:, channels:])
    for scratch in (padded, padded_grad):
        scratch[:MARGIN, :] = jnp.zeros((MARGIN, channels), FLOAT)
        scratch[MARGIN + row_count :, :] = jnp.zeros((MARGIN, channels), FLOAT)
    padded[MARGIN : MARGIN + row_count, :] = value * gate * valid
    padded_grad[MARGIN : MARGIN + row_count, :] = conv_grad
    taps_grad_ref[...] = jnp.zeros_like(taps_grad_ref)
    gated_grad = jnp.zeros((row_count, channels), FLOAT)
    for t in range(taps):
        offset = t - taps // 2
        read = padded[MARGIN + offset : MARGIN + offset + row_count, :]
        taps_grad_ref[t : t + 1, :] = jnp.sum(
            matches[t] * read * conv_grad, axis=0, keepdims=True
        )
        back = padded_grad[MARGIN - offset : MARGIN - offset + row_count, :]
        gated_grad += taps_ref[t : t + 1, :] * matches[taps - 1 - t] * back
    gated_grad = gated_grad * valid
    plain[:, :channels] = (gated_grad * gate).astype(LOW)
    plain[:, channels:] = (gated_grad * value * gate * (1.0 - gate)).astype(LOW)
    for q in range(pieces):
        lifted_grad_ref[q * row_block : (q + 1) * row_block, :] = plain[
            pl.ds(firsts[q], row_block), :
        ]
    wait(weight_copies_)

    @tiles(weight.shape[0])
    def _(features):
        write_parts(
            hi_ref, next_ref, own_ref, features,
            times_transposed(lifted_grad_ref[...], weight[features, :]),
        )


def conv_back(
    place, lengths, owners, taps, affine, sums, back, convolved, normal, lifted, weights, pieces,
    features,
):
    row_count, channels = convolved.shape
    return call(
        functools.partial(conv_back_kernel, pieces=pieces, weights=len(weights)),
        [((row_count, 2 * channels), LOW), ((8, channels), FLOAT)] + row_parts(row_count, features),
        [
            pltpu.VMEM((features, 2 * channels), LOW),
            pltpu.VMEM((row_count + 2 * MARGIN, channels), FLOAT),
            pltpu.VMEM((row_count + 2 * MARGIN, channels), FLOAT),
            pltpu.VMEM((row_count, 2 * channels), LOW),
            pltpu.SemaphoreType.DMA((weight_copies(weights, owners),)),
        ],
        4 * row_count * features * channels,
        ("smem", place), ("smem", lengths), ("smem", owners),
        *[
            ("vmem", array)
            for array in (taps, affine, sums, back, convolved, normal, lifted)
        ],
        *[("any", array) for array in weights],
    )


def standardize(values):
    average = jnp.mean(values, axis=-1, keepdims=True)
    centred = values - average
    spread_of = jnp.mean(centred * centred, axis=-1, keepdims=True)
    scale = lax.rsqrt(spread_of + EPSILON)
    return centred * scale, scale


def norm_back(values, norm_gain, normed_grad):
    hat, scale = standardize(values)
    gained = normed_grad * norm_gain
    first = jnp.mean(gained, axis=-1, keepdims=True)
    second = jnp.mean(gained * hat, axis=-1, keepdims=True)
    grad = (gained - first - hat * second) * scale
    return grad, jnp.sum(normed_grad * hat, axis=0, keepdims=True)


def middle_kernel(next_ref, arrived_ref, sent_ref):
    first = next_ref.shape[0]
    sent_ref[...] = (
        next_ref[...].astype(FLOAT) + arrived_ref[first:, :].astype(FLOAT)
    ).astype(LOW)


def sum_rows(hi, next_part, own_part):
    arrived = swap(hi, "mp", 1)
    (sent,) = call(
        middle_kernel, [(next_part.shape, LOW)], [], next_part.size,
        ("vmem", next_part), ("vmem", arrived),
    )
    return own_part, arrived, swap(sent, "mp", 2)


def summed(own_ref, near_ref, far_ref):
    rows = own_ref.shape[0]
    return own_ref[...] + near_ref[:rows, :].astype(FLOAT) + far_ref[...].astype(FLOAT)


def all_rows(own):
    across = swap(own, "mp", 2)
    return [own, across, swap(own, "mp", 1), swap(across, "mp", 1)]


def step_kernel(
    own_ref, near_ref, far_ref, residual_ref, gain_ref, next_ref, normed_ref, *, factor
):
    residual = residual_ref[...].astype(FLOAT) + factor * summed(own_ref, near_ref, far_ref)
    next_ref[...] = residual
    normed_ref[...] = (standardize(residual)[0] * gain_ref[...]).astype(LOW)


def step(parts, residual, gain, factor):
    shape = parts[0].shape
    return call(
        functools.partial(step_kernel, factor=factor), [(shape, FLOAT), (shape, LOW)], [],
        8 * math.prod(shape),
        *[("vmem", array) for array in (*parts, residual, gain)],
    )


def turn_kernel(
    own_ref, near_ref, far_ref, residual_ref, gain_ref, out_grad_ref,
    result_ref, grad_ref, branch_ref, gain_grad_ref,
):
    residual = residual_ref[...] + 0.5 * summed(own_ref, near_ref, far_ref)
    gain = gain_ref[...]
    result_ref[...] = (standardize(residual)[0] * gain).astype(LOW)
    grad, gain_grad = norm_back(residual, gain, out_grad_ref[...].astype(FLOAT))
    grad_ref[...] = grad
    branch_ref[...] = (0.5 * grad).astype(LOW)
    gain_grad_ref[...] = gain_grad


def turn(parts, residual, gain, out_grad):
    shape = parts[0].shape
    return call(
        turn_kernel,
        [(shape, LOW), (shape, FLOAT), (shape, LOW), ((1, shape[1]), FLOAT)], [],
        16 * math.prod(shape),
        *[("vmem", array) for array in (*parts, residual, gain, out_grad)],
    )


def step_back_kernel(
    own_ref, near_ref, far_ref, residual_ref, gain_ref, grad_ref,
    next_ref, branch_ref, gain_grad_ref, *, factor,
):
    normed_grad = summed(own_ref, near_ref, far_ref)
    grad, gain_grad = norm_back(residual_ref[...].astype(FLOAT), gain_ref[...], normed_grad)
    grad = grad_ref[...] + grad
    next_ref[...] = grad
    branch_ref[...] = (factor * grad).astype(LOW)
    gain_grad_ref[...] = gain_grad


def step_back(parts, residual, gain, grad, factor):
    shape = parts[0].shape
    return call(
        functools.partial(step_back_kernel, factor=factor),
        [(shape, FLOAT), (shape, LOW), ((1, shape[1]), FLOAT)], [],
        16 * math.prod(shape),
        *[("vmem", array) for array in (*parts, residual, gain, grad)],
    )


def select_kernel(place_ref, *refs):
    pieces, target_ref = refs[:-1], refs[-1]
    row_block = pieces[0].shape[0]
    for piece, first in zip(pieces, block_firsts(place_ref, len(pieces), row_block)):
        target_ref[pl.ds(first, row_block), :] = piece[...]


def select_rows(place, pieces):
    row_block, features = pieces[0].shape
    (outcome,) = call(
        select_kernel, [((len(pieces) * row_block, features), pieces[0].dtype)], [], 0,
        ("smem", place), *[("vmem", piece) for piece in pieces],
    )
    return outcome


def finish_kernel(*refs, counts):
    sources, targets = refs[: 2 * len(counts)], refs[2 * len(counts) :]
    at = 0
    for i, count in enumerate(counts):
        total = sources[2 * i][...] + sources[2 * i + 1][...].astype(FLOAT)
        first = 0
        for target in targets[at : at + count]:
            last = first + target.shape[1]
            target[...] = total[:, first:last]
            first = last
        at += count


def finish(sums, widths, *tokens):
    rows = sums[0].kept.shape[0]
    parts, counts, left = [], [], list(widths)
    for part in sums:
        parts += [("vmem", part.kept), ("vmem", after(part.sent, *tokens))]
        count, total = 0, 0
        while total < part.kept.shape[1]:
            total, count = total + left.pop(0), count + 1
        counts.append(count)
    return call(
        functools.partial(finish_kernel, counts=tuple(counts)),
        [((rows, width), FLOAT) for width in widths], [], 0, *parts,
    )


def join_kernel(*refs):
    target, first = refs[-1], 0
    for kept, arrived in zip(refs[0:-1:2], refs[1:-1:2]):
        last = first + kept.shape[1]
        target[:, first:last] = kept[...] + arrived[...].astype(FLOAT)
        first = last


def join(sums):
    rows, width = sums[0].kept.shape[0], sum(part.kept.shape[1] for part in sums)
    parts = []
    for part in sums:
        parts += [("vmem", part.kept), ("vmem", part.sent)]
    return call(join_kernel, [((rows, width), FLOAT)], [], 0, *parts)[0]


def per_device(
    inputs,
    lengths,
    out_grad,
    first_norm,
    first_up,
    first_down,
    attention_norm,
    query_weight,
    key_weight,
    value_weight,
    position_weight,
    output_weight,
    content_bias,
    position_bias,
    convolution_norm,
    pointwise_in,
    depthwise_kernel,
    batch_gain,
    batch_shift,
    pointwise_out,
    second_norm,
    second_up,
    second_down,
    final_norm,
):
    row_count, feature_count = inputs.shape
    dp_size, mp_size = lax.axis_size("dp"), lax.axis_size("mp")
    dp_at, mp_at = lax.axis_index("dp"), lax.axis_index("mp")
    block, hidden = first_up.shape
    row_block = row_count // mp_size
    bias_rows, head_count = content_bias.shape
    head_size = bias_rows * dp_size
    heads = head_count * head_size
    local_channels, tap_count = depthwise_kernel.shape
    channels = local_channels * dp_size
    place = mp_at.reshape(1).astype(jnp.int32)

    places = jnp.arange(feature_count, dtype=jnp.int32)
    owners = dp_at ^ reversed_bits(places // block, dp_size)
    source = owners * block + places % block
    selection = (places[:, None] == source[None, :]).astype(LOW)
    block_places = jnp.arange(dp_size, dtype=jnp.int32)
    block_owners = (dp_at ^ reversed_bits(block_places, dp_size)).astype(jnp.int32)
    block_selection = (block_places[:, None] == block_owners[None, :]).astype(LOW)

    up_own = first_up.astype(LOW)
    small_own = jnp.concatenate(
        [
            part.reshape(-1)
            for part in (
                first_norm, attention_norm, convolution_norm, second_norm, final_norm,
                content_bias, position_bias, depthwise_kernel, batch_gain, batch_shift,
            )
        ]
    )
    small_own = after(small_own, up_own).astype(LOW)
    links = Links(4)
    up_spread = Spread(links, up_own)
    up_spread.go(ORDER)
    ups = up_spread.blocks
    down_own = after(first_down, ups[1]).astype(LOW)
    down_spread = Spread(links, down_own)
    down_spread.go(ORDER)
    downs = down_spread.blocks
    gates, mask = [downs[1], ups[5], ups[3]], dp_size // 2
    small_all = small_own[None]
    while mask:
        arrived = swap(small_all, "dp", mask)
        if gates:
            arrived = after(arrived, gates.pop())
        small_all = jnp.concatenate([small_all, arrived], axis=0)
        mask //= 2

    def gather(values, *tokens):
        return [lax.all_gather(after(values, *tokens), "dp", axis=0, tiled=True)]

    attention_own = jnp.concatenate(
        after(
            (query_weight, key_weight, value_weight, position_weight, output_weight), ups[3]
        ),
        axis=1,
    ).astype(LOW)
    attention_spread = Spread(links, attention_own)
    attention_spread.go(ORDER[:3])
    pointwise_in, pointwise_out, second_up, second_down = after(
        (pointwise_in, pointwise_out, second_up, second_down), downs[3]
    )
    convolution_own = jnp.concatenate(
        [pointwise_in.reshape(block, 2 * channels), pointwise_out], axis=1
    ).astype(LOW)
    second_own = jnp.concatenate([second_up, second_down], axis=1).astype(LOW)

    whole, first_half, second_half = (
        slice(0, hidden), slice(0, hidden), slice(hidden, 2 * hidden)
    )

    norms = small_all[:, : 5 * block].astype(FLOAT).reshape(dp_size, 5, block)
    norms = norms.transpose(1, 0, 2).reshape(5, 1, feature_count)
    first_gain, attention_gain, convolution_gain, second_gain, final_gain = norms
    plain_small = matmul(block_selection, small_all[:, 5 * block :])
    cut = bias_rows * head_count
    content_all = plain_small[:, :cut].reshape(head_size, head_count).T
    position_all = plain_small[:, cut : 2 * cut].reshape(head_size, head_count).T
    at = 2 * cut + local_channels * tap_count
    taps = plain_small[:, 2 * cut : at].reshape(channels, tap_count).T
    affine = jnp.stack(
        [
            plain_small[:, at : at + local_channels].reshape(channels),
            plain_small[:, at + local_channels :].reshape(channels),
        ]
    )

    arranged = matmul(
        jnp.concatenate(
            [
                lax.dynamic_slice_in_dim(
                    inputs, (mp_at ^ fixed_reversed(q, mp_size)) * row_block, row_block, axis=0
                )
                for q in range(mp_size)
            ],
            axis=0,
        ),
        selection,
    )
    own_out_grad = matmul(
        lax.dynamic_slice_in_dim(out_grad, mp_at * row_block, row_block, axis=0), selection
    ).astype(LOW)
    table_places = after(jnp.arange(2 * row_count, dtype=jnp.int32), ups[3])
    sin_table = position_table(table_places, row_count, feature_count)
    sin_table = matmul(sin_table, selection).astype(LOW)

    residual_zero = arranged[:row_block].astype(LOW)
    hat_a = standardize(arranged)[0]
    normed_a = (hat_a * first_gain).astype(LOW)
    hat_a = hat_a.astype(LOW)
    _, before_a, active_a, hi, next_part, own_part = ffn_call(
        ffn_forward_kernel, block_owners, [normed_a], ups, downs, whole, whole
    )
    attention_spread.go(ORDER[3:], hi)
    attention_all = attention_spread.blocks
    residual_one, own_b = step(sum_rows(hi, next_part, own_part), residual_zero, attention_gain, 0.5)
    second_all = gather(second_own, attention_all[3])
    convolution_spread = Spread(links, after(convolution_own, hi))
    convolution_spread.go(ORDER[:2])

    normed_b, mixed_rows, prob, content_rows, position_rows, keys, values, position, hi, next_part, own_part = (
        attention_forward(
            place, lengths, block_owners, all_rows(own_b), attention_all, sin_table, content_all,
            position_all,
        )
    )
    convolution_spread.go(ORDER[2:], hi)
    convolution_all = convolution_spread.blocks
    residual_two, own_c = step(sum_rows(hi, next_part, own_part), residual_one, convolution_gain, 1.0)

    normed_c, lifted, convolved, sums = conv_lift(
        place, lengths, block_owners, taps, all_rows(own_c), convolution_all
    )
    sums, _ = total_hops(sums, "dp")
    swished, hi, next_part, own_part = conv_out(
        place, lengths, block_owners, affine, sums, convolved, convolution_all, mp_size,
        feature_count,
    )
    residual_three, own_d = step(sum_rows(hi, next_part, own_part), residual_two, second_gain, 1.0)

    normed_d, before_d, active_d, hi, next_part, own_part = ffn_call(
        ffn_forward_kernel, block_owners, all_rows(own_d), second_all, second_all, first_half,
        second_half,
    )
    own_result, residual_grad, branch, final_gain_grad = turn(
        sum_rows(hi, next_part, own_part), residual_three, final_gain, own_out_grad
    )

    branch_rows, before_grad, hi, next_part, own_part = ffn_call(
        ffn_backward_kernel, block_owners, all_rows(branch), second_all, second_all, first_half,
        second_half, before_d,
    )
    second_down_sum, second_up_sum = (
        WeightSum((branch_rows, active_d)), WeightSum((normed_d, before_grad))
    )
    links = Links(2, apart=True)
    second_down_sum.advance(links=links)
    residual_grad, branch, second_gain_grad = step_back(
        sum_rows(hi, next_part, own_part), residual_three, second_gain, residual_grad, 1.0
    )

    branch_rows, normal, back_sums = conv_back_sums(
        place, lengths, block_owners, affine, sums, convolved, all_rows(branch), convolution_all
    )
    back_sums, hops = total_hops(back_sums, "dp")
    second_down_sum.advance(hops[-2], links=links)
    second_up_sum.advance(hops[-1], links=links)
    lifted_grad, taps_grad, hi, next_part, own_part = conv_back(
        place, lengths, block_owners, taps, affine, sums, back_sums, convolved, normal, lifted,
        convolution_all, mp_size, feature_count,
    )
    convolution_sum = WeightSum((normed_c, lifted_grad), (branch_rows, swished))
    convolution_sum.advance(second_up_sum.upper, links=links)
    parts = sum_rows(hi, next_part, own_part)
    second_down_sum.advance(parts[1], links=links)
    residual_grad, branch, convolution_gain_grad = step_back(
        parts, residual_two, convolution_gain, residual_grad, 1.0
    )
    first_row = dp_at * local_channels
    gain_piece = lax.dynamic_slice_in_dim(back_sums[1], first_row, local_channels)
    shift_piece = lax.dynamic_slice_in_dim(back_sums[0], first_row, local_channels)

    rows = all_rows(branch)
    second_up_sum.advance(rows[1], links=links)
    branch_rows, qkv_grad, position_grad, bias_grads, hi, next_part, own_part = attention_backward(
        place, block_owners, rows, attention_all,
        (position, prob, content_rows, position_rows, keys, values), head_count,
    )
    convolution_sum.advance(hi, links=links)
    attention_sum = WeightSum(
        (normed_b, qkv_grad), (sin_table, position_grad), (branch_rows, mixed_rows)
    )
    attention_sum.advance(hi, links=links)
    parts = sum_rows(hi, next_part, own_part)
    second_up_sum.advance(parts[1], links=links)
    residual_grad, branch, attention_gain_grad = step_back(
        parts, residual_one, attention_gain, residual_grad, 0.5
    )
    convolution_sum.advance(branch, links=links)

    branch_rows, before_grad, hi, next_part, own_part, first_gain_grad = ffn_call(
        ffn_backward_kernel, block_owners, all_rows(branch), ups, downs, whole, whole, before_a,
        hat_a,
    )
    half = hidden // 2
    first_sums = [
        WeightSum((branch_rows, active_a[:, :half])),
        WeightSum((branch_rows, active_a[:, half:])),
        WeightSum((normed_a, before_grad[:, :half])),
        WeightSum((normed_a, before_grad[:, half:])),
    ]

    plain_grads = jnp.concatenate(
        [
            bias_grads[:head_count].T.reshape(dp_size, cut),
            bias_grads[head_count:].T.reshape(dp_size, cut),
            taps_grad[:tap_count].T.reshape(dp_size, local_channels * tap_count),
        ],
        axis=1,
    )
    plain_grads = lax.dot_general(
        block_selection.astype(FLOAT), plain_grads, (((0,), (0,)), ((), ())),
        precision=lax.Precision.HIGHEST, preferred_element_type=FLOAT,
    )
    gain_grads = jnp.concatenate(
        [
            first_gain_grad, attention_gain_grad, convolution_gain_grad, second_gain_grad,
            final_gain_grad,
        ],
        axis=0,
    )
    gain_grads = gain_grads.reshape(5, dp_size, block).transpose(1, 0, 2)
    small_grads = jnp.concatenate([gain_grads.reshape(dp_size, 5 * block), plain_grads], axis=1)

    smalls, mask = [small_grads], [1]

    def small_step():
        if mask[0] < dp_size:
            kept = smalls[0].shape[0] // 2
            smalls[0] = smalls[0][:kept] + links.swap(smalls[0][kept:], mask[0])
            mask[0] *= 2

    down_a, down_b, up_a, up_b = first_sums
    small_step()
    for part in (
        down_a, attention_sum, down_b, attention_sum, None, down_a, up_a, down_b, up_b, down_a,
        None, up_a, down_b, up_b, up_a, up_b,
    ):
        if part is None:
            small_step()
        else:
            part.advance(links=links)
    while mask[0] < dp_size:
        small_step()
    for part in (second_down_sum, second_up_sum, convolution_sum, attention_sum, *first_sums):
        part.rest()

    parts = sum_rows(hi, next_part, own_part)
    residual_grad, _, _ = step_back(parts, residual_zero, first_gain, residual_grad, 1.0)
    second_down_grad, second_up_grad, convolution_in_grad, convolution_out_grad = finish(
        [second_down_sum, second_up_sum, convolution_sum],
        [hidden, hidden, 2 * channels, channels], parts[2],
    )
    attention_grads = finish([attention_sum], [heads] * 5)
    first_down_grad, first_up_grad = join(first_sums[:2]), join(first_sums[2:])

    def plain_order(own):
        pieces = all_rows(times_transposed(own, selection).astype(LOW))
        return select_rows(place, pieces)

    result = plain_order(after(own_result, hi))
    inputs_grad = plain_order(residual_grad.astype(LOW)).astype(FLOAT)

    small_grads = smalls[0][0]
    gain_grads = total_over(small_grads[: 5 * block].reshape(5, block), "mp")
    plain_grads = small_grads[5 * block :]

    return (
        result,
        inputs_grad,
        gain_grads[0],
        first_up_grad,
        first_down_grad,
        gain_grads[1],
        *attention_grads,
        plain_grads[:cut].reshape(bias_rows, head_count),
        plain_grads[cut : 2 * cut].reshape(bias_rows, head_count),
        gain_grads[2],
        convolution_in_grad.reshape(block, 2, channels),
        plain_grads[2 * cut :].reshape(local_channels, tap_count),
        gain_piece,
        shift_piece,
        convolution_out_grad,
        gain_grads[3],
        second_up_grad,
        second_down_grad,
        gain_grads[4],
    )


def solution(mesh):
    return jax.shard_map(
        per_device,
        mesh=mesh,
        in_specs=(
            P("dp", None),
            P("dp", None),
            P("dp", None),
            P("dp"),
            P("dp", "mp"),
            P("dp", "mp"),
            P("dp"),
            P("dp", "mp"),
            P("dp", "mp"),
            P("dp", "mp"),
            P("dp", "mp"),
            P("dp", "mp"),
            P("dp", "mp"),
            P("dp", "mp"),
            P("dp"),
            P("dp", None, "mp"),
            P(("mp", "dp"), None),
            P(("mp", "dp")),
            P(("mp", "dp")),
            P("dp", "mp"),
            P("dp"),
            P("dp", "mp"),
            P("dp", "mp"),
            P("dp"),
        ),
        out_specs=(
            P("dp", None),
            P("dp", None),
            P("dp"),
            P("dp", "mp"),
            P("dp", "mp"),
            P("dp"),
            P("dp", "mp"),
            P("dp", "mp"),
            P("dp", "mp"),
            P("dp", "mp"),
            P("dp", "mp"),
            P("dp", "mp"),
            P("dp", "mp"),
            P("dp"),
            P("dp", None, "mp"),
            P(("mp", "dp"), None),
            P(("mp", "dp")),
            P(("mp", "dp")),
            P("dp", "mp"),
            P("dp"),
            P("dp", "mp"),
            P("dp", "mp"),
            P("dp"),
        ),
        check_vma=False,
    )
```

```python
import functools
import math

import jax
import jax.numpy as jnp
from jax import lax
from jax.experimental import pallas as pl
from jax.experimental.pallas import tpu as pltpu
from jax.sharding import PartitionSpec as P

EPSILON = 1e-05
LOW = jnp.bfloat16
FLOAT = jnp.float32


def matmul(left_side, right_side):
    return jnp.dot(left_side, right_side, preferred_element_type=FLOAT)


def times_transposed(left_side, right_side):
    return lax.dot_general(
        left_side, right_side, (((1,), (1,)), ((), ())), preferred_element_type=FLOAT
    )


def outer_sum(left_side, right_side):
    return lax.dot_general(
        left_side, right_side, (((0,), (0,)), ((), ())), preferred_element_type=FLOAT
    )


def reversed_bits(places, size):
    outcome = places * 0
    mask, back = size // 2, 1
    while mask:
        outcome = outcome + ((places // back) % 2) * mask
        mask, back = mask // 2, back * 2
    return outcome


def swap(values, axis, mask):
    size = lax.axis_size(axis)
    return lax.ppermute(values, axis, [(i, i ^ mask) for i in range(size)])


def after(values, *tokens):
    return lax.optimization_barrier((values, tokens))[0] if tokens else values


class Links:
    def __init__(self, depth, apart=False):
        self.depth, self.apart, self.queues = depth, apart, {}

    def swap(self, values, mask, time=None):
        queue, depth = self.queues.setdefault(self.apart and mask == 1, []), self.depth
        if len(queue) >= depth:
            values = after(values, *queue[-2 * depth : len(queue) + 1 - depth])
        arrived = swap(values, "dp", mask)
        queue.append(arrived if time is None else held(arrived, time))
        return queue[-1]


ORDER = (4, 1, 2, 3, 5, 6, 7)


def pass_kernel(source_ref, target_ref):
    pass


def held(values, microseconds):
    return pl.pallas_call(
        pass_kernel,
        out_shape=jax.ShapeDtypeStruct(values.shape, values.dtype),
        in_specs=[pl.BlockSpec(memory_space=pl.ANY)],
        out_specs=pl.BlockSpec(memory_space=pl.ANY),
        input_output_aliases={0: 0},
        cost_estimate=pl.CostEstimate(
            flops=int(1.1e9 * microseconds), bytes_accessed=0, transcendentals=0
        ),
    )(values)


class Spread:
    def __init__(self, links, own):
        self.links, self.mask = links, lax.axis_size("dp") // 2
        while self.mask > 4:
            own = jnp.concatenate([own, links.swap(own, self.mask)], axis=0)
            self.mask //= 2
        self.blocks = [own] + [None] * (2 * self.mask - 1)

    def go(self, places, *tokens, time=None):
        for p in places:
            if p < len(self.blocks):
                top = 1 << (p.bit_length() - 1)
                self.blocks[p] = self.links.swap(
                    after(self.blocks[p - top], *tokens), self.mask // top,
                    time if p < 4 or time is None else 10,
                )


def spread(values, axis):
    mask = lax.axis_size(axis) // 2
    while mask:
        values = jnp.concatenate([values, swap(values, axis, mask)], axis=0)
        mask //= 2
    return values


def collect(values, axis, wire, mask=1):
    while mask < lax.axis_size(axis):
        half = values.shape[0] // 2
        values = values[:half] + swap(values[half:].astype(wire), axis, mask).astype(FLOAT)
        mask *= 2
    return values


def total_over(values, axis):
    mask = 1
    while mask < lax.axis_size(axis):
        values = values + swap(values, axis, mask)
        mask *= 2
    return values


def total_hops(values, axis):
    arrivals, mask = [], lax.axis_size(axis) // 2
    while mask:
        arrivals.append(swap(values, axis, mask))
        values = values + arrivals[-1]
        mask //= 2
    return values, arrivals


class WeightSum:
    def __init__(self, *pairs):
        self.pairs, self.mask = pairs, 0

    def advance(self, *tokens, links=None, later=()):
        if not self.mask:
            half = self.pairs[0][0].shape[1] // 2
            upper = [outer_sum(left[:, half:], right).astype(LOW) for left, right in self.pairs]
            lower = [
                outer_sum(after(left[:, :half], *later), right) for left, right in self.pairs
            ]
            self.upper, self.kept = jnp.concatenate(upper, axis=1), jnp.concatenate(lower, axis=1)
            self.upper, self.mask = after(self.upper, *tokens), 1
        else:
            total = self.kept + after(self.sent, *tokens).astype(FLOAT)
            half = total.shape[0] // 2
            self.upper, self.kept = total[half:].astype(LOW), total[:half]
        if links is None:
            self.sent = swap(self.upper, "dp", self.mask)
        else:
            self.sent = links.swap(self.upper, self.mask)
        self.mask *= 2

    def rest(self, *tokens):
        while self.mask < lax.axis_size("dp"):
            self.advance(*tokens)


def position_table(places, row_count, feature_count):
    rates = jnp.exp(
        jnp.arange(0, feature_count, 2).astype(FLOAT) * (-math.log(10000.0) / feature_count)
    )
    stride = 32
    count = places.shape[0] // stride
    coarse = (row_count - 1 - stride * places[:count]).astype(FLOAT)[:, None] * rates[None, :]
    fine = -places[:stride].astype(FLOAT)[:, None] * rates[None, :]
    coarse_sin, coarse_cos = jnp.sin(coarse)[:, None], jnp.cos(coarse)[:, None]
    fine_sin, fine_cos = jnp.sin(fine)[None], jnp.cos(fine)[None]
    sines = coarse_sin * fine_cos + coarse_cos * fine_sin
    cosines = coarse_cos * fine_cos - coarse_sin * fine_sin
    table = jnp.concatenate([sines, cosines], axis=2).astype(LOW)
    return table.reshape(places.shape[0], feature_count)


def fixed_reversed(place, size):
    outcome, mask = 0, size // 2
    while mask:
        outcome, place, mask = outcome + (place % 2) * mask, place // 2, mask // 2
    return outcome


def relative_window(position_ref, first, row_block, columns):
    row_count = position_ref.shape[0] // 2
    start = pl.multiple_of(row_count - row_block - first, row_block)
    return position_ref.at[pl.ds(start, row_count + row_block), columns]


def in_smem():
    return pl.BlockSpec(memory_space=pltpu.SMEM)


def in_vmem():
    return pl.BlockSpec(memory_space=pltpu.VMEM)


def in_hbm():
    return pl.BlockSpec(memory_space=pltpu.HBM)


def anywhere():
    return pl.BlockSpec(memory_space=pl.ANY)


def call(kernel, outs, scratch, flops, *operands, limit=6, saved=()):
    places = dict(smem=in_smem, vmem=in_vmem, any=anywhere, hbm=in_hbm)
    count, inner = len(operands), len(scratch)

    def saving(*refs):
        sources, targets, rest = (
            refs[:count], list(refs[count : count + len(outs)]), refs[count + len(outs) :]
        )
        kept, held_refs, semaphores = rest[:inner], rest[inner:-1], rest[-1]
        copies = [
            pltpu.make_async_copy(ref, targets[i], semaphores.at[n])
            for n, (i, ref) in enumerate(zip(saved, held_refs))
        ]
        for i, ref in zip(saved, held_refs):
            targets[i] = ref

        def save():
            for copy in copies:
                copy.start()

        kernel(*sources, *targets, *kept, save=save)
        for copy in copies:
            copy.wait()

    extra = []
    if saved:
        extra = [pltpu.VMEM(*outs[i]) for i in saved] + [pltpu.SemaphoreType.DMA((len(saved),))]
    return pl.pallas_call(
        saving if saved else kernel,
        out_shape=tuple(jax.ShapeDtypeStruct(shape, kind) for shape, kind in outs),
        in_specs=[places[place]() for place, _ in operands],
        out_specs=tuple(in_hbm() if i in saved else in_vmem() for i in range(len(outs))),
        scratch_shapes=list(scratch) + extra,
        compiler_params=pltpu.CompilerParams(
            vmem_limit_bytes=(50 if scratch else limit) * 2**20
        ),
        cost_estimate=pl.CostEstimate(flops=flops, bytes_accessed=0, transcendentals=0),
    )(*[array for _, array in operands])


class Copies:
    def __init__(self, semaphores):
        self.semaphores, self.count = semaphores, 0

    def start(self, source, target):
        copy = pltpu.make_async_copy(source, target, self.semaphores.at[self.count])
        copy.start()
        self.count += 1
        return copy

    def stack(self, sources, target, columns=None):
        copies, block = [], target.shape[0] // len(sources)
        for p, source in enumerate(sources):
            if columns is not None:
                source = source.at[:, columns]
            copies.append(self.start(source, target.at[pl.ds(p * block, block)]))
        return copies

    def weight(self, sources, target, columns):
        if len(sources) > 1:
            return self.stack(sources, target, columns)
        return [self.start(sources[0].at[:, columns], target)]


def wait(copies):
    for copy in copies:
        copy.wait()


TILE = 256


def write_parts(hi_ref, next_ref, own_ref, columns, product):
    half, own = hi_ref.shape[0], own_ref.shape[0]
    hi_ref[:, columns] = product[half:].astype(LOW)
    next_ref[:, columns] = product[own:half].astype(LOW)
    own_ref[:, columns] = product[:own]


def tiles(count):
    def loop(body):
        @pl.loop(0, count // TILE)
        def _(t):
            body(pl.ds(pl.multiple_of(t * TILE, TILE), TILE))

    return loop


def ffn_forward_kernel(*refs, pieces, weights, up_columns, down_columns, save):
    row_refs, refs = refs[:pieces], refs[pieces:]
    up_refs, refs = refs[:weights], refs[weights:]
    down_refs, refs = refs[:weights], refs[weights:]
    rows_ref, before_ref, active_ref, up, down, hi_ref, next_ref, own_ref, semaphores = refs
    copies = Copies(semaphores)
    rows_copies = copies.stack(row_refs, rows_ref)
    up_copies = copies.weight(up_refs, up, up_columns)
    down_copies = copies.weight(down_refs, down, down_columns)
    wait(rows_copies + up_copies)

    @tiles(up.shape[1])
    def _(columns):
        before = matmul(rows_ref[...], up[:, columns])
        before_ref[:, columns] = before.astype(LOW)
        active_ref[:, columns] = (before * jax.nn.sigmoid(before)).astype(LOW)

    wait(down_copies)
    save()

    @tiles(down.shape[0])
    def _(features):
        write_parts(
            hi_ref, next_ref, own_ref, features, times_transposed(active_ref[...], down[features, :])
        )


def ffn_backward_kernel(*refs, pieces, weights, up_columns, down_columns, gains, save):
    if gains:
        hat_ref, gain_grad_ref, refs = refs[-10], refs[-4], refs[:-10] + refs[-9:-4] + refs[-3:]
    row_refs, refs = refs[:pieces], refs[pieces:]
    up_refs, refs = refs[:weights], refs[weights:]
    down_refs, refs = refs[:weights], refs[weights:]
    before_ref, rows_ref, grad_ref, hi_ref, next_ref, own_ref, up, down, semaphores = refs
    copies = Copies(semaphores)
    rows_copies = copies.stack(row_refs, rows_ref)
    down_copies = copies.weight(down_refs, down, down_columns)
    up_copies = copies.weight(up_refs, up, up_columns)
    wait(rows_copies + down_copies)

    @tiles(down.shape[1])
    def _(columns):
        before = before_ref[:, columns].astype(FLOAT)
        squashed = jax.nn.sigmoid(before)
        grad = matmul(rows_ref[...], down[:, columns])
        grad_ref[:, columns] = (grad * squashed * (1.0 + before * (1.0 - squashed))).astype(LOW)

    save()

    wait(up_copies)

    @tiles(up.shape[0])
    def _(features):
        product = times_transposed(grad_ref[...], up[features, :])
        write_parts(hi_ref, next_ref, own_ref, features, product)
        if gains:
            gain_grad_ref[:, features] = jnp.sum(
                product * hat_ref[:, features].astype(FLOAT), axis=0, keepdims=True
            )


def row_parts(rows, features):
    return [
        ((rows // 2, features), LOW), ((rows // 4, features), LOW), ((rows // 4, features), FLOAT)
    ]


def ffn_call(
    kernel, rows, ups, downs, up_columns, down_columns, before=None, hat=None
):
    row_count = len(rows) * rows[0].shape[0]
    features = rows[0].shape[1]
    hidden = up_columns.stop - up_columns.start
    outs = [((row_count, features), LOW)]
    outs += [((row_count, hidden), LOW)] * (2 if before is None else 1)
    weight = ((features, hidden), LOW)
    if before is None:
        outs += [weight] * 2
    count = len(rows) + 2 * len(ups)
    operands = [("any", array) for array in rows]
    operands += [("any" if len(ups) > 1 else "hbm", array) for array in list(ups) + list(downs)]
    if before is not None:
        operands.append(("vmem", before))
        kernel = functools.partial(kernel, gains=hat is not None)
    outs += row_parts(row_count, features)
    if hat is not None:
        operands.append(("vmem", hat))
        outs.append(((1, features), FLOAT))
    return call(
        functools.partial(
            kernel, pieces=len(rows), weights=len(ups), up_columns=up_columns,
            down_columns=down_columns,
        ),
        outs,
        [pltpu.VMEM(*weight)] * (0 if before is None else 2)
        + [pltpu.SemaphoreType.DMA((count,))],
        4 * row_count * features * hidden,
        *operands,
        saved=(0, 1, 2, 3, 4) if before is None else (0, 1),
    )


def segment_of(lengths_ref, places):
    bound, segment = 0, jnp.zeros(places.shape, jnp.int32)
    for s in range(lengths_ref.shape[1]):
        bound = bound + lengths_ref[0, s]
        segment = segment + (places >= bound).astype(jnp.int32)
    return segment


def block_firsts(place_ref, blocks, row_block):
    place = place_ref[0]
    return [
        pl.multiple_of((place ^ fixed_reversed(q, blocks)) * row_block, row_block)
        for q in range(blocks)
    ]


def attention_forward_kernel(*refs, pieces, weights, save):
    place_ref, lengths_ref, content_ref, shift_ref = refs[:4]
    refs = refs[4:]
    row_refs, refs = refs[:pieces], refs[pieces:]
    weight_refs, refs = refs[:weights], refs[weights:]
    (
        table_ref,
        rows_ref, mixed_ref, prob_ref, content_rows_ref, position_rows_ref, key_ref, value_ref,
        position_ref, weight, hi_ref, next_ref, own_ref,
        table, qkv, semaphores,
    ) = refs
    row_count, heads = mixed_ref.shape
    head_count, head_size = content_ref.shape
    row_block = row_count // pieces
    window = row_count + row_block
    copies = Copies(semaphores)
    rows_copies = copies.stack(row_refs, rows_ref)
    everything = slice(0, weight.shape[1])
    weight_copies_ = copies.weight(weight_refs, weight, everything)
    table_copy = copies.start(table_ref, table)
    firsts = block_firsts(place_ref, pieces, row_block)
    wait(rows_copies + weight_copies_)

    @tiles(3 * heads)
    def _(columns):
        qkv[:, columns] = matmul(rows_ref[...], weight[:, columns])

    table_copy.wait()

    @tiles(table.shape[0])
    def _(places):
        position_ref[places, :] = matmul(
            table[places, :], weight[:, 3 * heads : 4 * heads]
        ).astype(LOW)

    for q in range(pieces):
        rows = pl.ds(q * row_block, row_block)
        key_ref[pl.ds(firsts[q], row_block), :] = qkv[rows, heads : 2 * heads].astype(LOW)
        value_ref[pl.ds(firsts[q], row_block), :] = qkv[rows, 2 * heads :].astype(LOW)

    along = lax.broadcasted_iota(jnp.int32, (1, row_count), 1)
    column_segment = segment_of(lengths_ref, along)
    for q in range(pieces):
        rows = pl.ds(q * row_block, row_block)
        down = lax.broadcasted_iota(jnp.int32, (row_block, 1), 0) + firsts[q]
        matching = segment_of(lengths_ref, down) == column_segment
        for h in range(head_count):
            columns = slice(h * head_size, (h + 1) * head_size)
            query = qkv[rows, columns]
            with_content = (query + content_ref[h : h + 1, :]).astype(LOW)
            with_position = (query + shift_ref[h : h + 1, :]).astype(LOW)
            content_rows_ref[rows, columns] = with_content
            position_rows_ref[rows, columns] = with_position
            direct = times_transposed(with_content, key_ref[:, columns])
            relative = relative_window(position_ref, firsts[q], row_block, columns)[...]
            broad = times_transposed(with_position, relative)
            broad = pltpu.roll(
                broad, window - (row_block - 1), axis=1, stride=1, stride_axis=0
            )
            scores = (direct + broad[:, :row_count]) * head_size ** (-0.5)
            scores = jnp.where(matching, scores, -1e30)
            exponent = jnp.exp(scores - jnp.max(scores, axis=1, keepdims=True))
            prob = (exponent / jnp.sum(exponent, axis=1, keepdims=True)).astype(LOW)
            prob_ref[h, rows, :] = prob
            mixed_ref[rows, columns] = matmul(prob, value_ref[:, columns]).astype(LOW)

    save()

    @tiles(weight.shape[0])
    def _(features):
        write_parts(
            hi_ref, next_ref, own_ref, features,
            times_transposed(mixed_ref[...], weight[features, 4 * heads : 5 * heads]),
        )


def attention_forward(place, lengths, rows, weights, table, content_bias, position_bias):
    row_count, features = len(rows) * rows[0].shape[0], rows[0].shape[1]
    head_count, head_size = content_bias.shape
    heads = head_count * head_size
    row_array = ((row_count, heads), LOW)
    return call(
        functools.partial(attention_forward_kernel, pieces=len(rows), weights=len(weights)),
        [
            ((row_count, features), LOW), row_array,
            ((head_count, row_count, row_count), LOW),
            row_array, row_array, row_array, row_array,
            ((2 * row_count, heads), LOW), ((features, 5 * heads), LOW),
        ]
        + row_parts(row_count, features),
        [
            pltpu.VMEM(table.shape, LOW),
            pltpu.VMEM((row_count, 3 * heads), FLOAT),
            pltpu.SemaphoreType.DMA((len(rows) + len(weights) + 1,)),
        ],
        12 * row_count * features * heads + 9 * heads * row_count**2,
        ("smem", place), ("smem", lengths),
        ("vmem", content_bias), ("vmem", position_bias),
        *[("any", array) for array in list(rows) + list(weights)],
        ("hbm", table),
        saved=tuple(range(9)),
    )


def attention_backward_kernel(*refs, pieces, weights, head_count, save):
    place_ref, refs = refs[0], refs[1:]
    row_refs, refs = refs[:pieces], refs[pieces:]
    weight_refs, refs = refs[:weights], refs[weights:]
    (
        position_ref, prob_ref, content_rows_ref, position_rows_ref, key_ref, value_ref,
        rows_ref, qkv_grad_ref, position_grad_ref, bias_grad_ref, hi_ref, next_ref, own_ref,
        weight, mixed_grad_ref, key_sum, value_sum, position_sum, semaphores,
    ) = refs
    row_count, heads = mixed_grad_ref.shape
    head_size = heads // head_count
    row_block = row_count // pieces
    scale = head_size ** (-0.5)
    copies = Copies(semaphores)
    rows_copies = copies.stack(row_refs, rows_ref)
    everything = slice(0, weight.shape[1])
    weight_copies_ = copies.weight(weight_refs, weight, everything)
    firsts = block_firsts(place_ref, pieces, row_block)
    key_sum[...] = jnp.zeros_like(key_sum)
    value_sum[...] = jnp.zeros_like(value_sum)
    position_sum[...] = jnp.zeros_like(position_sum)
    turn = (
        lax.broadcasted_iota(jnp.int32, (row_block, row_block), 0)
        + lax.broadcasted_iota(jnp.int32, (row_block, row_block), 1)
        == row_block - 1
    ).astype(LOW)
    wait(rows_copies + weight_copies_)
    mixed_grad_ref[...] = matmul(rows_ref[...], weight[:, 4 * heads : 5 * heads]).astype(LOW)
    for h in range(head_count):
        columns = slice(h * head_size, (h + 1) * head_size)
        content_total = jnp.zeros((1, head_size), FLOAT)
        position_total = jnp.zeros((1, head_size), FLOAT)
        for q in range(pieces):
            rows = pl.ds(q * row_block, row_block)
            mixed_grad = mixed_grad_ref[rows, columns]
            prob = prob_ref[h, rows, :]
            prob_float = prob.astype(FLOAT)
            prob_grad = times_transposed(mixed_grad, value_ref[:, columns])
            inner = jnp.sum(prob_grad * prob_float, axis=1, keepdims=True)
            score_grad = (prob_float * (prob_grad - inner)).astype(LOW)
            value_sum[:, columns] += outer_sum(prob, mixed_grad)
            key_sum[:, columns] += outer_sum(score_grad, content_rows_ref[rows, columns])
            turned = matmul(turn, score_grad).astype(LOW)
            content_part = matmul(turned, key_ref[:, columns]) * scale
            broad = jnp.concatenate([turned, jnp.zeros((row_block, row_block), LOW)], axis=1)
            broad = pltpu.roll(broad, 0, axis=1, stride=1, stride_axis=0)
            relative = relative_window(position_ref, firsts[q], row_block, columns)[...]
            position_part = matmul(broad, relative) * scale
            turned_rows = matmul(turn, position_rows_ref[rows, columns]).astype(LOW)
            total_ref = relative_window(position_sum, firsts[q], row_block, columns)
            total_ref[...] += outer_sum(broad, turned_rows)
            query_grad = (content_part + position_part).astype(LOW)
            qkv_grad_ref[rows, columns] = matmul(turn, query_grad).astype(LOW)
            content_total += jnp.sum(content_part, axis=0, keepdims=True)
            position_total += jnp.sum(position_part, axis=0, keepdims=True)
        bias_grad_ref[h : h + 1, :] = content_total
        bias_grad_ref[head_count + h : head_count + h + 1, :] = position_total
    for q in range(pieces):
        rows, plain = pl.ds(q * row_block, row_block), pl.ds(firsts[q], row_block)
        qkv_grad_ref[rows, heads : 2 * heads] = (key_sum[plain, :] * scale).astype(LOW)
        qkv_grad_ref[rows, 2 * heads :] = value_sum[plain, :].astype(LOW)
    position_grad_ref[...] = (position_sum[...] * scale).astype(LOW)

    save()

    @tiles(weight.shape[0])
    def _(features):
        write_parts(
            hi_ref, next_ref, own_ref, features,
            times_transposed(qkv_grad_ref[...], weight[features, : 3 * heads]),
        )


def attention_backward(place, rows, weights, stored, head_count):
    row_count, features = len(rows) * rows[0].shape[0], rows[0].shape[1]
    position = stored[0]
    heads = position.shape[1]
    return call(
        functools.partial(
            attention_backward_kernel, pieces=len(rows), weights=len(weights),
            head_count=head_count,
        ),
        [
            ((row_count, features), LOW),
            ((row_count, 3 * heads), LOW),
            (position.shape, LOW),
            ((2 * head_count, heads // head_count), FLOAT),
        ]
        + row_parts(row_count, features),
        [
            pltpu.VMEM((features, 5 * heads), LOW),
            pltpu.VMEM((row_count, heads), LOW),
            pltpu.VMEM((row_count, heads), FLOAT),
            pltpu.VMEM((row_count, heads), FLOAT),
            pltpu.VMEM(position.shape, FLOAT),
            pltpu.SemaphoreType.DMA((len(rows) + len(weights),)),
        ],
        8 * row_count * features * heads + 16 * heads * row_count**2,
        ("smem", place),
        *[("any", array) for array in rows],
        *[("any" if len(weights) > 1 else "hbm", array) for array in weights],
        *[("vmem", array) for array in stored],
        saved=(0, 1, 2),
    )


MARGIN = 8


def conv_matches(lengths_ref, row_count, taps):
    places = lax.broadcasted_iota(jnp.int32, (row_count, 1), 0)
    segment = segment_of(lengths_ref, places)
    valid = (segment < lengths_ref.shape[1]).astype(FLOAT)
    matches = []
    for t in range(taps):
        other = segment_of(lengths_ref, places + (t - taps // 2))
        matches.append((other == segment).astype(FLOAT))
    return valid, matches


def conv_lift_kernel(*refs, pieces, weights, save):
    place_ref, lengths_ref, taps_ref = refs[:3]
    refs = refs[3:]
    row_refs, refs = refs[:pieces], refs[pieces:]
    weight_refs, refs = refs[:weights], refs[weights:]
    rows_ref, lifted_ref, weight, convolved_ref, sums_ref, padded, semaphores = refs
    row_count, channels = convolved_ref.shape
    taps = taps_ref.shape[0]
    row_block = row_count // pieces
    copies = Copies(semaphores)
    rows_copies = copies.stack(row_refs, rows_ref)
    weight_copies_ = copies.weight(weight_refs, weight, slice(0, 3 * channels))
    firsts = block_firsts(place_ref, pieces, row_block)
    valid, matches = conv_matches(lengths_ref, row_count, taps)
    padded[:MARGIN, :] = jnp.zeros((MARGIN, channels), FLOAT)
    padded[MARGIN + row_count :, :] = jnp.zeros((MARGIN, channels), FLOAT)
    wait(rows_copies + weight_copies_)
    lifted = matmul(rows_ref[...], weight[:, : 2 * channels])
    for q in range(pieces):
        lifted_ref[pl.ds(firsts[q], row_block), :] = lifted[q * row_block : (q + 1) * row_block]
    gated = lifted_ref[:, :channels] * jax.nn.sigmoid(lifted_ref[:, channels:]) * valid
    padded[MARGIN : MARGIN + row_count, :] = gated
    convolved = jnp.zeros((row_count, channels), FLOAT)
    for t in range(taps):
        first = MARGIN + t - taps // 2
        convolved += taps_ref[t : t + 1, :] * matches[t] * padded[first : first + row_count, :]
    convolved_ref[...] = convolved
    save()

    masked = convolved * valid
    sums_ref[...] = jnp.zeros_like(sums_ref)
    sums_ref[0:1, :] = jnp.sum(masked, axis=0, keepdims=True)
    sums_ref[1:2, :] = jnp.sum(masked * convolved, axis=0, keepdims=True)
    sums_ref[2:3, :] = jnp.zeros((1, channels), FLOAT) + jnp.sum(valid, axis=0, keepdims=True)


def conv_lift(place, lengths, taps, rows, weights):
    row_count, features = len(rows) * rows[0].shape[0], rows[0].shape[1]
    channels = taps.shape[1]
    return call(
        functools.partial(conv_lift_kernel, pieces=len(rows), weights=len(weights)),
        [
            ((row_count, features), LOW),
            ((row_count, 2 * channels), FLOAT),
            ((features, 3 * channels), LOW),
            ((row_count, channels), FLOAT),
            ((8, channels), FLOAT),
        ],
        [
            pltpu.VMEM((row_count + 2 * MARGIN, channels), FLOAT),
            pltpu.SemaphoreType.DMA((len(rows) + len(weights),)),
        ],
        4 * row_count * features * channels,
        ("smem", place), ("smem", lengths), ("vmem", taps),
        *[("any", array) for array in rows],
        *[("any" if len(weights) > 1 else "hbm", array) for array in weights],
        saved=(0, 1, 2),
    )


def batch_scales(sums_ref):
    count = sums_ref[2:3, :]
    average = sums_ref[0:1, :] / count
    return count, average, lax.rsqrt(sums_ref[1:2, :] / count - average * average + EPSILON)


def conv_out_kernel(*refs, pieces, weights, save):
    place_ref, lengths_ref, affine_ref, sums_ref, convolved_ref = refs[:5]
    refs = refs[5:]
    weight_refs, refs = refs[:weights], refs[weights:]
    swished_ref, hi_ref, next_ref, own_ref, weight, plain, semaphores = refs
    row_count, channels = convolved_ref.shape
    row_block = row_count // pieces
    copies = Copies(semaphores)
    weight_copies_ = copies.weight(
        weight_refs, weight, slice(2 * channels, 3 * channels)
    )
    firsts = block_firsts(place_ref, pieces, row_block)
    places = lax.broadcasted_iota(jnp.int32, (row_count, 1), 0)
    valid = (segment_of(lengths_ref, places) < lengths_ref.shape[1]).astype(FLOAT)
    _, average, inverse = batch_scales(sums_ref)
    hatted = (convolved_ref[...] - average) * inverse
    normalized = hatted * affine_ref[0:1, :] + affine_ref[1:2, :]
    plain[...] = (normalized * jax.nn.sigmoid(normalized) * valid).astype(LOW)
    for q in range(pieces):
        swished_ref[q * row_block : (q + 1) * row_block, :] = plain[
            pl.ds(firsts[q], row_block), :
        ]
    save()

    wait(weight_copies_)

    @tiles(weight.shape[0])
    def _(features):
        write_parts(
            hi_ref, next_ref, own_ref, features, times_transposed(swished_ref[...], weight[features, :])
        )


def conv_out(place, lengths, affine, sums, convolved, weights, pieces, features):
    row_count, channels = convolved.shape
    return call(
        functools.partial(conv_out_kernel, pieces=pieces, weights=len(weights)),
        [((row_count, channels), LOW)] + row_parts(row_count, features),
        [
            pltpu.VMEM((features, channels), LOW),
            pltpu.VMEM((row_count, channels), LOW),
            pltpu.SemaphoreType.DMA((len(weights),)),
        ],
        2 * row_count * features * channels,
        ("smem", place), ("smem", lengths),
        ("vmem", affine), ("vmem", sums), ("vmem", convolved),
        *[("any" if len(weights) > 1 else "hbm", array) for array in weights],
        saved=(0,),
    )


def conv_back_sums_kernel(*refs, pieces, weights, save):
    place_ref, lengths_ref, affine_ref, sums_ref, convolved_ref = refs[:5]
    refs = refs[5:]
    row_refs, refs = refs[:pieces], refs[pieces:]
    weight_refs, refs = refs[:weights], refs[weights:]
    rows_ref, normal_ref, back_ref, weight, plain, semaphores = refs
    row_count, channels = convolved_ref.shape
    row_block = row_count // pieces
    copies = Copies(semaphores)
    rows_copies = copies.stack(row_refs, rows_ref)
    weight_copies_ = copies.weight(
        weight_refs, weight, slice(2 * channels, 3 * channels)
    )
    firsts = block_firsts(place_ref, pieces, row_block)
    places = lax.broadcasted_iota(jnp.int32, (row_count, 1), 0)
    valid = (segment_of(lengths_ref, places) < lengths_ref.shape[1]).astype(FLOAT)
    _, average, inverse = batch_scales(sums_ref)
    hatted = (convolved_ref[...] - average) * inverse
    normalized = hatted * affine_ref[0:1, :] + affine_ref[1:2, :]
    squashed = jax.nn.sigmoid(normalized)
    wait(rows_copies + weight_copies_)
    product = matmul(rows_ref[...], weight[...])
    for q in range(pieces):
        plain[pl.ds(firsts[q], row_block), :] = product[q * row_block : (q + 1) * row_block]
    save()

    normal = plain[...] * valid * squashed * (1.0 + normalized * (1.0 - squashed))
    normal_ref[...] = normal
    back_ref[...] = jnp.zeros_like(back_ref)
    back_ref[0:1, :] = jnp.sum(normal, axis=0, keepdims=True)
    back_ref[1:2, :] = jnp.sum(normal * hatted, axis=0, keepdims=True)


def conv_back_sums(place, lengths, affine, sums, convolved, rows, weights):
    row_count, channels = convolved.shape
    features = rows[0].shape[1]
    return call(
        functools.partial(conv_back_sums_kernel, pieces=len(rows), weights=len(weights)),
        [
            ((row_count, features), LOW), ((row_count, channels), FLOAT), ((8, channels), FLOAT)
        ],
        [
            pltpu.VMEM((features, channels), LOW),
            pltpu.VMEM((row_count, channels), FLOAT),
            pltpu.SemaphoreType.DMA((len(rows) + len(weights),)),
        ],
        2 * row_count * features * channels,
        ("smem", place), ("smem", lengths),
        ("vmem", affine), ("vmem", sums), ("vmem", convolved),
        *[("any", array) for array in rows],
        *[("any" if len(weights) > 1 else "hbm", array) for array in weights],
        saved=(0,),
    )


def conv_back_kernel(*refs, pieces, weights, save):
    (
        place_ref, lengths_ref, taps_ref, affine_ref, sums_ref, back_ref,
        convolved_ref, normal_ref, lifted_ref,
    ) = refs[:9]
    refs = refs[9:]
    weight_refs, refs = refs[:weights], refs[weights:]
    lifted_grad_ref, taps_grad_ref, hi_ref, next_ref, own_ref, weight, padded, padded_grad, plain, semaphores = refs
    row_count, channels = convolved_ref.shape
    taps = taps_ref.shape[0]
    row_block = row_count // pieces
    copies = Copies(semaphores)
    weight_copies_ = copies.weight(weight_refs, weight, slice(0, 2 * channels))
    firsts = block_firsts(place_ref, pieces, row_block)
    valid, matches = conv_matches(lengths_ref, row_count, taps)
    count, average, inverse = batch_scales(sums_ref)
    gain = affine_ref[0:1, :]
    hatted = (convolved_ref[...] - average) * inverse
    conv_grad = inverse * (
        normal_ref[...] * gain
        - valid * gain * (back_ref[0:1, :] + hatted * back_ref[1:2, :]) / count
    )
    value = lifted_ref[:, :channels]
    gate = jax.nn.sigmoid(lifted_ref[:, channels:])
    for scratch in (padded, padded_grad):
        scratch[:MARGIN, :] = jnp.zeros((MARGIN, channels), FLOAT)
        scratch[MARGIN + row_count :, :] = jnp.zeros((MARGIN, channels), FLOAT)
    padded[MARGIN : MARGIN + row_count, :] = value * gate * valid
    padded_grad[MARGIN : MARGIN + row_count, :] = conv_grad
    taps_grad_ref[...] = jnp.zeros_like(taps_grad_ref)
    gated_grad = jnp.zeros((row_count, channels), FLOAT)
    for t in range(taps):
        offset = t - taps // 2
        read = padded[MARGIN + offset : MARGIN + offset + row_count, :]
        taps_grad_ref[t : t + 1, :] = jnp.sum(
            matches[t] * read * conv_grad, axis=0, keepdims=True
        )
        back = padded_grad[MARGIN - offset : MARGIN - offset + row_count, :]
        gated_grad += taps_ref[t : t + 1, :] * matches[taps - 1 - t] * back
    gated_grad = gated_grad * valid
    plain[:, :channels] = (gated_grad * gate).astype(LOW)
    plain[:, channels:] = (gated_grad * value * gate * (1.0 - gate)).astype(LOW)
    for q in range(pieces):
        lifted_grad_ref[q * row_block : (q + 1) * row_block, :] = plain[
            pl.ds(firsts[q], row_block), :
        ]
    save()

    wait(weight_copies_)

    @tiles(weight.shape[0])
    def _(features):
        write_parts(
            hi_ref, next_ref, own_ref, features,
            times_transposed(lifted_grad_ref[...], weight[features, :]),
        )


def conv_back(
    place, lengths, taps, affine, sums, back, convolved, normal, lifted, weights, pieces,
    features,
):
    row_count, channels = convolved.shape
    return call(
        functools.partial(conv_back_kernel, pieces=pieces, weights=len(weights)),
        [((row_count, 2 * channels), LOW), ((8, channels), FLOAT)] + row_parts(row_count, features),
        [
            pltpu.VMEM((features, 2 * channels), LOW),
            pltpu.VMEM((row_count + 2 * MARGIN, channels), FLOAT),
            pltpu.VMEM((row_count + 2 * MARGIN, channels), FLOAT),
            pltpu.VMEM((row_count, 2 * channels), LOW),
            pltpu.SemaphoreType.DMA((len(weights),)),
        ],
        4 * row_count * features * channels,
        ("smem", place), ("smem", lengths),
        *[
            ("vmem", array)
            for array in (taps, affine, sums, back, convolved, normal, lifted)
        ],
        *[("any" if len(weights) > 1 else "hbm", array) for array in weights],
        saved=(0,),
    )


def standardize(values):
    average = jnp.mean(values, axis=-1, keepdims=True)
    centred = values - average
    spread_of = jnp.mean(centred * centred, axis=-1, keepdims=True)
    scale = lax.rsqrt(spread_of + EPSILON)
    return centred * scale, scale


def norm_back(values, norm_gain, normed_grad):
    hat, scale = standardize(values)
    gained = normed_grad * norm_gain
    first = jnp.mean(gained, axis=-1, keepdims=True)
    second = jnp.mean(gained * hat, axis=-1, keepdims=True)
    grad = (gained - first - hat * second) * scale
    return grad, jnp.sum(normed_grad * hat, axis=0, keepdims=True)


def middle_kernel(next_ref, arrived_ref, sent_ref):
    first = next_ref.shape[0]
    sent_ref[...] = (
        next_ref[...].astype(FLOAT) + arrived_ref[first:, :].astype(FLOAT)
    ).astype(LOW)


def sum_rows(hi, next_part, own_part):
    arrived = swap(hi, "mp", 1)
    (sent,) = call(
        middle_kernel, [(next_part.shape, LOW)], [], next_part.size,
        ("vmem", next_part), ("vmem", arrived),
    )
    return (own_part, arrived, swap(sent, "mp", 2)), sent


def summed(own_ref, near_ref, far_ref):
    rows = own_ref.shape[0]
    return own_ref[...] + near_ref[:rows, :].astype(FLOAT) + far_ref[...].astype(FLOAT)


def all_rows(own):
    across = swap(own, "mp", 2)
    return [own, across, swap(own, "mp", 1), swap(across, "mp", 1)]


def step_kernel(
    own_ref, near_ref, far_ref, residual_ref, gain_ref, next_ref, normed_ref, *, factor
):
    residual = residual_ref[...].astype(FLOAT) + factor * summed(own_ref, near_ref, far_ref)
    next_ref[...] = residual
    normed_ref[...] = (standardize(residual)[0] * gain_ref[...]).astype(LOW)


def step(parts, residual, gain, factor):
    shape = parts[0].shape
    return call(
        functools.partial(step_kernel, factor=factor), [(shape, FLOAT), (shape, LOW)], [],
        8 * math.prod(shape),
        *[("vmem", array) for array in (*parts, residual, gain)],
    )


def turn_kernel(
    own_ref, near_ref, far_ref, residual_ref, gain_ref, out_grad_ref,
    result_ref, grad_ref, branch_ref, gain_grad_ref,
):
    residual = residual_ref[...] + 0.5 * summed(own_ref, near_ref, far_ref)
    gain = gain_ref[...]
    result_ref[...] = (standardize(residual)[0] * gain).astype(LOW)
    grad, gain_grad = norm_back(residual, gain, out_grad_ref[...].astype(FLOAT))
    grad_ref[...] = grad
    branch_ref[...] = (0.5 * grad).astype(LOW)
    gain_grad_ref[...] = gain_grad


def turn(parts, residual, gain, out_grad):
    shape = parts[0].shape
    return call(
        turn_kernel,
        [(shape, LOW), (shape, FLOAT), (shape, LOW), ((1, shape[1]), FLOAT)], [],
        16 * math.prod(shape),
        *[("vmem", array) for array in (*parts, residual, gain, out_grad)],
    )


def step_back_kernel(
    own_ref, near_ref, far_ref, residual_ref, gain_ref, grad_ref,
    next_ref, branch_ref, gain_grad_ref, *, factor,
):
    normed_grad = summed(own_ref, near_ref, far_ref)
    grad, gain_grad = norm_back(residual_ref[...].astype(FLOAT), gain_ref[...], normed_grad)
    grad = grad_ref[...] + grad
    next_ref[...] = grad
    branch_ref[...] = (factor * grad).astype(LOW)
    gain_grad_ref[...] = gain_grad


def step_back(parts, residual, gain, grad, factor):
    shape = parts[0].shape
    return call(
        functools.partial(step_back_kernel, factor=factor),
        [(shape, FLOAT), (shape, LOW), ((1, shape[1]), FLOAT)], [],
        16 * math.prod(shape),
        *[("vmem", array) for array in (*parts, residual, gain, grad)],
    )


def select_kernel(place_ref, *refs):
    pieces, target_ref = refs[:-1], refs[-1]
    row_block = pieces[0].shape[0]
    for piece, first in zip(pieces, block_firsts(place_ref, len(pieces), row_block)):
        target_ref[pl.ds(first, row_block), :] = piece[...].astype(target_ref.dtype)


def select_rows(place, pieces, kind):
    row_block, features = pieces[0].shape
    (outcome,) = call(
        select_kernel, [((len(pieces) * row_block, features), kind)], [], 0,
        ("smem", place), *[("vmem", piece) for piece in pieces], limit=16,
    )
    return outcome


def finish_kernel(*refs, counts):
    sources, targets = refs[: 2 * len(counts)], refs[2 * len(counts) :]
    at = 0
    for i, count in enumerate(counts):
        total = sources[2 * i][...] + sources[2 * i + 1][...].astype(FLOAT)
        first = 0
        for target in targets[at : at + count]:
            last = first + target.shape[1]
            target[...] = total[:, first:last]
            first = last
        at += count


def finish(sums, widths, *tokens):
    rows = sums[0].kept.shape[0]
    parts, counts, left = [], [], list(widths)
    for part in sums:
        parts += [("vmem", part.kept), ("vmem", after(part.sent, *tokens))]
        count, total = 0, 0
        while total < part.kept.shape[1]:
            total, count = total + left.pop(0), count + 1
        counts.append(count)
    return call(
        functools.partial(finish_kernel, counts=tuple(counts)),
        [((rows, width), FLOAT) for width in widths], [], 0, *parts,
    )


def join_kernel(*refs):
    target, first = refs[-1], 0
    for kept, arrived in zip(refs[0:-1:2], refs[1:-1:2]):
        last = first + kept.shape[1]
        target[:, first:last] = kept[...] + arrived[...].astype(FLOAT)
        first = last


def join(sums):
    rows, width = sums[0].kept.shape[0], sum(part.kept.shape[1] for part in sums)
    parts = []
    for part in sums:
        parts += [("vmem", part.kept), ("vmem", part.sent)]
    return call(join_kernel, [((rows, width), FLOAT)], [], 0, *parts)[0]


def per_device(
    inputs,
    lengths,
    out_grad,
    first_norm,
    first_up,
    first_down,
    attention_norm,
    query_weight,
    key_weight,
    value_weight,
    position_weight,
    output_weight,
    content_bias,
    position_bias,
    convolution_norm,
    pointwise_in,
    depthwise_kernel,
    batch_gain,
    batch_shift,
    pointwise_out,
    second_norm,
    second_up,
    second_down,
    final_norm,
):
    row_count, feature_count = inputs.shape
    dp_size, mp_size = lax.axis_size("dp"), lax.axis_size("mp")
    dp_at, mp_at = lax.axis_index("dp"), lax.axis_index("mp")
    block, hidden = first_up.shape
    row_block = row_count // mp_size
    bias_rows, head_count = content_bias.shape
    head_size = bias_rows * dp_size
    heads = head_count * head_size
    local_channels, tap_count = depthwise_kernel.shape
    channels = local_channels * dp_size
    place = mp_at.reshape(1).astype(jnp.int32)

    places = jnp.arange(feature_count, dtype=jnp.int32)
    owners = dp_at ^ reversed_bits(places // block, dp_size)
    source = owners * block + places % block
    selection = (places[:, None] == source[None, :]).astype(LOW)
    block_places = jnp.arange(dp_size, dtype=jnp.int32)
    block_owners = (dp_at ^ reversed_bits(block_places, dp_size)).astype(jnp.int32)
    block_selection = (block_places[:, None] == block_owners[None, :]).astype(LOW)

    up_own = first_up.astype(LOW)
    small_own = jnp.concatenate(
        [
            part.reshape(-1)
            for part in (
                first_norm, attention_norm, convolution_norm, second_norm, final_norm,
                content_bias, position_bias, depthwise_kernel, batch_gain, batch_shift,
            )
        ]
    )
    small_own = after(small_own, up_own).astype(LOW)
    links = Links(4)
    up_spread = Spread(links, up_own)
    up_spread.go(ORDER)
    ups = up_spread.blocks
    down_own = after(first_down, ups[1]).astype(LOW)
    down_spread = Spread(links, down_own)
    down_spread.go(ORDER)
    downs = down_spread.blocks
    gates, mask = [downs[1], ups[5], ups[3]], dp_size // 2
    small_all = small_own[None]
    while mask:
        arrived = swap(small_all, "dp", mask)
        if gates:
            arrived = after(arrived, gates.pop())
        small_all = jnp.concatenate([small_all, arrived], axis=0)
        mask //= 2

    attention_own = jnp.concatenate(
        after(
            (query_weight, key_weight, value_weight, position_weight, output_weight), ups[3]
        ),
        axis=1,
    ).astype(LOW)
    attention_spread = Spread(links, attention_own)
    attention_spread.go(ORDER[:3], time=10)
    pointwise_in, pointwise_out, second_up, second_down = after(
        (pointwise_in, pointwise_out, second_up, second_down), ups[2]
    )
    convolution_own = jnp.concatenate(
        [pointwise_in.reshape(block, 2 * channels), pointwise_out], axis=1
    ).astype(LOW)
    second_own = jnp.concatenate([second_up, second_down], axis=1).astype(LOW)

    whole, first_half, second_half = (
        slice(0, hidden), slice(0, hidden), slice(hidden, 2 * hidden)
    )

    norms = small_all[:, : 5 * block].astype(FLOAT).reshape(dp_size, 5, block)
    norms = norms.transpose(1, 0, 2).reshape(5, 1, feature_count)
    first_gain, attention_gain, convolution_gain, second_gain, final_gain = norms
    plain_small = matmul(block_selection, small_all[:, 5 * block :])
    cut = bias_rows * head_count
    content_all = plain_small[:, :cut].reshape(head_size, head_count).T
    position_all = plain_small[:, cut : 2 * cut].reshape(head_size, head_count).T
    at = 2 * cut + local_channels * tap_count
    taps = plain_small[:, 2 * cut : at].reshape(channels, tap_count).T
    affine = jnp.stack(
        [
            plain_small[:, at : at + local_channels].reshape(channels),
            plain_small[:, at + local_channels :].reshape(channels),
        ]
    )

    arranged = matmul(
        jnp.concatenate(
            [
                lax.dynamic_slice_in_dim(
                    inputs, (mp_at ^ fixed_reversed(q, mp_size)) * row_block, row_block, axis=0
                )
                for q in range(mp_size)
            ],
            axis=0,
        ),
        selection,
    )
    own_out_grad = matmul(
        lax.dynamic_slice_in_dim(out_grad, mp_at * row_block, row_block, axis=0), selection
    ).astype(LOW)
    table_places = after(jnp.arange(2 * row_count, dtype=jnp.int32), ups[3])
    sin_table = position_table(table_places, row_count, feature_count)
    sin_table = matmul(sin_table, selection).astype(LOW)

    residual_zero = arranged[:row_block].astype(LOW)
    hat_a = standardize(arranged)[0]
    normed_a = (hat_a * first_gain).astype(LOW)
    hat_a = hat_a.astype(LOW)
    _, before_a, active_a, up_a, down_a, hi, next_part, own_part = ffn_call(
        ffn_forward_kernel, [normed_a], ups, downs, whole, whole
    )
    attention_spread.go((3, 5), hi, time=10)
    parts, sent = sum_rows(hi, next_part, own_part)
    attention_spread.go((6,), sent, time=10)
    attention_spread.go((7,), parts[2], time=10)
    attention_all = attention_spread.blocks
    convolution_spread = Spread(links, after(convolution_own, sent))
    convolution_spread.go(ORDER[:3], time=10)
    residual_one, own_b = step(parts, residual_zero, attention_gain, 0.5)
    second_spread = Spread(links, after(second_own, sent))

    (
        normed_b, mixed_rows, prob, content_rows, position_rows, keys, values, position,
        attention_weight, hi, next_part, own_part,
    ) = attention_forward(
        place, lengths, all_rows(own_b), attention_all, sin_table, content_all,
        position_all,
    )
    parts, sent = sum_rows(hi, next_part, own_part)
    convolution_spread.go((3, 5, 6), sent, time=10)
    convolution_spread.go((7,), parts[2], time=10)
    convolution_all = convolution_spread.blocks
    second_spread.go(ORDER[:3], time=10)
    residual_two, own_c = step(parts, residual_one, convolution_gain, 1.0)
    rows = all_rows(own_c)

    normed_c, lifted, convolution_weight, convolved, sums = conv_lift(
        place, lengths, taps, rows, convolution_all
    )
    second_spread.go(ORDER[3:5], sums, time=10)
    sums, _ = total_hops(sums, "dp")
    second_spread.go(ORDER[5:], sums, time=10)
    swished, hi, next_part, own_part = conv_out(
        place, lengths, affine, sums, convolved, [convolution_weight], mp_size,
        feature_count,
    )
    parts, sent = sum_rows(hi, next_part, own_part)
    residual_three, own_d = step(parts, residual_two, second_gain, 1.0)
    second_all = second_spread.blocks

    normed_d, before_d, active_d, up_d, down_d, hi, next_part, own_part = ffn_call(
        ffn_forward_kernel, all_rows(own_d), second_all, second_all, first_half,
        second_half,
    )
    parts, sent = sum_rows(hi, next_part, own_part)
    own_result, residual_grad, branch, final_gain_grad = turn(
        parts, residual_three, final_gain, own_out_grad
    )

    branch_rows, before_grad, hi, next_part, own_part = ffn_call(
        ffn_backward_kernel, all_rows(branch), [up_d], [down_d], whole, whole, before_d,
    )
    links = Links(3, apart=True)
    parts, sent = sum_rows(hi, next_part, own_part)
    second_down_sum = WeightSum((after(branch_rows, sent), active_d))
    second_down_sum.advance(links=links)
    residual_grad, branch, second_gain_grad = step_back(
        parts, residual_three, second_gain, residual_grad, 1.0
    )
    second_up_sum = WeightSum((after(normed_d, branch), before_grad))

    branch_rows, normal, back_sums = conv_back_sums(
        place, lengths, affine, sums, convolved, all_rows(branch), [convolution_weight]
    )
    back_sums, hops = total_hops(back_sums, "dp")
    second_down_sum.advance(hops[-2], links=links)
    second_up_sum.advance(hops[-1], links=links)
    lifted_grad, taps_grad, hi, next_part, own_part = conv_back(
        place, lengths, taps, affine, sums, back_sums, convolved, normal, lifted,
        [convolution_weight], mp_size, feature_count,
    )
    parts, sent = sum_rows(hi, next_part, own_part)
    convolution_sum = WeightSum(
        (normed_c, after(lifted_grad, sent)), (branch_rows, after(swished, sent))
    )
    convolution_sum.advance(links=links)
    second_down_sum.advance(sent, links=links)
    residual_grad, branch, convolution_gain_grad = step_back(
        parts, residual_two, convolution_gain, residual_grad, 1.0
    )
    first_row = dp_at * local_channels
    gain_piece = lax.dynamic_slice_in_dim(back_sums[1], first_row, local_channels)
    shift_piece = lax.dynamic_slice_in_dim(back_sums[0], first_row, local_channels)

    branch_rows, qkv_grad, position_grad, bias_grads, hi, next_part, own_part = attention_backward(
        place, all_rows(branch), [attention_weight],
        (position, prob, content_rows, position_rows, keys, values), head_count,
    )
    parts, sent = sum_rows(hi, next_part, own_part)
    convolution_sum.advance(sent, links=links)
    residual_grad, branch, attention_gain_grad = step_back(
        parts, residual_one, attention_gain, residual_grad, 0.5
    )
    attention_sum = WeightSum(
        (normed_b, after(qkv_grad, sent)), (sin_table, after(position_grad, sent)),
        (branch_rows, after(mixed_rows, sent)),
    )
    attention_sum.advance(links=links, later=(branch,))
    second_up_sum.advance(branch, links=links)

    branch_rows, before_grad, hi, next_part, own_part, first_gain_grad = ffn_call(
        ffn_backward_kernel, all_rows(branch), [up_a], [down_a], whole, whole, before_a,
        hat_a,
    )
    first_down_sum = WeightSum((branch_rows, active_a))
    first_up_sum = WeightSum((normed_a, before_grad))

    bias_grads, taps_grad = after((bias_grads, taps_grad), branch)
    plain_grads = jnp.concatenate(
        [
            bias_grads[:head_count].T.reshape(dp_size, cut),
            bias_grads[head_count:].T.reshape(dp_size, cut),
            taps_grad[:tap_count].T.reshape(dp_size, local_channels * tap_count),
        ],
        axis=1,
    )
    plain_grads = lax.dot_general(
        block_selection.astype(FLOAT), plain_grads, (((0,), (0,)), ((), ())),
        precision=lax.Precision.HIGHEST, preferred_element_type=FLOAT,
    )
    parts, sent = sum_rows(hi, next_part, own_part)
    first_gain_grad = after(first_gain_grad, sent)
    gain_grads = jnp.concatenate(
        [
            first_gain_grad, attention_gain_grad, convolution_gain_grad, second_gain_grad,
            final_gain_grad,
        ],
        axis=0,
    )
    gain_grads = gain_grads.reshape(5, dp_size, block).transpose(1, 0, 2)
    small_grads = jnp.concatenate([gain_grads.reshape(dp_size, 5 * block), plain_grads], axis=1)

    first_down_sum.advance(later=(sent,))
    convolution_sum.advance(first_down_sum.upper)
    attention_sum.advance()
    first_up_sum.advance(attention_sum.sent, later=(sent,))
    second_up_sum.advance(first_down_sum.upper)
    residual_grad, _, _ = step_back(parts, residual_zero, first_gain, residual_grad, 1.0)
    inputs_rows = all_rows(
        times_transposed(residual_grad.astype(LOW), selection).astype(LOW)
    )
    result_rows = all_rows(
        times_transposed(after(own_result, parts[2]), selection).astype(LOW)
    )
    mask, small_grads, down_hop = 1, after(small_grads, first_down_sum.upper), first_down_sum.sent
    while mask < dp_size:
        kept = small_grads.shape[0] // 2
        small_token = after(swap(small_grads[kept:], "dp", mask), down_hop)
        small_grads = small_grads[:kept] + small_token
        mask *= 2
    first_down_sum.advance()
    attention_sum.advance(first_down_sum.upper)
    down_hop = first_down_sum.sent
    first_down_sum.advance(attention_sum.upper)
    first_up_sum.advance(down_hop, inputs_rows[3], result_rows[3], small_token)
    first_up_sum.advance(attention_sum.sent, first_down_sum.sent)
    for part in (
        second_down_sum, second_up_sum, convolution_sum, attention_sum, first_down_sum,
        first_up_sum,
    ):
        part.rest()

    second_down_grad, second_up_grad, convolution_in_grad, convolution_out_grad = finish(
        [second_down_sum, second_up_sum, convolution_sum],
        [hidden, hidden, 2 * channels, channels], parts[2],
    )
    attention_grads = finish([attention_sum], [heads] * 5)
    first_down_grad, first_up_grad = join([first_down_sum]), join([first_up_sum])

    result = select_rows(place, result_rows, LOW)
    inputs_grad = select_rows(place, inputs_rows, FLOAT)

    small_grads = small_grads[0]
    gain_grads = total_over(small_grads[: 5 * block].reshape(5, block), "mp")
    plain_grads = small_grads[5 * block :]

    return (
        result,
        inputs_grad,
        gain_grads[0],
        first_up_grad,
        first_down_grad,
        gain_grads[1],
        *attention_grads,
        plain_grads[:cut].reshape(bias_rows, head_count),
        plain_grads[cut : 2 * cut].reshape(bias_rows, head_count),
        gain_grads[2],
        convolution_in_grad.reshape(block, 2, channels),
        plain_grads[2 * cut :].reshape(local_channels, tap_count),
        gain_piece,
        shift_piece,
        convolution_out_grad,
        gain_grads[3],
        second_up_grad,
        second_down_grad,
        gain_grads[4],
    )


def solution(mesh):
    return jax.shard_map(
        per_device,
        mesh=mesh,
        in_specs=(
            P("dp", None),
            P("dp", None),
            P("dp", None),
            P("dp"),
            P("dp", "mp"),
            P("dp", "mp"),
            P("dp"),
            P("dp", "mp"),
            P("dp", "mp"),
            P("dp", "mp"),
            P("dp", "mp"),
            P("dp", "mp"),
            P("dp", "mp"),
            P("dp", "mp"),
            P("dp"),
            P("dp", None, "mp"),
            P(("mp", "dp"), None),
            P(("mp", "dp")),
            P(("mp", "dp")),
            P("dp", "mp"),
            P("dp"),
            P("dp", "mp"),
            P("dp", "mp"),
            P("dp"),
        ),
        out_specs=(
            P("dp", None),
            P("dp", None),
            P("dp"),
            P("dp", "mp"),
            P("dp", "mp"),
            P("dp"),
            P("dp", "mp"),
            P("dp", "mp"),
            P("dp", "mp"),
            P("dp", "mp"),
            P("dp", "mp"),
            P("dp", "mp"),
            P("dp", "mp"),
            P("dp"),
            P("dp", None, "mp"),
            P(("mp", "dp"), None),
            P(("mp", "dp")),
            P(("mp", "dp")),
            P("dp", "mp"),
            P("dp"),
            P("dp", "mp"),
            P("dp", "mp"),
            P("dp"),
        ),
        check_vma=False,
    )
```

```python
import functools
import math

import jax
import jax.numpy as jnp
from jax import lax
from jax.experimental import pallas as pl
from jax.experimental.pallas import tpu as pltpu
from jax.sharding import PartitionSpec as P

EPSILON = 1e-05
LOW = jnp.bfloat16
FLOAT = jnp.float32


def matmul(left_side, right_side):
    return jnp.dot(left_side, right_side, preferred_element_type=FLOAT)


def times_transposed(left_side, right_side):
    return lax.dot_general(
        left_side, right_side, (((1,), (1,)), ((), ())), preferred_element_type=FLOAT
    )


def outer_sum(left_side, right_side):
    return lax.dot_general(
        left_side, right_side, (((0,), (0,)), ((), ())), preferred_element_type=FLOAT
    )


def reversed_bits(places, size):
    outcome = places * 0
    mask, back = size // 2, 1
    while mask:
        outcome = outcome + ((places // back) % 2) * mask
        mask, back = mask // 2, back * 2
    return outcome


def swap(values, axis, mask):
    size = lax.axis_size(axis)
    return lax.ppermute(values, axis, [(i, i ^ mask) for i in range(size)])


def after(values, *tokens):
    return lax.optimization_barrier((values, tokens))[0] if tokens else values


class Links:
    def __init__(self, depth, apart=False):
        self.depth, self.apart, self.queues = depth, apart, {}

    def swap(self, values, mask, time=None):
        queue, depth = self.queues.setdefault(self.apart and mask == 1, []), self.depth
        if len(queue) >= depth:
            values = after(values, *queue[-2 * depth : len(queue) + 1 - depth])
        arrived = swap(values, "dp", mask)
        queue.append(arrived if time is None else held(arrived, time))
        return queue[-1]


ORDER = (4, 1, 2, 3, 5, 6, 7)


def pass_kernel(source_ref, target_ref):
    pass


def held(values, microseconds):
    return pl.pallas_call(
        pass_kernel,
        out_shape=jax.ShapeDtypeStruct(values.shape, values.dtype),
        in_specs=[pl.BlockSpec(memory_space=pl.ANY)],
        out_specs=pl.BlockSpec(memory_space=pl.ANY),
        input_output_aliases={0: 0},
        cost_estimate=pl.CostEstimate(
            flops=int(1.1e9 * microseconds), bytes_accessed=0, transcendentals=0
        ),
    )(values)


class Spread:
    def __init__(self, links, own):
        self.links, self.mask = links, lax.axis_size("dp") // 2
        while self.mask > 4:
            own = jnp.concatenate([own, links.swap(own, self.mask)], axis=0)
            self.mask //= 2
        self.blocks = [own] + [None] * (2 * self.mask - 1)

    def go(self, places, *tokens, time=None):
        for p in places:
            if p < len(self.blocks):
                top = 1 << (p.bit_length() - 1)
                self.blocks[p] = self.links.swap(
                    after(self.blocks[p - top], *tokens), self.mask // top,
                    time if p < 4 or time is None else 10,
                )


def spread(values, axis):
    mask = lax.axis_size(axis) // 2
    while mask:
        values = jnp.concatenate([values, swap(values, axis, mask)], axis=0)
        mask //= 2
    return values


def collect(values, axis, wire, mask=1):
    while mask < lax.axis_size(axis):
        half = values.shape[0] // 2
        values = values[:half] + swap(values[half:].astype(wire), axis, mask).astype(FLOAT)
        mask *= 2
    return values


def total_over(values, axis):
    mask = 1
    while mask < lax.axis_size(axis):
        values = values + swap(values, axis, mask)
        mask *= 2
    return values


def total_hops(values, axis):
    arrivals, mask = [], lax.axis_size(axis) // 2
    while mask:
        arrivals.append(swap(values, axis, mask))
        values = values + arrivals[-1]
        mask //= 2
    return values, arrivals


class WeightSum:
    def __init__(self, *pairs):
        self.pairs, self.mask = pairs, 0

    def advance(self, *tokens, links=None, later=()):
        if not self.mask:
            half = self.pairs[0][0].shape[1] // 2
            upper = [outer_sum(left[:, half:], right).astype(LOW) for left, right in self.pairs]
            self.later = later
            self.upper, self.mask = after(jnp.concatenate(upper, axis=1), *tokens), 1
        else:
            if self.mask == 1 << 1:
                lower = [
                    outer_sum(after(left, *self.later)[:, : left.shape[1] // 2], right)
                    for left, right in self.pairs
                ]
                self.kept = jnp.concatenate(lower, axis=1)
            total = self.kept + after(self.sent, *tokens).astype(FLOAT)
            half = total.shape[0] // 2
            self.upper, self.kept = total[half:].astype(LOW), total[:half]
        if links is None:
            self.sent = swap(self.upper, "dp", self.mask)
        else:
            self.sent = links.swap(self.upper, self.mask)
        self.mask *= 2

    def rest(self, *tokens):
        while self.mask < lax.axis_size("dp"):
            self.advance(*tokens)


def position_table(places, row_count, feature_count):
    rates = jnp.exp(
        jnp.arange(0, feature_count, 2).astype(FLOAT) * (-math.log(10000.0) / feature_count)
    )
    stride = 32
    count = places.shape[0] // stride
    coarse = (row_count - 1 - stride * places[:count]).astype(FLOAT)[:, None] * rates[None, :]
    fine = -places[:stride].astype(FLOAT)[:, None] * rates[None, :]
    coarse_sin, coarse_cos = jnp.sin(coarse)[:, None], jnp.cos(coarse)[:, None]
    fine_sin, fine_cos = jnp.sin(fine)[None], jnp.cos(fine)[None]
    sines = coarse_sin * fine_cos + coarse_cos * fine_sin
    cosines = coarse_cos * fine_cos - coarse_sin * fine_sin
    table = jnp.concatenate([sines, cosines], axis=2).astype(LOW)
    return table.reshape(places.shape[0], feature_count)


def fixed_reversed(place, size):
    outcome, mask = 0, size // 2
    while mask:
        outcome, place, mask = outcome + (place % 2) * mask, place // 2, mask // 2
    return outcome


def relative_window(position_ref, first, row_block, columns):
    row_count = position_ref.shape[0] // 2
    start = pl.multiple_of(row_count - row_block - first, row_block)
    return position_ref.at[pl.ds(start, row_count + row_block), columns]


def in_smem():
    return pl.BlockSpec(memory_space=pltpu.SMEM)


def in_vmem():
    return pl.BlockSpec(memory_space=pltpu.VMEM)


def in_hbm():
    return pl.BlockSpec(memory_space=pltpu.HBM)


def anywhere():
    return pl.BlockSpec(memory_space=pl.ANY)


def call(kernel, outs, scratch, flops, *operands, limit=6, room=50, saved=()):
    places = dict(smem=in_smem, vmem=in_vmem, any=anywhere, hbm=in_hbm)
    count, inner = len(operands), len(scratch)

    def saving(*refs):
        sources, targets, rest = (
            refs[:count], list(refs[count : count + len(outs)]), refs[count + len(outs) :]
        )
        kept, held_refs, semaphores = rest[:inner], rest[inner:-1], rest[-1]
        copies = [
            pltpu.make_async_copy(ref, targets[i], semaphores.at[n])
            for n, (i, ref) in enumerate(zip(saved, held_refs))
        ]
        for i, ref in zip(saved, held_refs):
            targets[i] = ref

        def save():
            for copy in copies:
                copy.start()

        kernel(*sources, *targets, *kept, save=save)
        for copy in copies:
            copy.wait()

    extra = []
    if saved:
        extra = [pltpu.VMEM(*outs[i]) for i in saved] + [pltpu.SemaphoreType.DMA((len(saved),))]
    return pl.pallas_call(
        saving if saved else kernel,
        out_shape=tuple(jax.ShapeDtypeStruct(shape, kind) for shape, kind in outs),
        in_specs=[places[place]() for place, _ in operands],
        out_specs=tuple(in_hbm() if i in saved else in_vmem() for i in range(len(outs))),
        scratch_shapes=list(scratch) + extra,
        compiler_params=pltpu.CompilerParams(
            vmem_limit_bytes=(room if scratch else limit) * 2**20
        ),
        cost_estimate=pl.CostEstimate(flops=flops, bytes_accessed=0, transcendentals=0),
    )(*[array for _, array in operands])


class Copies:
    def __init__(self, semaphores):
        self.semaphores, self.count = semaphores, 0

    def start(self, source, target):
        copy = pltpu.make_async_copy(source, target, self.semaphores.at[self.count])
        copy.start()
        self.count += 1
        return copy

    def stack(self, sources, target, columns=None):
        copies, block = [], target.shape[0] // len(sources)
        for p, source in enumerate(sources):
            if columns is not None:
                source = source.at[:, columns]
            copies.append(self.start(source, target.at[pl.ds(p * block, block)]))
        return copies

    def weight(self, sources, target, columns):
        if len(sources) > 1:
            return self.stack(sources, target, columns)
        return [self.start(sources[0].at[:, columns], target)]


def wait(copies):
    for copy in copies:
        copy.wait()


TILE = 256


def write_parts(hi_ref, next_ref, own_ref, columns, product):
    half, own = hi_ref.shape[0], own_ref.shape[0]
    hi_ref[:, columns] = product[half:].astype(LOW)
    next_ref[:, columns] = product[own:half].astype(LOW)
    own_ref[:, columns] = product[:own]


def tiles(count):
    def loop(body):
        @pl.loop(0, count // TILE)
        def _(t):
            body(pl.ds(pl.multiple_of(t * TILE, TILE), TILE))

    return loop


def ffn_forward_kernel(*refs, pieces, weights, up_columns, down_columns, save):
    row_refs, refs = refs[:pieces], refs[pieces:]
    up_refs, refs = refs[:weights], refs[weights:]
    down_refs, refs = refs[:weights], refs[weights:]
    rows_ref, before_ref, active_ref, up, down, hi_ref, next_ref, own_ref, semaphores = refs
    copies = Copies(semaphores)
    rows_copies = copies.stack(row_refs, rows_ref)
    up_copies = copies.weight(up_refs, up, up_columns)
    down_copies = copies.weight(down_refs, down, down_columns)
    wait(rows_copies + up_copies)

    @tiles(up.shape[1])
    def _(columns):
        before = matmul(rows_ref[...], up[:, columns])
        before_ref[:, columns] = before.astype(LOW)
        active_ref[:, columns] = (before * jax.nn.sigmoid(before)).astype(LOW)

    wait(down_copies)
    save()

    @tiles(down.shape[0])
    def _(features):
        write_parts(
            hi_ref, next_ref, own_ref, features, times_transposed(active_ref[...], down[features, :])
        )


def ffn_backward_kernel(*refs, pieces, weights, up_columns, down_columns, gains, save):
    if gains:
        (hat_ref, *others), gain_grad_ref, refs = (
            refs[-9 - gains : -9], refs[-4], refs[: -9 - gains] + refs[-9:-4] + refs[-3:]
        )
        gain_grad_ref[...] = jnp.zeros_like(gain_grad_ref)
        for n, other in enumerate(others):
            gain_grad_ref[n + 1 : n + 2, :] = other[...]
    row_refs, refs = refs[:pieces], refs[pieces:]
    up_refs, refs = refs[:weights], refs[weights:]
    down_refs, refs = refs[:weights], refs[weights:]
    before_ref, rows_ref, grad_ref, hi_ref, next_ref, own_ref, up, down, semaphores = refs
    copies = Copies(semaphores)
    rows_copies = copies.stack(row_refs, rows_ref)
    down_copies = copies.weight(down_refs, down, down_columns)
    up_copies = copies.weight(up_refs, up, up_columns)
    wait(rows_copies + down_copies)

    @tiles(down.shape[1])
    def _(columns):
        before = before_ref[:, columns].astype(FLOAT)
        squashed = jax.nn.sigmoid(before)
        grad = matmul(rows_ref[...], down[:, columns])
        grad_ref[:, columns] = (grad * squashed * (1.0 + before * (1.0 - squashed))).astype(LOW)

    save()

    wait(up_copies)

    @tiles(up.shape[0])
    def _(features):
        product = times_transposed(grad_ref[...], up[features, :])
        write_parts(hi_ref, next_ref, own_ref, features, product)
        if gains:
            gain_grad_ref[0:1, features] = jnp.sum(
                product * hat_ref[:, features].astype(FLOAT), axis=0, keepdims=True
            )


def row_parts(rows, features):
    return [
        ((rows // 2, features), LOW), ((rows // 4, features), LOW), ((rows // 4, features), FLOAT)
    ]


def ffn_call(
    kernel, rows, ups, downs, up_columns, down_columns, before=None, hats=(), room=50
):
    row_count = len(rows) * rows[0].shape[0]
    features = rows[0].shape[1]
    hidden = up_columns.stop - up_columns.start
    outs = [((row_count, features), LOW)]
    outs += [((row_count, hidden), LOW)] * (2 if before is None else 1)
    weight = ((features, hidden), LOW)
    if before is None:
        outs += [weight] * 2
    count = len(rows) + 2 * len(ups)
    operands = [("any", array) for array in rows]
    operands += [("any" if len(ups) > 1 else "hbm", array) for array in list(ups) + list(downs)]
    if before is not None:
        operands.append(("vmem", before))
        kernel = functools.partial(kernel, gains=len(hats))
    outs += row_parts(row_count, features)
    if hats:
        operands += [("vmem", array) for array in hats]
        outs.append(((8, features), FLOAT))
    return call(
        functools.partial(
            kernel, pieces=len(rows), weights=len(ups), up_columns=up_columns,
            down_columns=down_columns,
        ),
        outs,
        [pltpu.VMEM(*weight)] * (0 if before is None else 2)
        + [pltpu.SemaphoreType.DMA((count,))],
        4 * row_count * features * hidden,
        *operands,
        saved=(0, 1, 2, 3, 4) if before is None else (0, 1), room=room,
    )


def segment_of(lengths_ref, places):
    bound, segment = 0, jnp.zeros(places.shape, jnp.int32)
    for s in range(lengths_ref.shape[1]):
        bound = bound + lengths_ref[0, s]
        segment = segment + (places >= bound).astype(jnp.int32)
    return segment


def block_firsts(place_ref, blocks, row_block):
    place = place_ref[0]
    return [
        pl.multiple_of((place ^ fixed_reversed(q, blocks)) * row_block, row_block)
        for q in range(blocks)
    ]


def attention_forward_kernel(*refs, pieces, weights, save):
    place_ref, lengths_ref, content_ref, shift_ref = refs[:4]
    refs = refs[4:]
    row_refs, refs = refs[:pieces], refs[pieces:]
    weight_refs, refs = refs[:weights], refs[weights:]
    (
        table_ref,
        rows_ref, mixed_ref, prob_ref, content_rows_ref, position_rows_ref, key_ref, value_ref,
        position_ref, weight, hi_ref, next_ref, own_ref,
        table, qkv, semaphores,
    ) = refs
    row_count, heads = mixed_ref.shape
    head_count, head_size = content_ref.shape
    row_block = row_count // pieces
    window = row_count + row_block
    copies = Copies(semaphores)
    rows_copies = copies.stack(row_refs, rows_ref)
    everything = slice(0, weight.shape[1])
    weight_copies_ = copies.weight(weight_refs, weight, everything)
    table_copy = copies.start(table_ref, table)
    firsts = block_firsts(place_ref, pieces, row_block)
    wait(rows_copies + weight_copies_)

    @tiles(3 * heads)
    def _(columns):
        qkv[:, columns] = matmul(rows_ref[...], weight[:, columns])

    table_copy.wait()

    @tiles(table.shape[0])
    def _(places):
        position_ref[places, :] = matmul(
            table[places, :], weight[:, 3 * heads : 4 * heads]
        ).astype(LOW)

    for q in range(pieces):
        rows = pl.ds(q * row_block, row_block)
        key_ref[pl.ds(firsts[q], row_block), :] = qkv[rows, heads : 2 * heads].astype(LOW)
        value_ref[pl.ds(firsts[q], row_block), :] = qkv[rows, 2 * heads :].astype(LOW)

    along = lax.broadcasted_iota(jnp.int32, (1, row_count), 1)
    column_segment = segment_of(lengths_ref, along)
    for q in range(pieces):
        rows = pl.ds(q * row_block, row_block)
        down = lax.broadcasted_iota(jnp.int32, (row_block, 1), 0) + firsts[q]
        matching = segment_of(lengths_ref, down) == column_segment
        for h in range(head_count):
            columns = slice(h * head_size, (h + 1) * head_size)
            query = qkv[rows, columns]
            with_content = (query + content_ref[h : h + 1, :]).astype(LOW)
            with_position = (query + shift_ref[h : h + 1, :]).astype(LOW)
            content_rows_ref[rows, columns] = with_content
            position_rows_ref[rows, columns] = with_position
            direct = times_transposed(with_content, key_ref[:, columns])
            relative = relative_window(position_ref, firsts[q], row_block, columns)[...]
            broad = times_transposed(with_position, relative)
            broad = pltpu.roll(
                broad, window - (row_block - 1), axis=1, stride=1, stride_axis=0
            )
            scores = (direct + broad[:, :row_count]) * head_size ** (-0.5)
            scores = jnp.where(matching, scores, -1e30)
            exponent = jnp.exp(scores - jnp.max(scores, axis=1, keepdims=True))
            prob = (exponent / jnp.sum(exponent, axis=1, keepdims=True)).astype(LOW)
            prob_ref[h, rows, :] = prob
            mixed_ref[rows, columns] = matmul(prob, value_ref[:, columns]).astype(LOW)

    save()

    @tiles(weight.shape[0])
    def _(features):
        write_parts(
            hi_ref, next_ref, own_ref, features,
            times_transposed(mixed_ref[...], weight[features, 4 * heads : 5 * heads]),
        )


def attention_forward(place, lengths, rows, weights, table, content_bias, position_bias):
    row_count, features = len(rows) * rows[0].shape[0], rows[0].shape[1]
    head_count, head_size = content_bias.shape
    heads = head_count * head_size
    row_array = ((row_count, heads), LOW)
    return call(
        functools.partial(attention_forward_kernel, pieces=len(rows), weights=len(weights)),
        [
            ((row_count, features), LOW), row_array,
            ((head_count, row_count, row_count), LOW),
            row_array, row_array, row_array, row_array,
            ((2 * row_count, heads), LOW), ((features, 5 * heads), LOW),
        ]
        + row_parts(row_count, features),
        [
            pltpu.VMEM(table.shape, LOW),
            pltpu.VMEM((row_count, 3 * heads), FLOAT),
            pltpu.SemaphoreType.DMA((len(rows) + len(weights) + 1,)),
        ],
        12 * row_count * features * heads + 9 * heads * row_count**2,
        ("smem", place), ("smem", lengths),
        ("vmem", content_bias), ("vmem", position_bias),
        *[("any", array) for array in list(rows) + list(weights)],
        ("hbm", table),
        saved=tuple(range(9)), room=54,
    )


def attention_backward_kernel(*refs, pieces, weights, head_count, save):
    place_ref, refs = refs[0], refs[1:]
    row_refs, refs = refs[:pieces], refs[pieces:]
    weight_refs, refs = refs[:weights], refs[weights:]
    (
        position_ref, prob_ref, content_rows_ref, position_rows_ref, key_ref, value_ref,
        rows_ref, qkv_grad_ref, position_grad_ref, bias_grad_ref, hi_ref, next_ref, own_ref,
        weight, mixed_grad_ref, key_sum, value_sum, position_sum, semaphores,
    ) = refs
    row_count, heads = mixed_grad_ref.shape
    head_size = heads // head_count
    row_block = row_count // pieces
    scale = head_size ** (-0.5)
    copies = Copies(semaphores)
    rows_copies = copies.stack(row_refs, rows_ref)
    everything = slice(0, weight.shape[1])
    weight_copies_ = copies.weight(weight_refs, weight, everything)
    firsts = block_firsts(place_ref, pieces, row_block)
    key_sum[...] = jnp.zeros_like(key_sum)
    value_sum[...] = jnp.zeros_like(value_sum)
    position_sum[...] = jnp.zeros_like(position_sum)
    turn = (
        lax.broadcasted_iota(jnp.int32, (row_block, row_block), 0)
        + lax.broadcasted_iota(jnp.int32, (row_block, row_block), 1)
        == row_block - 1
    ).astype(LOW)
    wait(rows_copies + weight_copies_)
    mixed_grad_ref[...] = matmul(rows_ref[...], weight[:, 4 * heads : 5 * heads]).astype(LOW)
    for h in range(head_count):
        columns = slice(h * head_size, (h + 1) * head_size)
        content_total = jnp.zeros((1, head_size), FLOAT)
        position_total = jnp.zeros((1, head_size), FLOAT)
        for q in range(pieces):
            rows = pl.ds(q * row_block, row_block)
            mixed_grad = mixed_grad_ref[rows, columns]
            prob = prob_ref[h, rows, :]
            prob_float = prob.astype(FLOAT)
            prob_grad = times_transposed(mixed_grad, value_ref[:, columns])
            inner = jnp.sum(prob_grad * prob_float, axis=1, keepdims=True)
            score_grad = (prob_float * (prob_grad - inner)).astype(LOW)
            value_sum[:, columns] += outer_sum(prob, mixed_grad)
            key_sum[:, columns] += outer_sum(score_grad, content_rows_ref[rows, columns])
            turned = matmul(turn, score_grad).astype(LOW)
            content_part = matmul(turned, key_ref[:, columns]) * scale
            broad = jnp.concatenate([turned, jnp.zeros((row_block, row_block), LOW)], axis=1)
            broad = pltpu.roll(broad, 0, axis=1, stride=1, stride_axis=0)
            relative = relative_window(position_ref, firsts[q], row_block, columns)[...]
            position_part = matmul(broad, relative) * scale
            turned_rows = matmul(turn, position_rows_ref[rows, columns]).astype(LOW)
            total_ref = relative_window(position_sum, firsts[q], row_block, columns)
            total_ref[...] += outer_sum(broad, turned_rows)
            query_grad = (content_part + position_part).astype(LOW)
            qkv_grad_ref[rows, columns] = matmul(turn, query_grad).astype(LOW)
            content_total += jnp.sum(content_part, axis=0, keepdims=True)
            position_total += jnp.sum(position_part, axis=0, keepdims=True)
        bias_grad_ref[h : h + 1, :] = content_total
        bias_grad_ref[head_count + h : head_count + h + 1, :] = position_total
    for q in range(pieces):
        rows, plain = pl.ds(q * row_block, row_block), pl.ds(firsts[q], row_block)
        qkv_grad_ref[rows, heads : 2 * heads] = (key_sum[plain, :] * scale).astype(LOW)
        qkv_grad_ref[rows, 2 * heads :] = value_sum[plain, :].astype(LOW)
    position_grad_ref[...] = (position_sum[...] * scale).astype(LOW)

    save()

    @tiles(weight.shape[0])
    def _(features):
        write_parts(
            hi_ref, next_ref, own_ref, features,
            times_transposed(qkv_grad_ref[...], weight[features, : 3 * heads]),
        )


def attention_backward(place, rows, weights, stored, head_count):
    row_count, features = len(rows) * rows[0].shape[0], rows[0].shape[1]
    position = stored[0]
    heads = position.shape[1]
    return call(
        functools.partial(
            attention_backward_kernel, pieces=len(rows), weights=len(weights),
            head_count=head_count,
        ),
        [
            ((row_count, features), LOW),
            ((row_count, 3 * heads), LOW),
            (position.shape, LOW),
            ((2 * head_count, heads // head_count), FLOAT),
        ]
        + row_parts(row_count, features),
        [
            pltpu.VMEM((features, 5 * heads), LOW),
            pltpu.VMEM((row_count, heads), LOW),
            pltpu.VMEM((row_count, heads), FLOAT),
            pltpu.VMEM((row_count, heads), FLOAT),
            pltpu.VMEM(position.shape, FLOAT),
            pltpu.SemaphoreType.DMA((len(rows) + len(weights),)),
        ],
        8 * row_count * features * heads + 16 * heads * row_count**2,
        ("smem", place),
        *[("any", array) for array in rows],
        *[("any" if len(weights) > 1 else "hbm", array) for array in weights],
        *[("vmem", array) for array in stored],
        saved=(0, 1, 2),
    )


MARGIN = 8


def conv_matches(lengths_ref, row_count, taps):
    places = lax.broadcasted_iota(jnp.int32, (row_count, 1), 0)
    segment = segment_of(lengths_ref, places)
    valid = (segment < lengths_ref.shape[1]).astype(FLOAT)
    matches = []
    for t in range(taps):
        other = segment_of(lengths_ref, places + (t - taps // 2))
        matches.append((other == segment).astype(FLOAT))
    return valid, matches


def conv_lift_kernel(*refs, pieces, weights, save):
    place_ref, lengths_ref, taps_ref = refs[:3]
    refs = refs[3:]
    row_refs, refs = refs[:pieces], refs[pieces:]
    weight_refs, refs = refs[:weights], refs[weights:]
    rows_ref, lifted_ref, weight, convolved_ref, sums_ref, padded, semaphores = refs
    row_count, channels = convolved_ref.shape
    taps = taps_ref.shape[0]
    row_block = row_count // pieces
    copies = Copies(semaphores)
    rows_copies = copies.stack(row_refs, rows_ref)
    weight_copies_ = copies.weight(weight_refs, weight, slice(0, 3 * channels))
    firsts = block_firsts(place_ref, pieces, row_block)
    valid, matches = conv_matches(lengths_ref, row_count, taps)
    padded[:MARGIN, :] = jnp.zeros((MARGIN, channels), FLOAT)
    padded[MARGIN + row_count :, :] = jnp.zeros((MARGIN, channels), FLOAT)
    wait(rows_copies + weight_copies_)
    lifted = matmul(rows_ref[...], weight[:, : 2 * channels])
    for q in range(pieces):
        lifted_ref[pl.ds(firsts[q], row_block), :] = lifted[q * row_block : (q + 1) * row_block]
    gated = lifted_ref[:, :channels] * jax.nn.sigmoid(lifted_ref[:, channels:]) * valid
    padded[MARGIN : MARGIN + row_count, :] = gated
    convolved = jnp.zeros((row_count, channels), FLOAT)
    for t in range(taps):
        first = MARGIN + t - taps // 2
        convolved += taps_ref[t : t + 1, :] * matches[t] * padded[first : first + row_count, :]
    convolved_ref[...] = convolved
    save()

    masked = convolved * valid
    sums_ref[...] = jnp.zeros_like(sums_ref)
    sums_ref[0:1, :] = jnp.sum(masked, axis=0, keepdims=True)
    sums_ref[1:2, :] = jnp.sum(masked * convolved, axis=0, keepdims=True)
    sums_ref[2:3, :] = jnp.zeros((1, channels), FLOAT) + jnp.sum(valid, axis=0, keepdims=True)


def conv_lift(place, lengths, taps, rows, weights):
    row_count, features = len(rows) * rows[0].shape[0], rows[0].shape[1]
    channels = taps.shape[1]
    return call(
        functools.partial(conv_lift_kernel, pieces=len(rows), weights=len(weights)),
        [
            ((row_count, features), LOW),
            ((row_count, 2 * channels), FLOAT),
            ((features, 3 * channels), LOW),
            ((row_count, channels), FLOAT),
            ((8, channels), FLOAT),
        ],
        [
            pltpu.VMEM((row_count + 2 * MARGIN, channels), FLOAT),
            pltpu.SemaphoreType.DMA((len(rows) + len(weights),)),
        ],
        4 * row_count * features * channels,
        ("smem", place), ("smem", lengths), ("vmem", taps),
        *[("any", array) for array in rows],
        *[("any" if len(weights) > 1 else "hbm", array) for array in weights],
        saved=(0, 1, 2), room=54,
    )


def batch_scales(sums_ref):
    count = sums_ref[2:3, :]
    average = sums_ref[0:1, :] / count
    return count, average, lax.rsqrt(sums_ref[1:2, :] / count - average * average + EPSILON)


def conv_out_kernel(*refs, pieces, weights, save):
    place_ref, lengths_ref, affine_ref, sums_ref, convolved_ref = refs[:5]
    refs = refs[5:]
    weight_refs, refs = refs[:weights], refs[weights:]
    swished_ref, hi_ref, next_ref, own_ref, weight, plain, semaphores = refs
    row_count, channels = convolved_ref.shape
    row_block = row_count // pieces
    copies = Copies(semaphores)
    weight_copies_ = copies.weight(
        weight_refs, weight, slice(2 * channels, 3 * channels)
    )
    firsts = block_firsts(place_ref, pieces, row_block)
    places = lax.broadcasted_iota(jnp.int32, (row_count, 1), 0)
    valid = (segment_of(lengths_ref, places) < lengths_ref.shape[1]).astype(FLOAT)
    _, average, inverse = batch_scales(sums_ref)
    hatted = (convolved_ref[...] - average) * inverse
    normalized = hatted * affine_ref[0:1, :] + affine_ref[1:2, :]
    plain[...] = (normalized * jax.nn.sigmoid(normalized) * valid).astype(LOW)
    for q in range(pieces):
        swished_ref[q * row_block : (q + 1) * row_block, :] = plain[
            pl.ds(firsts[q], row_block), :
        ]
    save()

    wait(weight_copies_)

    @tiles(weight.shape[0])
    def _(features):
        write_parts(
            hi_ref, next_ref, own_ref, features, times_transposed(swished_ref[...], weight[features, :])
        )


def conv_out(place, lengths, affine, sums, convolved, weights, pieces, features):
    row_count, channels = convolved.shape
    return call(
        functools.partial(conv_out_kernel, pieces=pieces, weights=len(weights)),
        [((row_count, channels), LOW)] + row_parts(row_count, features),
        [
            pltpu.VMEM((features, channels), LOW),
            pltpu.VMEM((row_count, channels), LOW),
            pltpu.SemaphoreType.DMA((len(weights),)),
        ],
        2 * row_count * features * channels,
        ("smem", place), ("smem", lengths),
        ("vmem", affine), ("vmem", sums), ("vmem", convolved),
        *[("any" if len(weights) > 1 else "hbm", array) for array in weights],
        saved=(0,), room=50,
    )


def conv_back_sums_kernel(*refs, pieces, weights, save):
    place_ref, lengths_ref, affine_ref, sums_ref, convolved_ref = refs[:5]
    refs = refs[5:]
    row_refs, refs = refs[:pieces], refs[pieces:]
    weight_refs, refs = refs[:weights], refs[weights:]
    rows_ref, normal_ref, back_ref, weight, plain, semaphores = refs
    row_count, channels = convolved_ref.shape
    row_block = row_count // pieces
    copies = Copies(semaphores)
    rows_copies = copies.stack(row_refs, rows_ref)
    weight_copies_ = copies.weight(
        weight_refs, weight, slice(2 * channels, 3 * channels)
    )
    firsts = block_firsts(place_ref, pieces, row_block)
    places = lax.broadcasted_iota(jnp.int32, (row_count, 1), 0)
    valid = (segment_of(lengths_ref, places) < lengths_ref.shape[1]).astype(FLOAT)
    _, average, inverse = batch_scales(sums_ref)
    hatted = (convolved_ref[...] - average) * inverse
    normalized = hatted * affine_ref[0:1, :] + affine_ref[1:2, :]
    squashed = jax.nn.sigmoid(normalized)
    wait(rows_copies + weight_copies_)
    product = matmul(rows_ref[...], weight[...])
    for q in range(pieces):
        plain[pl.ds(firsts[q], row_block), :] = product[q * row_block : (q + 1) * row_block]
    save()

    normal = plain[...] * valid * squashed * (1.0 + normalized * (1.0 - squashed))
    normal_ref[...] = normal
    back_ref[...] = jnp.zeros_like(back_ref)
    back_ref[0:1, :] = jnp.sum(normal, axis=0, keepdims=True)
    back_ref[1:2, :] = jnp.sum(normal * hatted, axis=0, keepdims=True)


def conv_back_sums(place, lengths, affine, sums, convolved, rows, weights):
    row_count, channels = convolved.shape
    features = rows[0].shape[1]
    return call(
        functools.partial(conv_back_sums_kernel, pieces=len(rows), weights=len(weights)),
        [
            ((row_count, features), LOW), ((row_count, channels), FLOAT), ((8, channels), FLOAT)
        ],
        [
            pltpu.VMEM((features, channels), LOW),
            pltpu.VMEM((row_count, channels), FLOAT),
            pltpu.SemaphoreType.DMA((len(rows) + len(weights),)),
        ],
        2 * row_count * features * channels,
        ("smem", place), ("smem", lengths),
        ("vmem", affine), ("vmem", sums), ("vmem", convolved),
        *[("any", array) for array in rows],
        *[("any" if len(weights) > 1 else "hbm", array) for array in weights],
        saved=(0,),
    )


def conv_back_kernel(*refs, pieces, weights, save):
    (
        place_ref, lengths_ref, taps_ref, affine_ref, sums_ref, back_ref,
        convolved_ref, normal_ref, lifted_ref,
    ) = refs[:9]
    refs = refs[9:]
    weight_refs, refs = refs[:weights], refs[weights:]
    lifted_grad_ref, taps_grad_ref, hi_ref, next_ref, own_ref, weight, padded, padded_grad, plain, semaphores = refs
    row_count, channels = convolved_ref.shape
    taps = taps_ref.shape[0]
    row_block = row_count // pieces
    copies = Copies(semaphores)
    weight_copies_ = copies.weight(weight_refs, weight, slice(0, 2 * channels))
    firsts = block_firsts(place_ref, pieces, row_block)
    valid, matches = conv_matches(lengths_ref, row_count, taps)
    count, average, inverse = batch_scales(sums_ref)
    gain = affine_ref[0:1, :]
    hatted = (convolved_ref[...] - average) * inverse
    conv_grad = inverse * (
        normal_ref[...] * gain
        - valid * gain * (back_ref[0:1, :] + hatted * back_ref[1:2, :]) / count
    )
    value = lifted_ref[:, :channels]
    gate = jax.nn.sigmoid(lifted_ref[:, channels:])
    for scratch in (padded, padded_grad):
        scratch[:MARGIN, :] = jnp.zeros((MARGIN, channels), FLOAT)
        scratch[MARGIN + row_count :, :] = jnp.zeros((MARGIN, channels), FLOAT)
    padded[MARGIN : MARGIN + row_count, :] = value * gate * valid
    padded_grad[MARGIN : MARGIN + row_count, :] = conv_grad
    taps_grad_ref[...] = jnp.zeros_like(taps_grad_ref)
    gated_grad = jnp.zeros((row_count, channels), FLOAT)
    for t in range(taps):
        offset = t - taps // 2
        read = padded[MARGIN + offset : MARGIN + offset + row_count, :]
        taps_grad_ref[t : t + 1, :] = jnp.sum(
            matches[t] * read * conv_grad, axis=0, keepdims=True
        )
        back = padded_grad[MARGIN - offset : MARGIN - offset + row_count, :]
        gated_grad += taps_ref[t : t + 1, :] * matches[taps - 1 - t] * back
    gated_grad = gated_grad * valid
    plain[:, :channels] = (gated_grad * gate).astype(LOW)
    plain[:, channels:] = (gated_grad * value * gate * (1.0 - gate)).astype(LOW)
    for q in range(pieces):
        lifted_grad_ref[q * row_block : (q + 1) * row_block, :] = plain[
            pl.ds(firsts[q], row_block), :
        ]
    save()

    wait(weight_copies_)

    @tiles(weight.shape[0])
    def _(features):
        write_parts(
            hi_ref, next_ref, own_ref, features,
            times_transposed(lifted_grad_ref[...], weight[features, :]),
        )


def conv_back(
    place, lengths, taps, affine, sums, back, convolved, normal, lifted, weights, pieces,
    features,
):
    row_count, channels = convolved.shape
    return call(
        functools.partial(conv_back_kernel, pieces=pieces, weights=len(weights)),
        [((row_count, 2 * channels), LOW), ((8, channels), FLOAT)] + row_parts(row_count, features),
        [
            pltpu.VMEM((features, 2 * channels), LOW),
            pltpu.VMEM((row_count + 2 * MARGIN, channels), FLOAT),
            pltpu.VMEM((row_count + 2 * MARGIN, channels), FLOAT),
            pltpu.VMEM((row_count, 2 * channels), LOW),
            pltpu.SemaphoreType.DMA((len(weights),)),
        ],
        4 * row_count * features * channels,
        ("smem", place), ("smem", lengths),
        *[
            ("vmem", array)
            for array in (taps, affine, sums, back, convolved, normal, lifted)
        ],
        *[("any" if len(weights) > 1 else "hbm", array) for array in weights],
        saved=(0,),
    )


def standardize(values):
    average = jnp.mean(values, axis=-1, keepdims=True)
    centred = values - average
    spread_of = jnp.mean(centred * centred, axis=-1, keepdims=True)
    scale = lax.rsqrt(spread_of + EPSILON)
    return centred * scale, scale


def norm_back(values, norm_gain, normed_grad):
    hat, scale = standardize(values)
    gained = normed_grad * norm_gain
    first = jnp.mean(gained, axis=-1, keepdims=True)
    second = jnp.mean(gained * hat, axis=-1, keepdims=True)
    grad = (gained - first - hat * second) * scale
    return grad, jnp.sum(normed_grad * hat, axis=0, keepdims=True)


def middle_kernel(next_ref, arrived_ref, sent_ref):
    first = next_ref.shape[0]
    sent_ref[...] = (
        next_ref[...].astype(FLOAT) + arrived_ref[first:, :].astype(FLOAT)
    ).astype(LOW)


def sum_rows(hi, next_part, own_part):
    arrived = swap(hi, "mp", 1)
    (sent,) = call(
        middle_kernel, [(next_part.shape, LOW)], [], next_part.size,
        ("vmem", next_part), ("vmem", arrived),
    )
    return (own_part, arrived, swap(sent, "mp", 2)), sent


def summed(own_ref, near_ref, far_ref):
    rows = own_ref.shape[0]
    return own_ref[...] + near_ref[:rows, :].astype(FLOAT) + far_ref[...].astype(FLOAT)


def all_rows(own):
    across = swap(own, "mp", 2)
    return [own, across, swap(own, "mp", 1), swap(across, "mp", 1)]


def step_kernel(
    own_ref, near_ref, far_ref, residual_ref, gain_ref, next_ref, normed_ref, *, factor
):
    residual = residual_ref[...].astype(FLOAT) + factor * summed(own_ref, near_ref, far_ref)
    next_ref[...] = residual
    normed_ref[...] = (standardize(residual)[0] * gain_ref[...]).astype(LOW)


def step(parts, residual, gain, factor):
    shape = parts[0].shape
    return call(
        functools.partial(step_kernel, factor=factor), [(shape, FLOAT), (shape, LOW)], [],
        8 * math.prod(shape),
        *[("vmem", array) for array in (*parts, residual, gain)],
    )


def turn_kernel(
    own_ref, near_ref, far_ref, residual_ref, gain_ref, out_grad_ref,
    result_ref, grad_ref, branch_ref, gain_grad_ref,
):
    residual = residual_ref[...] + 0.5 * summed(own_ref, near_ref, far_ref)
    gain = gain_ref[...]
    result_ref[...] = (standardize(residual)[0] * gain).astype(LOW)
    grad, gain_grad = norm_back(residual, gain, out_grad_ref[...].astype(FLOAT))
    grad_ref[...] = grad
    branch_ref[...] = (0.5 * grad).astype(LOW)
    gain_grad_ref[...] = gain_grad


def turn(parts, residual, gain, out_grad):
    shape = parts[0].shape
    return call(
        turn_kernel,
        [(shape, LOW), (shape, FLOAT), (shape, LOW), ((1, shape[1]), FLOAT)], [],
        16 * math.prod(shape),
        *[("vmem", array) for array in (*parts, residual, gain, out_grad)],
    )


def step_back_kernel(
    own_ref, near_ref, far_ref, residual_ref, gain_ref, grad_ref,
    next_ref, branch_ref, gain_grad_ref, *, factor,
):
    normed_grad = summed(own_ref, near_ref, far_ref)
    grad, gain_grad = norm_back(residual_ref[...].astype(FLOAT), gain_ref[...], normed_grad)
    grad = grad_ref[...] + grad
    next_ref[...] = grad
    branch_ref[...] = (factor * grad).astype(LOW)
    gain_grad_ref[...] = gain_grad


def step_back(parts, residual, gain, grad, factor):
    shape = parts[0].shape
    return call(
        functools.partial(step_back_kernel, factor=factor),
        [(shape, FLOAT), (shape, LOW), ((1, shape[1]), FLOAT)], [],
        16 * math.prod(shape),
        *[("vmem", array) for array in (*parts, residual, gain, grad)],
    )


def select_kernel(place_ref, *refs):
    pieces, target_ref = refs[:-1], refs[-1]
    row_block = pieces[0].shape[0]
    for piece, first in zip(pieces, block_firsts(place_ref, len(pieces), row_block)):
        target_ref[pl.ds(first, row_block), :] = piece[...].astype(target_ref.dtype)


def select_rows(place, pieces, kind):
    row_block, features = pieces[0].shape
    (outcome,) = call(
        select_kernel, [((len(pieces) * row_block, features), kind)], [], 0,
        ("smem", place), *[("vmem", piece) for piece in pieces], limit=16,
    )
    return outcome


def finish_kernel(*refs, counts):
    sources, targets = refs[: 2 * len(counts)], refs[2 * len(counts) :]
    at = 0
    for i, count in enumerate(counts):
        total = sources[2 * i][...] + sources[2 * i + 1][...].astype(FLOAT)
        first = 0
        for target in targets[at : at + count]:
            last = first + target.shape[1]
            target[...] = total[:, first:last]
            first = last
        at += count


def finish(sums, widths, *tokens):
    rows = sums[0].kept.shape[0]
    parts, counts, left = [], [], list(widths)
    for part in sums:
        parts += [("vmem", part.kept), ("vmem", after(part.sent, *tokens))]
        count, total = 0, 0
        while total < part.kept.shape[1]:
            total, count = total + left.pop(0), count + 1
        counts.append(count)
    return call(
        functools.partial(finish_kernel, counts=tuple(counts)),
        [((rows, width), FLOAT) for width in widths], [], 0, *parts,
    )


def join_kernel(*refs):
    target, first = refs[-1], 0
    for kept, arrived in zip(refs[0:-1:2], refs[1:-1:2]):
        last = first + kept.shape[1]
        target[:, first:last] = kept[...] + arrived[...].astype(FLOAT)
        first = last


def join(sums):
    rows, width = sums[0].kept.shape[0], sum(part.kept.shape[1] for part in sums)
    parts = []
    for part in sums:
        parts += [("vmem", part.kept), ("vmem", part.sent)]
    return call(join_kernel, [((rows, width), FLOAT)], [], 0, *parts)[0]


def per_device(
    inputs,
    lengths,
    out_grad,
    first_norm,
    first_up,
    first_down,
    attention_norm,
    query_weight,
    key_weight,
    value_weight,
    position_weight,
    output_weight,
    content_bias,
    position_bias,
    convolution_norm,
    pointwise_in,
    depthwise_kernel,
    batch_gain,
    batch_shift,
    pointwise_out,
    second_norm,
    second_up,
    second_down,
    final_norm,
):
    row_count, feature_count = inputs.shape
    dp_size, mp_size = lax.axis_size("dp"), lax.axis_size("mp")
    dp_at, mp_at = lax.axis_index("dp"), lax.axis_index("mp")
    block, hidden = first_up.shape
    row_block = row_count // mp_size
    bias_rows, head_count = content_bias.shape
    head_size = bias_rows * dp_size
    heads = head_count * head_size
    local_channels, tap_count = depthwise_kernel.shape
    channels = local_channels * dp_size
    place = mp_at.reshape(1).astype(jnp.int32)

    places = jnp.arange(feature_count, dtype=jnp.int32)
    owners = dp_at ^ reversed_bits(places // block, dp_size)
    source = owners * block + places % block
    selection = (places[:, None] == source[None, :]).astype(LOW)
    block_places = jnp.arange(dp_size, dtype=jnp.int32)
    block_owners = (dp_at ^ reversed_bits(block_places, dp_size)).astype(jnp.int32)
    block_selection = (block_places[:, None] == block_owners[None, :]).astype(LOW)

    up_own = first_up.astype(LOW)
    small_own = jnp.concatenate(
        [
            part.reshape(-1)
            for part in (
                first_norm, attention_norm, convolution_norm, second_norm, final_norm,
                content_bias, position_bias, depthwise_kernel, batch_gain, batch_shift,
            )
        ]
    )
    small_own = after(small_own, up_own).astype(LOW)
    links = Links(4)
    up_spread = Spread(links, up_own)
    up_spread.go(ORDER)
    ups = up_spread.blocks
    down_own = after(first_down, ups[1]).astype(LOW)
    down_spread = Spread(links, down_own)
    down_spread.go(ORDER)
    downs = down_spread.blocks
    gates, mask = [downs[1], ups[5], ups[3]], dp_size // 2
    small_all = small_own[None]
    while mask:
        arrived = swap(small_all, "dp", mask)
        if gates:
            arrived = after(arrived, gates.pop())
        small_all = jnp.concatenate([small_all, arrived], axis=0)
        mask //= 2

    attention_own = jnp.concatenate(
        after(
            (query_weight, key_weight, value_weight, position_weight, output_weight), ups[3]
        ),
        axis=1,
    ).astype(LOW)
    attention_spread = Spread(links, attention_own)
    attention_spread.go(ORDER[:3], time=10)
    pointwise_in, pointwise_out, second_up, second_down = after(
        (pointwise_in, pointwise_out, second_up, second_down), ups[2]
    )
    convolution_own = jnp.concatenate(
        [pointwise_in.reshape(block, 2 * channels), pointwise_out], axis=1
    ).astype(LOW)
    second_own = jnp.concatenate([second_up, second_down], axis=1).astype(LOW)

    whole, first_half, second_half = (
        slice(0, hidden), slice(0, hidden), slice(hidden, 2 * hidden)
    )

    norms = small_all[:, : 5 * block].astype(FLOAT).reshape(dp_size, 5, block)
    norms = norms.transpose(1, 0, 2).reshape(5, 1, feature_count)
    first_gain, attention_gain, convolution_gain, second_gain, final_gain = norms
    plain_small = matmul(block_selection, small_all[:, 5 * block :])
    cut = bias_rows * head_count
    content_all = plain_small[:, :cut].reshape(head_size, head_count).T
    position_all = plain_small[:, cut : 2 * cut].reshape(head_size, head_count).T
    at = 2 * cut + local_channels * tap_count
    taps = plain_small[:, 2 * cut : at].reshape(channels, tap_count).T
    affine = jnp.stack(
        [
            plain_small[:, at : at + local_channels].reshape(channels),
            plain_small[:, at + local_channels :].reshape(channels),
        ]
    )

    arranged = matmul(
        jnp.concatenate(
            [
                lax.dynamic_slice_in_dim(
                    inputs, (mp_at ^ fixed_reversed(q, mp_size)) * row_block, row_block, axis=0
                )
                for q in range(mp_size)
            ],
            axis=0,
        ),
        selection,
    )
    own_out_grad = matmul(
        lax.dynamic_slice_in_dim(out_grad, mp_at * row_block, row_block, axis=0), selection
    ).astype(LOW)
    table_places = after(jnp.arange(2 * row_count, dtype=jnp.int32), ups[3])
    sin_table = position_table(table_places, row_count, feature_count)
    sin_table = matmul(sin_table, selection).astype(LOW)

    residual_zero = arranged[:row_block].astype(LOW)
    hat_a = standardize(arranged)[0]
    normed_a = (hat_a * first_gain).astype(LOW)
    hat_a = hat_a.astype(LOW)
    _, before_a, active_a, up_a, down_a, hi, next_part, own_part = ffn_call(
        ffn_forward_kernel, [normed_a], ups, downs, whole, whole, room=54
    )
    attention_spread.go((3, 5), hi, time=10)
    parts, sent = sum_rows(hi, next_part, own_part)
    attention_spread.go((6,), sent, time=10)
    attention_spread.go((7,), parts[2], time=10)
    attention_all = attention_spread.blocks
    convolution_spread = Spread(links, after(convolution_own, sent))
    convolution_spread.go(ORDER[:3], time=10)
    residual_one, own_b = step(parts, residual_zero, attention_gain, 0.5)
    second_spread = Spread(links, after(second_own, sent))

    (
        normed_b, mixed_rows, prob, content_rows, position_rows, keys, values, position,
        attention_weight, hi, next_part, own_part,
    ) = attention_forward(
        place, lengths, all_rows(own_b), attention_all, sin_table, content_all,
        position_all,
    )
    parts, sent = sum_rows(hi, next_part, own_part)
    convolution_spread.go((3, 5, 6), sent, time=10)
    convolution_spread.go((7,), parts[2], time=10)
    convolution_all = convolution_spread.blocks
    second_spread.go(ORDER[:3], time=10)
    residual_two, own_c = step(parts, residual_one, convolution_gain, 1.0)
    rows = all_rows(own_c)

    normed_c, lifted, convolution_weight, convolved, sums = conv_lift(
        place, lengths, taps, rows, convolution_all
    )
    second_spread.go(ORDER[3:5], sums, time=10)
    sums, _ = total_hops(sums, "dp")
    second_spread.go(ORDER[5:], sums, time=10)
    swished, hi, next_part, own_part = conv_out(
        place, lengths, affine, sums, convolved, [convolution_weight], mp_size,
        feature_count,
    )
    parts, sent = sum_rows(hi, next_part, own_part)
    residual_three, own_d = step(parts, residual_two, second_gain, 1.0)
    second_all = second_spread.blocks

    normed_d, before_d, active_d, up_d, down_d, hi, next_part, own_part = ffn_call(
        ffn_forward_kernel, all_rows(own_d), second_all, second_all, first_half,
        second_half, room=50,
    )
    parts, sent = sum_rows(hi, next_part, own_part)
    own_result, residual_grad, branch, final_gain_grad = turn(
        parts, residual_three, final_gain, own_out_grad
    )

    branch_rows, before_grad, hi, next_part, own_part = ffn_call(
        ffn_backward_kernel, all_rows(branch), [up_d], [down_d], whole, whole, before_d,
    )
    links = Links(3, apart=True)
    parts, sent = sum_rows(hi, next_part, own_part)
    second_down_sum = WeightSum((after(branch_rows, sent), active_d))
    second_down_sum.advance(links=links)
    residual_grad, branch, second_gain_grad = step_back(
        parts, residual_three, second_gain, residual_grad, 1.0
    )
    second_up_sum = WeightSum((after(normed_d, branch), before_grad))

    branch_rows, normal, back_sums = conv_back_sums(
        place, lengths, affine, sums, convolved, all_rows(branch), [convolution_weight]
    )
    back_sums, hops = total_hops(back_sums, "dp")
    second_down_sum.advance(hops[-2], links=links)
    second_up_sum.advance(hops[-1], links=links)
    lifted_grad, taps_grad, hi, next_part, own_part = conv_back(
        place, lengths, taps, affine, sums, back_sums, convolved, normal, lifted,
        [convolution_weight], mp_size, feature_count,
    )
    parts, sent = sum_rows(hi, next_part, own_part)
    convolution_sum = WeightSum(
        (normed_c, after(lifted_grad, sent)), (branch_rows, after(swished, sent))
    )
    convolution_sum.advance(links=links)
    residual_grad, branch, convolution_gain_grad = step_back(
        parts, residual_two, convolution_gain, residual_grad, 1.0
    )
    second_down_sum.advance(branch, links=links)
    first_row = dp_at * local_channels
    gain_piece = lax.dynamic_slice_in_dim(back_sums[1], first_row, local_channels)
    shift_piece = lax.dynamic_slice_in_dim(back_sums[0], first_row, local_channels)

    branch_rows, qkv_grad, position_grad, bias_grads, hi, next_part, own_part = attention_backward(
        place, all_rows(branch), [attention_weight],
        (position, prob, content_rows, position_rows, keys, values), head_count,
    )
    parts, sent = sum_rows(hi, next_part, own_part)
    convolution_sum.advance(sent, links=links)
    residual_grad, branch, attention_gain_grad = step_back(
        parts, residual_one, attention_gain, residual_grad, 0.5
    )
    attention_sum = WeightSum(
        (normed_b, after(qkv_grad, sent)), (sin_table, after(position_grad, sent)),
        (branch_rows, after(mixed_rows, sent)),
    )
    attention_later = []
    attention_sum.advance(links=links, later=attention_later)
    second_up_sum.advance(branch, links=links)

    bias_grads, taps_grad = after((bias_grads, taps_grad), branch)
    plain_grads = jnp.concatenate(
        [
            bias_grads[:head_count].T.reshape(dp_size, cut),
            bias_grads[head_count:].T.reshape(dp_size, cut),
            taps_grad[:tap_count].T.reshape(dp_size, local_channels * tap_count),
        ],
        axis=1,
    )
    plain_grads = lax.dot_general(
        block_selection.astype(FLOAT), plain_grads, (((0,), (0,)), ((), ())),
        precision=lax.Precision.HIGHEST, preferred_element_type=FLOAT,
    )

    branch_rows, before_grad, hi, next_part, own_part, gain_grads = ffn_call(
        ffn_backward_kernel, all_rows(branch), [up_a], [down_a], whole, whole, before_a,
        (
            hat_a, attention_gain_grad, convolution_gain_grad, second_gain_grad, final_gain_grad
        ),
    )
    attention_later.append(hi)
    first_down_sum = WeightSum((branch_rows, active_a))
    first_up_sum = WeightSum((normed_a, before_grad))

    parts, sent = sum_rows(hi, next_part, own_part)
    first_down_sum.advance(later=(sent,))
    first_up_sum.advance(first_down_sum.upper, later=(sent,))
    convolution_sum.advance(first_down_sum.upper)
    second_up_sum.advance(first_down_sum.upper)
    attention_sum.advance()
    residual_grad, _, _ = step_back(
        after(parts, attention_sum.upper), residual_zero, first_gain, residual_grad, 1.0
    )
    inputs_rows = all_rows(
        times_transposed(residual_grad.astype(LOW), selection).astype(LOW)
    )
    result_rows = all_rows(
        times_transposed(after(own_result, parts[2]), selection).astype(LOW)
    )
    first_down_sum.advance(attention_sum.upper)

    attention_sum.advance(
        first_down_sum.upper, convolution_sum.sent, second_up_sum.sent, second_down_sum.sent
    )
    gain_grads, plain_grads = after((gain_grads, plain_grads), attention_sum.upper)
    mask, small_hops = 1, []
    while 4 * mask < dp_size:
        width, count = gain_grads.shape[1] // 2, plain_grads.shape[0] // 2
        small_hops.append(
            (swap(gain_grads[:, width:], "dp", mask), swap(plain_grads[count:], "dp", mask))
        )
        if 8 * mask < dp_size:
            gain_grads = gain_grads[:, :width] + small_hops[-1][0]
            plain_grads = plain_grads[:count] + small_hops[-1][1]
        mask *= 2

    first_down_sum.advance(attention_sum.upper)
    first_up_sum.advance(first_down_sum.upper, inputs_rows[3], result_rows[3])

    arrived = after(small_hops[-1], first_up_sum.upper)
    gain_grads = gain_grads[:, :width] + arrived[0]
    plain_grads = plain_grads[:count] + arrived[1]
    arrived = []
    masks = (dp_size // 2, dp_size // 4, 3 * dp_size // 4)
    for p, mask in enumerate(masks):
        columns = slice((p + 1) * block, (p + 2) * block)
        arrived.append(
            (
                swap(gain_grads[:, columns], "dp", mask),
                swap(plain_grads[p + 1 : p + 2], "dp", mask),
            )
        )
    gain_grads, plain_grads = gain_grads[:, :block], plain_grads[:1]

    last_hop = first_up_sum.sent
    first_up_sum.advance(attention_sum.sent, first_down_sum.sent)
    arrived = after(arrived, first_up_sum.upper)
    for gain_hop, plain_hop in arrived:
        gain_grads = gain_grads + gain_hop
        plain_grads = plain_grads + plain_hop
    for part in (
        second_down_sum, second_up_sum, convolution_sum, attention_sum, first_down_sum,
        first_up_sum,
    ):
        part.rest()

    second_down_grad, second_up_grad, convolution_in_grad, convolution_out_grad = finish(
        [second_down_sum, second_up_sum, convolution_sum],
        [hidden, hidden, 2 * channels, channels], last_hop,
    )
    attention_grads = finish([attention_sum], [heads] * 5, last_hop)
    first_down_grad, first_up_grad = join([first_down_sum]), join([first_up_sum])

    result = select_rows(place, after(result_rows, first_up_sum.upper), LOW)
    inputs_grad = select_rows(place, after(inputs_rows, first_up_sum.upper), FLOAT)

    gain_grads, plain_grads = total_over(gain_grads, "mp"), plain_grads[0]

    return (
        result,
        inputs_grad,
        gain_grads[0],
        first_up_grad,
        first_down_grad,
        gain_grads[1],
        *attention_grads,
        plain_grads[:cut].reshape(bias_rows, head_count),
        plain_grads[cut : 2 * cut].reshape(bias_rows, head_count),
        gain_grads[2],
        convolution_in_grad.reshape(block, 2, channels),
        plain_grads[2 * cut :].reshape(local_channels, tap_count),
        gain_piece,
        shift_piece,
        convolution_out_grad,
        gain_grads[3],
        second_up_grad,
        second_down_grad,
        gain_grads[4],
    )


def solution(mesh):
    return jax.shard_map(
        per_device,
        mesh=mesh,
        in_specs=(
            P("dp", None),
            P("dp", None),
            P("dp", None),
            P("dp"),
            P("dp", "mp"),
            P("dp", "mp"),
            P("dp"),
            P("dp", "mp"),
            P("dp", "mp"),
            P("dp", "mp"),
            P("dp", "mp"),
            P("dp", "mp"),
            P("dp", "mp"),
            P("dp", "mp"),
            P("dp"),
            P("dp", None, "mp"),
            P(("mp", "dp"), None),
            P(("mp", "dp")),
            P(("mp", "dp")),
            P("dp", "mp"),
            P("dp"),
            P("dp", "mp"),
            P("dp", "mp"),
            P("dp"),
        ),
        out_specs=(
            P("dp", None),
            P("dp", None),
            P("dp"),
            P("dp", "mp"),
            P("dp", "mp"),
            P("dp"),
            P("dp", "mp"),
            P("dp", "mp"),
            P("dp", "mp"),
            P("dp", "mp"),
            P("dp", "mp"),
            P("dp", "mp"),
            P("dp", "mp"),
            P("dp"),
            P("dp", None, "mp"),
            P(("mp", "dp"), None),
            P(("mp", "dp")),
            P(("mp", "dp")),
            P("dp", "mp"),
            P("dp"),
            P("dp", "mp"),
            P("dp", "mp"),
            P("dp"),
        ),
        check_vma=False,
    )
```

```python
import functools
import math

import jax
import jax.numpy as jnp
from jax import lax
from jax.experimental import pallas as pl
from jax.experimental.pallas import tpu as pltpu
from jax.sharding import PartitionSpec as P

EPSILON = 1e-05
LOW = jnp.bfloat16
FLOAT = jnp.float32


def matmul(left_side, right_side):
    return jnp.dot(left_side, right_side, preferred_element_type=FLOAT)


def times_transposed(left_side, right_side):
    return lax.dot_general(
        left_side, right_side, (((1,), (1,)), ((), ())), preferred_element_type=FLOAT
    )


def outer_sum(left_side, right_side):
    return lax.dot_general(
        left_side, right_side, (((0,), (0,)), ((), ())), preferred_element_type=FLOAT
    )


def reversed_bits(places, size):
    outcome = places * 0
    mask, back = size // 2, 1
    while mask:
        outcome = outcome + ((places // back) % 2) * mask
        mask, back = mask // 2, back * 2
    return outcome


def swap(values, axis, mask):
    size = lax.axis_size(axis)
    return lax.ppermute(values, axis, [(i, i ^ mask) for i in range(size)])


def after(values, *tokens):
    return lax.optimization_barrier((values, tokens))[0] if tokens else values


class Links:
    def __init__(self, depth, apart=False):
        self.depth, self.apart, self.queues = depth, apart, {}

    def swap(self, values, mask, time=None):
        queue, depth = self.queues.setdefault(self.apart and mask == 1, []), self.depth
        if len(queue) >= depth:
            values = after(values, *queue[-2 * depth : len(queue) + 1 - depth])
        arrived = swap(values, "dp", mask)
        queue.append(arrived if time is None else held(arrived, time))
        return queue[-1]


ORDER = (4, 1, 2, 3, 5, 6, 7)


def pass_kernel(source_ref, target_ref):
    pass


def held(values, microseconds):
    return pl.pallas_call(
        pass_kernel,
        out_shape=jax.ShapeDtypeStruct(values.shape, values.dtype),
        in_specs=[pl.BlockSpec(memory_space=pl.ANY)],
        out_specs=pl.BlockSpec(memory_space=pl.ANY),
        input_output_aliases={0: 0},
        cost_estimate=pl.CostEstimate(
            flops=int(1.1e9 * microseconds), bytes_accessed=0, transcendentals=0
        ),
    )(values)


class Spread:
    def __init__(self, links, own):
        self.links, self.mask = links, lax.axis_size("dp") // 2
        while self.mask > 4:
            own = jnp.concatenate([own, links.swap(own, self.mask)], axis=0)
            self.mask //= 2
        self.blocks = [own] + [None] * (2 * self.mask - 1)

    def go(self, places, *tokens, time=None):
        for p in places:
            if p < len(self.blocks):
                top = 1 << (p.bit_length() - 1)
                self.blocks[p] = self.links.swap(
                    after(self.blocks[p - top], *tokens), self.mask // top,
                    time if p < 4 or time is None else 10,
                )


def spread(values, axis):
    mask = lax.axis_size(axis) // 2
    while mask:
        values = jnp.concatenate([values, swap(values, axis, mask)], axis=0)
        mask //= 2
    return values


def collect(values, axis, wire, mask=1):
    while mask < lax.axis_size(axis):
        half = values.shape[0] // 2
        values = values[:half] + swap(values[half:].astype(wire), axis, mask).astype(FLOAT)
        mask *= 2
    return values


def total_over(values, axis):
    mask = 1
    while mask < lax.axis_size(axis):
        values = values + swap(values, axis, mask)
        mask *= 2
    return values


def total_hops(values, axis):
    arrivals, mask = [], lax.axis_size(axis) // 2
    while mask:
        arrivals.append(swap(values, axis, mask))
        values = values + arrivals[-1]
        mask //= 2
    return values, arrivals


class WeightSum:
    def __init__(self, *pairs):
        self.pairs, self.mask = pairs, 0

    def advance(self, *tokens, links=None, later=()):
        if not self.mask:
            half = self.pairs[0][0].shape[1] // 2
            upper = [outer_sum(left[:, half:], right).astype(LOW) for left, right in self.pairs]
            self.later = later
            self.upper, self.mask = after(jnp.concatenate(upper, axis=1), *tokens), 1
        else:
            if self.mask == 1 << 1:
                lower = [
                    outer_sum(after(left, *self.later)[:, : left.shape[1] // 2], right)
                    for left, right in self.pairs
                ]
                self.kept = jnp.concatenate(lower, axis=1)
            total = self.kept + after(self.sent, *tokens).astype(FLOAT)
            half = total.shape[0] // 2
            self.upper, self.kept = total[half:].astype(LOW), total[:half]
        if links is None:
            self.sent = swap(self.upper, "dp", self.mask)
        else:
            self.sent = links.swap(self.upper, self.mask)
        self.mask *= 2

    def rest(self, *tokens):
        while self.mask < lax.axis_size("dp"):
            self.advance(*tokens)


def position_table(places, row_count, feature_count):
    rates = jnp.exp(
        jnp.arange(0, feature_count, 2).astype(FLOAT) * (-math.log(10000.0) / feature_count)
    )
    stride = 32
    count = places.shape[0] // stride
    coarse = (row_count - 1 - stride * places[:count]).astype(FLOAT)[:, None] * rates[None, :]
    fine = -places[:stride].astype(FLOAT)[:, None] * rates[None, :]
    coarse_sin, coarse_cos = jnp.sin(coarse)[:, None], jnp.cos(coarse)[:, None]
    fine_sin, fine_cos = jnp.sin(fine)[None], jnp.cos(fine)[None]
    sines = coarse_sin * fine_cos + coarse_cos * fine_sin
    cosines = coarse_cos * fine_cos - coarse_sin * fine_sin
    table = jnp.concatenate([sines, cosines], axis=2).astype(LOW)
    return table.reshape(places.shape[0], feature_count)


def fixed_reversed(place, size):
    outcome, mask = 0, size // 2
    while mask:
        outcome, place, mask = outcome + (place % 2) * mask, place // 2, mask // 2
    return outcome


def relative_window(position_ref, first, row_block, columns):
    row_count = position_ref.shape[0] // 2
    start = pl.multiple_of(row_count - row_block - first, row_block)
    return position_ref.at[pl.ds(start, row_count + row_block), columns]


def in_smem():
    return pl.BlockSpec(memory_space=pltpu.SMEM)


def in_vmem():
    return pl.BlockSpec(memory_space=pltpu.VMEM)


def in_hbm():
    return pl.BlockSpec(memory_space=pltpu.HBM)


def anywhere():
    return pl.BlockSpec(memory_space=pl.ANY)


def call(kernel, outs, scratch, flops, *operands, limit=6, room=50, saved=()):
    places = dict(smem=in_smem, vmem=in_vmem, any=anywhere, hbm=in_hbm)
    count, inner = len(operands), len(scratch)

    def saving(*refs):
        sources, targets, rest = (
            refs[:count], list(refs[count : count + len(outs)]), refs[count + len(outs) :]
        )
        kept, held_refs, semaphores = rest[:inner], rest[inner:-1], rest[-1]
        copies = [
            pltpu.make_async_copy(ref, targets[i], semaphores.at[n])
            for n, (i, ref) in enumerate(zip(saved, held_refs))
        ]
        for i, ref in zip(saved, held_refs):
            targets[i] = ref

        def save(*which):
            for n in which:
                copies[n].start()

        kernel(*sources, *targets, *kept, save=save)
        for copy in copies:
            copy.wait()

    extra = []
    if saved:
        extra = [pltpu.VMEM(*outs[i]) for i in saved] + [pltpu.SemaphoreType.DMA((len(saved),))]
    return pl.pallas_call(
        saving if saved else kernel,
        out_shape=tuple(jax.ShapeDtypeStruct(shape, kind) for shape, kind in outs),
        in_specs=[places[place]() for place, _ in operands],
        out_specs=tuple(in_hbm() if i in saved else in_vmem() for i in range(len(outs))),
        scratch_shapes=list(scratch) + extra,
        compiler_params=pltpu.CompilerParams(
            vmem_limit_bytes=(room if scratch else limit) * 2**20
        ),
        cost_estimate=pl.CostEstimate(flops=flops, bytes_accessed=0, transcendentals=0),
    )(*[array for _, array in operands])


class Copies:
    def __init__(self, semaphores):
        self.semaphores, self.count = semaphores, 0

    def start(self, source, target):
        copy = pltpu.make_async_copy(source, target, self.semaphores.at[self.count])
        copy.start()
        self.count += 1
        return copy

    def stack(self, sources, target, columns=None):
        copies, block = [], target.shape[0] // len(sources)
        for p, source in enumerate(sources):
            if columns is not None:
                source = source.at[:, columns]
            copies.append(self.start(source, target.at[pl.ds(p * block, block)]))
        return copies

    def weight(self, sources, target, columns):
        if len(sources) > 1:
            return self.stack(sources, target, columns)
        return [self.start(sources[0].at[:, columns], target)]


def wait(copies):
    for copy in copies:
        copy.wait()


TILE = 256


def write_parts(hi_ref, next_ref, own_ref, columns, product):
    half, own = hi_ref.shape[0], own_ref.shape[0]
    hi_ref[:, columns] = product[half:].astype(LOW)
    next_ref[:, columns] = product[own:half].astype(LOW)
    own_ref[:, columns] = product[:own]


def tiles(count):
    def loop(body):
        @pl.loop(0, count // TILE)
        def _(t):
            body(pl.ds(pl.multiple_of(t * TILE, TILE), TILE))

    return loop


def ffn_forward_kernel(*refs, pieces, weights, up_columns, down_columns, save):
    row_refs, refs = refs[:pieces], refs[pieces:]
    up_refs, refs = refs[:weights], refs[weights:]
    down_refs, refs = refs[:weights], refs[weights:]
    rows_ref, before_ref, active_ref, up, down, hi_ref, next_ref, own_ref, semaphores = refs
    copies = Copies(semaphores)
    rows_copies = copies.stack(row_refs, rows_ref)
    up_copies = copies.weight(up_refs, up, up_columns)
    down_copies = copies.weight(down_refs, down, down_columns)
    wait(rows_copies + up_copies)
    save(0, 3)

    @tiles(up.shape[1])
    def _(columns):
        before = matmul(rows_ref[...], up[:, columns])
        before_ref[:, columns] = before.astype(LOW)
        active_ref[:, columns] = (before * jax.nn.sigmoid(before)).astype(LOW)

    save(1, 2)
    wait(down_copies)
    save(4)

    @tiles(down.shape[0])
    def _(features):
        write_parts(
            hi_ref, next_ref, own_ref, features, times_transposed(active_ref[...], down[features, :])
        )


def ffn_backward_kernel(*refs, pieces, weights, up_columns, down_columns, gains, save):
    if gains:
        (hat_ref, *others), gain_grad_ref, refs = (
            refs[-9 - gains : -9], refs[-4], refs[: -9 - gains] + refs[-9:-4] + refs[-3:]
        )
        gain_grad_ref[...] = jnp.zeros_like(gain_grad_ref)
        for n, other in enumerate(others):
            gain_grad_ref[n + 1 : n + 2, :] = other[...]
    row_refs, refs = refs[:pieces], refs[pieces:]
    up_refs, refs = refs[:weights], refs[weights:]
    down_refs, refs = refs[:weights], refs[weights:]
    before_ref, rows_ref, grad_ref, hi_ref, next_ref, own_ref, up, down, semaphores = refs
    copies = Copies(semaphores)
    rows_copies = copies.stack(row_refs, rows_ref)
    down_copies = copies.weight(down_refs, down, down_columns)
    up_copies = copies.weight(up_refs, up, up_columns)
    wait(rows_copies + down_copies)
    save(0)

    @tiles(down.shape[1])
    def _(columns):
        before = before_ref[:, columns].astype(FLOAT)
        squashed = jax.nn.sigmoid(before)
        grad = matmul(rows_ref[...], down[:, columns])
        grad_ref[:, columns] = (grad * squashed * (1.0 + before * (1.0 - squashed))).astype(LOW)

    save(1)

    wait(up_copies)

    @tiles(up.shape[0])
    def _(features):
        product = times_transposed(grad_ref[...], up[features, :])
        write_parts(hi_ref, next_ref, own_ref, features, product)
        if gains:
            gain_grad_ref[0:1, features] = jnp.sum(
                product * hat_ref[:, features].astype(FLOAT), axis=0, keepdims=True
            )


def row_parts(rows, features):
    return [
        ((rows // 2, features), LOW), ((rows // 4, features), LOW), ((rows // 4, features), FLOAT)
    ]


def ffn_call(
    kernel, rows, ups, downs, up_columns, down_columns, before=None, hats=(), room=50
):
    row_count = len(rows) * rows[0].shape[0]
    features = rows[0].shape[1]
    hidden = up_columns.stop - up_columns.start
    outs = [((row_count, features), LOW)]
    outs += [((row_count, hidden), LOW)] * (2 if before is None else 1)
    weight = ((features, hidden), LOW)
    if before is None:
        outs += [weight] * 2
    count = len(rows) + 2 * len(ups)
    operands = [("any", array) for array in rows]
    operands += [("any" if len(ups) > 1 else "hbm", array) for array in list(ups) + list(downs)]
    if before is not None:
        operands.append(("vmem", before))
        kernel = functools.partial(kernel, gains=len(hats))
    outs += row_parts(row_count, features)
    if hats:
        operands += [("vmem", array) for array in hats]
        outs.append(((8, features), FLOAT))
    return call(
        functools.partial(
            kernel, pieces=len(rows), weights=len(ups), up_columns=up_columns,
            down_columns=down_columns,
        ),
        outs,
        [pltpu.VMEM(*weight)] * (0 if before is None else 2)
        + [pltpu.SemaphoreType.DMA((count,))],
        4 * row_count * features * hidden,
        *operands,
        saved=(0, 1, 2, 3, 4) if before is None else (0, 1), room=room,
    )


def segment_of(lengths_ref, places):
    bound, segment = 0, jnp.zeros(places.shape, jnp.int32)
    for s in range(lengths_ref.shape[1]):
        bound = bound + lengths_ref[0, s]
        segment = segment + (places >= bound).astype(jnp.int32)
    return segment


def block_firsts(place_ref, blocks, row_block):
    place = place_ref[0]
    return [
        pl.multiple_of((place ^ fixed_reversed(q, blocks)) * row_block, row_block)
        for q in range(blocks)
    ]


def attention_forward_kernel(*refs, pieces, weights, save):
    place_ref, lengths_ref, content_ref, shift_ref = refs[:4]
    refs = refs[4:]
    row_refs, refs = refs[:pieces], refs[pieces:]
    weight_refs, refs = refs[:weights], refs[weights:]
    (
        table_ref,
        rows_ref, mixed_ref, prob_ref, content_rows_ref, position_rows_ref, key_ref, value_ref,
        position_ref, weight, hi_ref, next_ref, own_ref,
        table, qkv, semaphores,
    ) = refs
    row_count, heads = mixed_ref.shape
    head_count, head_size = content_ref.shape
    row_block = row_count // pieces
    window = row_count + row_block
    copies = Copies(semaphores)
    rows_copies = copies.stack(row_refs, rows_ref)
    everything = slice(0, weight.shape[1])
    weight_copies_ = copies.weight(weight_refs, weight, everything)
    table_copy = copies.start(table_ref, table)
    firsts = block_firsts(place_ref, pieces, row_block)
    wait(rows_copies + weight_copies_)
    save(0, 8)

    @tiles(3 * heads)
    def _(columns):
        qkv[:, columns] = matmul(rows_ref[...], weight[:, columns])

    table_copy.wait()

    @tiles(table.shape[0])
    def _(places):
        position_ref[places, :] = matmul(
            table[places, :], weight[:, 3 * heads : 4 * heads]
        ).astype(LOW)

    for q in range(pieces):
        rows = pl.ds(q * row_block, row_block)
        key_ref[pl.ds(firsts[q], row_block), :] = qkv[rows, heads : 2 * heads].astype(LOW)
        value_ref[pl.ds(firsts[q], row_block), :] = qkv[rows, 2 * heads :].astype(LOW)

    save(5, 6, 7)

    along = lax.broadcasted_iota(jnp.int32, (1, row_count), 1)
    column_segment = segment_of(lengths_ref, along)
    for q in range(pieces):
        rows = pl.ds(q * row_block, row_block)
        down = lax.broadcasted_iota(jnp.int32, (row_block, 1), 0) + firsts[q]
        matching = segment_of(lengths_ref, down) == column_segment
        for h in range(head_count):
            columns = slice(h * head_size, (h + 1) * head_size)
            query = qkv[rows, columns]
            with_content = (query + content_ref[h : h + 1, :]).astype(LOW)
            with_position = (query + shift_ref[h : h + 1, :]).astype(LOW)
            content_rows_ref[rows, columns] = with_content
            position_rows_ref[rows, columns] = with_position
            direct = times_transposed(with_content, key_ref[:, columns])
            relative = relative_window(position_ref, firsts[q], row_block, columns)[...]
            broad = times_transposed(with_position, relative)
            broad = pltpu.roll(
                broad, window - (row_block - 1), axis=1, stride=1, stride_axis=0
            )
            scores = (direct + broad[:, :row_count]) * head_size ** (-0.5)
            scores = jnp.where(matching, scores, -1e30)
            exponent = jnp.exp(scores - jnp.max(scores, axis=1, keepdims=True))
            prob = (exponent / jnp.sum(exponent, axis=1, keepdims=True)).astype(LOW)
            prob_ref[h, rows, :] = prob
            mixed_ref[rows, columns] = matmul(prob, value_ref[:, columns]).astype(LOW)

    save(1, 2, 3, 4)

    @tiles(weight.shape[0])
    def _(features):
        write_parts(
            hi_ref, next_ref, own_ref, features,
            times_transposed(mixed_ref[...], weight[features, 4 * heads : 5 * heads]),
        )


def attention_forward(place, lengths, rows, weights, table, content_bias, position_bias):
    row_count, features = len(rows) * rows[0].shape[0], rows[0].shape[1]
    head_count, head_size = content_bias.shape
    heads = head_count * head_size
    row_array = ((row_count, heads), LOW)
    return call(
        functools.partial(attention_forward_kernel, pieces=len(rows), weights=len(weights)),
        [
            ((row_count, features), LOW), row_array,
            ((head_count, row_count, row_count), LOW),
            row_array, row_array, row_array, row_array,
            ((2 * row_count, heads), LOW), ((features, 5 * heads), LOW),
        ]
        + row_parts(row_count, features),
        [
            pltpu.VMEM(table.shape, LOW),
            pltpu.VMEM((row_count, 3 * heads), FLOAT),
            pltpu.SemaphoreType.DMA((len(rows) + len(weights) + 1,)),
        ],
        12 * row_count * features * heads + 9 * heads * row_count**2,
        ("smem", place), ("smem", lengths),
        ("vmem", content_bias), ("vmem", position_bias),
        *[("any", array) for array in list(rows) + list(weights)],
        ("hbm", table),
        saved=tuple(range(9)), room=54,
    )


def attention_backward_kernel(*refs, pieces, weights, head_count, save):
    place_ref, refs = refs[0], refs[1:]
    row_refs, refs = refs[:pieces], refs[pieces:]
    weight_refs, refs = refs[:weights], refs[weights:]
    (
        position_ref, prob_ref, content_rows_ref, position_rows_ref, key_ref, value_ref,
        rows_ref, qkv_grad_ref, position_grad_ref, bias_grad_ref, hi_ref, next_ref, own_ref,
        weight, mixed_grad_ref, key_sum, value_sum, position_sum, semaphores,
    ) = refs
    row_count, heads = mixed_grad_ref.shape
    head_size = heads // head_count
    row_block = row_count // pieces
    scale = head_size ** (-0.5)
    copies = Copies(semaphores)
    rows_copies = copies.stack(row_refs, rows_ref)
    everything = slice(0, weight.shape[1])
    weight_copies_ = copies.weight(weight_refs, weight, everything)
    firsts = block_firsts(place_ref, pieces, row_block)
    key_sum[...] = jnp.zeros_like(key_sum)
    value_sum[...] = jnp.zeros_like(value_sum)
    position_sum[...] = jnp.zeros_like(position_sum)
    turn = (
        lax.broadcasted_iota(jnp.int32, (row_block, row_block), 0)
        + lax.broadcasted_iota(jnp.int32, (row_block, row_block), 1)
        == row_block - 1
    ).astype(LOW)
    wait(rows_copies + weight_copies_)
    save(0)
    mixed_grad_ref[...] = matmul(rows_ref[...], weight[:, 4 * heads : 5 * heads]).astype(LOW)
    for h in range(head_count):
        columns = slice(h * head_size, (h + 1) * head_size)
        content_total = jnp.zeros((1, head_size), FLOAT)
        position_total = jnp.zeros((1, head_size), FLOAT)
        for q in range(pieces):
            rows = pl.ds(q * row_block, row_block)
            mixed_grad = mixed_grad_ref[rows, columns]
            prob = prob_ref[h, rows, :]
            prob_float = prob.astype(FLOAT)
            prob_grad = times_transposed(mixed_grad, value_ref[:, columns])
            inner = jnp.sum(prob_grad * prob_float, axis=1, keepdims=True)
            score_grad = (prob_float * (prob_grad - inner)).astype(LOW)
            value_sum[:, columns] += outer_sum(prob, mixed_grad)
            key_sum[:, columns] += outer_sum(score_grad, content_rows_ref[rows, columns])
            turned = matmul(turn, score_grad).astype(LOW)
            content_part = matmul(turned, key_ref[:, columns]) * scale
            broad = jnp.concatenate([turned, jnp.zeros((row_block, row_block), LOW)], axis=1)
            broad = pltpu.roll(broad, 0, axis=1, stride=1, stride_axis=0)
            relative = relative_window(position_ref, firsts[q], row_block, columns)[...]
            position_part = matmul(broad, relative) * scale
            turned_rows = matmul(turn, position_rows_ref[rows, columns]).astype(LOW)
            total_ref = relative_window(position_sum, firsts[q], row_block, columns)
            total_ref[...] += outer_sum(broad, turned_rows)
            query_grad = (content_part + position_part).astype(LOW)
            qkv_grad_ref[rows, columns] = matmul(turn, query_grad).astype(LOW)
            content_total += jnp.sum(content_part, axis=0, keepdims=True)
            position_total += jnp.sum(position_part, axis=0, keepdims=True)
        bias_grad_ref[h : h + 1, :] = content_total
        bias_grad_ref[head_count + h : head_count + h + 1, :] = position_total
    for q in range(pieces):
        rows, plain = pl.ds(q * row_block, row_block), pl.ds(firsts[q], row_block)
        qkv_grad_ref[rows, heads : 2 * heads] = (key_sum[plain, :] * scale).astype(LOW)
        qkv_grad_ref[rows, 2 * heads :] = value_sum[plain, :].astype(LOW)
    position_grad_ref[...] = (position_sum[...] * scale).astype(LOW)

    save(1, 2)

    @tiles(weight.shape[0])
    def _(features):
        write_parts(
            hi_ref, next_ref, own_ref, features,
            times_transposed(qkv_grad_ref[...], weight[features, : 3 * heads]),
        )


def attention_backward(place, rows, weights, stored, head_count):
    row_count, features = len(rows) * rows[0].shape[0], rows[0].shape[1]
    position = stored[0]
    heads = position.shape[1]
    return call(
        functools.partial(
            attention_backward_kernel, pieces=len(rows), weights=len(weights),
            head_count=head_count,
        ),
        [
            ((row_count, features), LOW),
            ((row_count, 3 * heads), LOW),
            (position.shape, LOW),
            ((2 * head_count, heads // head_count), FLOAT),
        ]
        + row_parts(row_count, features),
        [
            pltpu.VMEM((features, 5 * heads), LOW),
            pltpu.VMEM((row_count, heads), LOW),
            pltpu.VMEM((row_count, heads), FLOAT),
            pltpu.VMEM((row_count, heads), FLOAT),
            pltpu.VMEM(position.shape, FLOAT),
            pltpu.SemaphoreType.DMA((len(rows) + len(weights),)),
        ],
        8 * row_count * features * heads + 16 * heads * row_count**2,
        ("smem", place),
        *[("any", array) for array in rows],
        *[("any" if len(weights) > 1 else "hbm", array) for array in weights],
        *[("vmem", array) for array in stored],
        saved=(0, 1, 2),
    )


MARGIN = 8


def conv_matches(lengths_ref, row_count, taps):
    places = lax.broadcasted_iota(jnp.int32, (row_count, 1), 0)
    segment = segment_of(lengths_ref, places)
    valid = (segment < lengths_ref.shape[1]).astype(FLOAT)
    matches = []
    for t in range(taps):
        other = segment_of(lengths_ref, places + (t - taps // 2))
        matches.append((other == segment).astype(FLOAT))
    return valid, matches


def conv_lift_kernel(*refs, pieces, weights, save):
    place_ref, lengths_ref, taps_ref = refs[:3]
    refs = refs[3:]
    row_refs, refs = refs[:pieces], refs[pieces:]
    weight_refs, refs = refs[:weights], refs[weights:]
    rows_ref, lifted_ref, weight, convolved_ref, sums_ref, padded, semaphores = refs
    row_count, channels = convolved_ref.shape
    taps = taps_ref.shape[0]
    row_block = row_count // pieces
    copies = Copies(semaphores)
    rows_copies = copies.stack(row_refs, rows_ref)
    weight_copies_ = copies.weight(weight_refs, weight, slice(0, 3 * channels))
    firsts = block_firsts(place_ref, pieces, row_block)
    valid, matches = conv_matches(lengths_ref, row_count, taps)
    padded[:MARGIN, :] = jnp.zeros((MARGIN, channels), FLOAT)
    padded[MARGIN + row_count :, :] = jnp.zeros((MARGIN, channels), FLOAT)
    wait(rows_copies + weight_copies_)
    save(0, 2)
    lifted = matmul(rows_ref[...], weight[:, : 2 * channels])
    for q in range(pieces):
        lifted_ref[pl.ds(firsts[q], row_block), :] = lifted[q * row_block : (q + 1) * row_block]
    gated = lifted_ref[:, :channels] * jax.nn.sigmoid(lifted_ref[:, channels:]) * valid
    padded[MARGIN : MARGIN + row_count, :] = gated
    convolved = jnp.zeros((row_count, channels), FLOAT)
    for t in range(taps):
        first = MARGIN + t - taps // 2
        convolved += taps_ref[t : t + 1, :] * matches[t] * padded[first : first + row_count, :]
    convolved_ref[...] = convolved
    save(1)

    masked = convolved * valid
    sums_ref[...] = jnp.zeros_like(sums_ref)
    sums_ref[0:1, :] = jnp.sum(masked, axis=0, keepdims=True)
    sums_ref[1:2, :] = jnp.sum(masked * convolved, axis=0, keepdims=True)
    sums_ref[2:3, :] = jnp.zeros((1, channels), FLOAT) + jnp.sum(valid, axis=0, keepdims=True)


def conv_lift(place, lengths, taps, rows, weights):
    row_count, features = len(rows) * rows[0].shape[0], rows[0].shape[1]
    channels = taps.shape[1]
    return call(
        functools.partial(conv_lift_kernel, pieces=len(rows), weights=len(weights)),
        [
            ((row_count, features), LOW),
            ((row_count, 2 * channels), FLOAT),
            ((features, 3 * channels), LOW),
            ((row_count, channels), FLOAT),
            ((8, channels), FLOAT),
        ],
        [
            pltpu.VMEM((row_count + 2 * MARGIN, channels), FLOAT),
            pltpu.SemaphoreType.DMA((len(rows) + len(weights),)),
        ],
        4 * row_count * features * channels,
        ("smem", place), ("smem", lengths), ("vmem", taps),
        *[("any", array) for array in rows],
        *[("any" if len(weights) > 1 else "hbm", array) for array in weights],
        saved=(0, 1, 2), room=54,
    )


def batch_scales(sums_ref):
    count = sums_ref[2:3, :]
    average = sums_ref[0:1, :] / count
    return count, average, lax.rsqrt(sums_ref[1:2, :] / count - average * average + EPSILON)


def conv_out_kernel(*refs, pieces, weights, save):
    place_ref, lengths_ref, affine_ref, sums_ref, convolved_ref = refs[:5]
    refs = refs[5:]
    weight_refs, refs = refs[:weights], refs[weights:]
    swished_ref, hi_ref, next_ref, own_ref, weight, plain, semaphores = refs
    row_count, channels = convolved_ref.shape
    row_block = row_count // pieces
    copies = Copies(semaphores)
    weight_copies_ = copies.weight(
        weight_refs, weight, slice(2 * channels, 3 * channels)
    )
    firsts = block_firsts(place_ref, pieces, row_block)
    places = lax.broadcasted_iota(jnp.int32, (row_count, 1), 0)
    valid = (segment_of(lengths_ref, places) < lengths_ref.shape[1]).astype(FLOAT)
    _, average, inverse = batch_scales(sums_ref)
    hatted = (convolved_ref[...] - average) * inverse
    normalized = hatted * affine_ref[0:1, :] + affine_ref[1:2, :]
    plain[...] = (normalized * jax.nn.sigmoid(normalized) * valid).astype(LOW)
    for q in range(pieces):
        swished_ref[q * row_block : (q + 1) * row_block, :] = plain[
            pl.ds(firsts[q], row_block), :
        ]
    save(0)

    wait(weight_copies_)

    @tiles(weight.shape[0])
    def _(features):
        write_parts(
            hi_ref, next_ref, own_ref, features, times_transposed(swished_ref[...], weight[features, :])
        )


def conv_out(place, lengths, affine, sums, convolved, weights, pieces, features):
    row_count, channels = convolved.shape
    return call(
        functools.partial(conv_out_kernel, pieces=pieces, weights=len(weights)),
        [((row_count, channels), LOW)] + row_parts(row_count, features),
        [
            pltpu.VMEM((features, channels), LOW),
            pltpu.VMEM((row_count, channels), LOW),
            pltpu.SemaphoreType.DMA((len(weights),)),
        ],
        2 * row_count * features * channels,
        ("smem", place), ("smem", lengths),
        ("vmem", affine), ("vmem", sums), ("vmem", convolved),
        *[("any" if len(weights) > 1 else "hbm", array) for array in weights],
        saved=(0,), room=50,
    )


def conv_back_sums_kernel(*refs, pieces, weights, save):
    place_ref, lengths_ref, affine_ref, sums_ref, convolved_ref = refs[:5]
    refs = refs[5:]
    row_refs, refs = refs[:pieces], refs[pieces:]
    weight_refs, refs = refs[:weights], refs[weights:]
    rows_ref, normal_ref, back_ref, weight, plain, semaphores = refs
    row_count, channels = convolved_ref.shape
    row_block = row_count // pieces
    copies = Copies(semaphores)
    rows_copies = copies.stack(row_refs, rows_ref)
    weight_copies_ = copies.weight(
        weight_refs, weight, slice(2 * channels, 3 * channels)
    )
    firsts = block_firsts(place_ref, pieces, row_block)
    places = lax.broadcasted_iota(jnp.int32, (row_count, 1), 0)
    valid = (segment_of(lengths_ref, places) < lengths_ref.shape[1]).astype(FLOAT)
    _, average, inverse = batch_scales(sums_ref)
    hatted = (convolved_ref[...] - average) * inverse
    normalized = hatted * affine_ref[0:1, :] + affine_ref[1:2, :]
    squashed = jax.nn.sigmoid(normalized)
    wait(rows_copies + weight_copies_)
    product = matmul(rows_ref[...], weight[...])
    for q in range(pieces):
        plain[pl.ds(firsts[q], row_block), :] = product[q * row_block : (q + 1) * row_block]
    save(0)

    normal = plain[...] * valid * squashed * (1.0 + normalized * (1.0 - squashed))
    normal_ref[...] = normal
    back_ref[...] = jnp.zeros_like(back_ref)
    back_ref[0:1, :] = jnp.sum(normal, axis=0, keepdims=True)
    back_ref[1:2, :] = jnp.sum(normal * hatted, axis=0, keepdims=True)


def conv_back_sums(place, lengths, affine, sums, convolved, rows, weights):
    row_count, channels = convolved.shape
    features = rows[0].shape[1]
    return call(
        functools.partial(conv_back_sums_kernel, pieces=len(rows), weights=len(weights)),
        [
            ((row_count, features), LOW), ((row_count, channels), FLOAT), ((8, channels), FLOAT)
        ],
        [
            pltpu.VMEM((features, channels), LOW),
            pltpu.VMEM((row_count, channels), FLOAT),
            pltpu.SemaphoreType.DMA((len(rows) + len(weights),)),
        ],
        2 * row_count * features * channels,
        ("smem", place), ("smem", lengths),
        ("vmem", affine), ("vmem", sums), ("vmem", convolved),
        *[("any", array) for array in rows],
        *[("any" if len(weights) > 1 else "hbm", array) for array in weights],
        saved=(0,),
    )


def conv_back_kernel(*refs, pieces, weights, save):
    (
        place_ref, lengths_ref, taps_ref, affine_ref, sums_ref, back_ref,
        convolved_ref, normal_ref, lifted_ref,
    ) = refs[:9]
    refs = refs[9:]
    weight_refs, refs = refs[:weights], refs[weights:]
    lifted_grad_ref, taps_grad_ref, hi_ref, next_ref, own_ref, weight, padded, padded_grad, plain, semaphores = refs
    row_count, channels = convolved_ref.shape
    taps = taps_ref.shape[0]
    row_block = row_count // pieces
    copies = Copies(semaphores)
    weight_copies_ = copies.weight(weight_refs, weight, slice(0, 2 * channels))
    firsts = block_firsts(place_ref, pieces, row_block)
    valid, matches = conv_matches(lengths_ref, row_count, taps)
    count, average, inverse = batch_scales(sums_ref)
    gain = affine_ref[0:1, :]
    hatted = (convolved_ref[...] - average) * inverse
    conv_grad = inverse * (
        normal_ref[...] * gain
        - valid * gain * (back_ref[0:1, :] + hatted * back_ref[1:2, :]) / count
    )
    value = lifted_ref[:, :channels]
    gate = jax.nn.sigmoid(lifted_ref[:, channels:])
    for scratch in (padded, padded_grad):
        scratch[:MARGIN, :] = jnp.zeros((MARGIN, channels), FLOAT)
        scratch[MARGIN + row_count :, :] = jnp.zeros((MARGIN, channels), FLOAT)
    padded[MARGIN : MARGIN + row_count, :] = value * gate * valid
    padded_grad[MARGIN : MARGIN + row_count, :] = conv_grad
    taps_grad_ref[...] = jnp.zeros_like(taps_grad_ref)
    gated_grad = jnp.zeros((row_count, channels), FLOAT)
    for t in range(taps):
        offset = t - taps // 2
        read = padded[MARGIN + offset : MARGIN + offset + row_count, :]
        taps_grad_ref[t : t + 1, :] = jnp.sum(
            matches[t] * read * conv_grad, axis=0, keepdims=True
        )
        back = padded_grad[MARGIN - offset : MARGIN - offset + row_count, :]
        gated_grad += taps_ref[t : t + 1, :] * matches[taps - 1 - t] * back
    gated_grad = gated_grad * valid
    plain[:, :channels] = (gated_grad * gate).astype(LOW)
    plain[:, channels:] = (gated_grad * value * gate * (1.0 - gate)).astype(LOW)
    for q in range(pieces):
        lifted_grad_ref[q * row_block : (q + 1) * row_block, :] = plain[
            pl.ds(firsts[q], row_block), :
        ]
    save(0)

    wait(weight_copies_)

    @tiles(weight.shape[0])
    def _(features):
        write_parts(
            hi_ref, next_ref, own_ref, features,
            times_transposed(lifted_grad_ref[...], weight[features, :]),
        )


def conv_back(
    place, lengths, taps, affine, sums, back, convolved, normal, lifted, weights, pieces,
    features,
):
    row_count, channels = convolved.shape
    return call(
        functools.partial(conv_back_kernel, pieces=pieces, weights=len(weights)),
        [((row_count, 2 * channels), LOW), ((8, channels), FLOAT)] + row_parts(row_count, features),
        [
            pltpu.VMEM((features, 2 * channels), LOW),
            pltpu.VMEM((row_count + 2 * MARGIN, channels), FLOAT),
            pltpu.VMEM((row_count + 2 * MARGIN, channels), FLOAT),
            pltpu.VMEM((row_count, 2 * channels), LOW),
            pltpu.SemaphoreType.DMA((len(weights),)),
        ],
        4 * row_count * features * channels,
        ("smem", place), ("smem", lengths),
        *[
            ("vmem", array)
            for array in (taps, affine, sums, back, convolved, normal, lifted)
        ],
        *[("any" if len(weights) > 1 else "hbm", array) for array in weights],
        saved=(0,),
    )


def standardize(values):
    average = jnp.mean(values, axis=-1, keepdims=True)
    centred = values - average
    spread_of = jnp.mean(centred * centred, axis=-1, keepdims=True)
    scale = lax.rsqrt(spread_of + EPSILON)
    return centred * scale, scale


def norm_back(values, norm_gain, normed_grad):
    hat, scale = standardize(values)
    gained = normed_grad * norm_gain
    first = jnp.mean(gained, axis=-1, keepdims=True)
    second = jnp.mean(gained * hat, axis=-1, keepdims=True)
    grad = (gained - first - hat * second) * scale
    return grad, jnp.sum(normed_grad * hat, axis=0, keepdims=True)


def middle_kernel(next_ref, arrived_ref, sent_ref):
    first = next_ref.shape[0]
    sent_ref[...] = (
        next_ref[...].astype(FLOAT) + arrived_ref[first:, :].astype(FLOAT)
    ).astype(LOW)


def sum_rows(hi, next_part, own_part):
    arrived = swap(hi, "mp", 1)
    (sent,) = call(
        middle_kernel, [(next_part.shape, LOW)], [], next_part.size,
        ("vmem", next_part), ("vmem", arrived),
    )
    return (own_part, arrived, swap(sent, "mp", 2)), sent


def summed(own_ref, near_ref, far_ref):
    rows = own_ref.shape[0]
    return own_ref[...] + near_ref[:rows, :].astype(FLOAT) + far_ref[...].astype(FLOAT)


def all_rows(own):
    across = swap(own, "mp", 2)
    return [own, across, swap(own, "mp", 1), swap(across, "mp", 1)]


def step_kernel(
    own_ref, near_ref, far_ref, residual_ref, gain_ref, next_ref, normed_ref, *, factor
):
    residual = residual_ref[...].astype(FLOAT) + factor * summed(own_ref, near_ref, far_ref)
    next_ref[...] = residual
    normed_ref[...] = (standardize(residual)[0] * gain_ref[...]).astype(LOW)


def step(parts, residual, gain, factor):
    shape = parts[0].shape
    return call(
        functools.partial(step_kernel, factor=factor), [(shape, FLOAT), (shape, LOW)], [],
        8 * math.prod(shape),
        *[("vmem", array) for array in (*parts, residual, gain)],
    )


def turn_kernel(
    own_ref, near_ref, far_ref, residual_ref, gain_ref, out_grad_ref,
    result_ref, grad_ref, branch_ref, gain_grad_ref,
):
    residual = residual_ref[...] + 0.5 * summed(own_ref, near_ref, far_ref)
    gain = gain_ref[...]
    result_ref[...] = (standardize(residual)[0] * gain).astype(LOW)
    grad, gain_grad = norm_back(residual, gain, out_grad_ref[...].astype(FLOAT))
    grad_ref[...] = grad
    branch_ref[...] = (0.5 * grad).astype(LOW)
    gain_grad_ref[...] = gain_grad


def turn(parts, residual, gain, out_grad):
    shape = parts[0].shape
    return call(
        turn_kernel,
        [(shape, LOW), (shape, FLOAT), (shape, LOW), ((1, shape[1]), FLOAT)], [],
        16 * math.prod(shape),
        *[("vmem", array) for array in (*parts, residual, gain, out_grad)],
    )


def step_back_kernel(
    own_ref, near_ref, far_ref, residual_ref, gain_ref, grad_ref,
    next_ref, branch_ref, gain_grad_ref, *, factor,
):
    normed_grad = summed(own_ref, near_ref, far_ref)
    grad, gain_grad = norm_back(residual_ref[...].astype(FLOAT), gain_ref[...], normed_grad)
    grad = grad_ref[...] + grad
    next_ref[...] = grad
    branch_ref[...] = (factor * grad).astype(LOW)
    gain_grad_ref[...] = gain_grad


def step_back(parts, residual, gain, grad, factor):
    shape = parts[0].shape
    return call(
        functools.partial(step_back_kernel, factor=factor),
        [(shape, FLOAT), (shape, LOW), ((1, shape[1]), FLOAT)], [],
        16 * math.prod(shape),
        *[("vmem", array) for array in (*parts, residual, gain, grad)],
    )


def select_kernel(place_ref, *refs):
    pieces, target_ref = refs[:-1], refs[-1]
    row_block = pieces[0].shape[0]
    for piece, first in zip(pieces, block_firsts(place_ref, len(pieces), row_block)):
        target_ref[pl.ds(first, row_block), :] = piece[...].astype(target_ref.dtype)


def select_rows(place, pieces, kind):
    row_block, features = pieces[0].shape
    (outcome,) = call(
        select_kernel, [((len(pieces) * row_block, features), kind)], [], 0,
        ("smem", place), *[("vmem", piece) for piece in pieces], limit=16,
    )
    return outcome


def finish_kernel(*refs, counts):
    sources, targets = refs[: 2 * len(counts)], refs[2 * len(counts) :]
    at = 0
    for i, count in enumerate(counts):
        total = sources[2 * i][...] + sources[2 * i + 1][...].astype(FLOAT)
        first = 0
        for target in targets[at : at + count]:
            last = first + target.shape[1]
            target[...] = total[:, first:last]
            first = last
        at += count


def finish(sums, widths, *tokens):
    rows = sums[0].kept.shape[0]
    parts, counts, left = [], [], list(widths)
    for part in sums:
        parts += [("vmem", part.kept), ("vmem", after(part.sent, *tokens))]
        count, total = 0, 0
        while total < part.kept.shape[1]:
            total, count = total + left.pop(0), count + 1
        counts.append(count)
    return call(
        functools.partial(finish_kernel, counts=tuple(counts)),
        [((rows, width), FLOAT) for width in widths], [], 0, *parts,
    )


def join_kernel(*refs):
    target, first = refs[-1], 0
    for kept, arrived in zip(refs[0:-1:2], refs[1:-1:2]):
        last = first + kept.shape[1]
        target[:, first:last] = kept[...] + arrived[...].astype(FLOAT)
        first = last


def join(sums):
    rows, width = sums[0].kept.shape[0], sum(part.kept.shape[1] for part in sums)
    parts = []
    for part in sums:
        parts += [("vmem", part.kept), ("vmem", part.sent)]
    return call(join_kernel, [((rows, width), FLOAT)], [], 0, *parts)[0]


def per_device(
    inputs,
    lengths,
    out_grad,
    first_norm,
    first_up,
    first_down,
    attention_norm,
    query_weight,
    key_weight,
    value_weight,
    position_weight,
    output_weight,
    content_bias,
    position_bias,
    convolution_norm,
    pointwise_in,
    depthwise_kernel,
    batch_gain,
    batch_shift,
    pointwise_out,
    second_norm,
    second_up,
    second_down,
    final_norm,
):
    row_count, feature_count = inputs.shape
    dp_size, mp_size = lax.axis_size("dp"), lax.axis_size("mp")
    dp_at, mp_at = lax.axis_index("dp"), lax.axis_index("mp")
    block, hidden = first_up.shape
    row_block = row_count // mp_size
    bias_rows, head_count = content_bias.shape
    head_size = bias_rows * dp_size
    heads = head_count * head_size
    local_channels, tap_count = depthwise_kernel.shape
    channels = local_channels * dp_size
    place = mp_at.reshape(1).astype(jnp.int32)

    places = jnp.arange(feature_count, dtype=jnp.int32)
    owners = dp_at ^ reversed_bits(places // block, dp_size)
    source = owners * block + places % block
    selection = (places[:, None] == source[None, :]).astype(LOW)
    block_places = jnp.arange(dp_size, dtype=jnp.int32)
    block_owners = (dp_at ^ reversed_bits(block_places, dp_size)).astype(jnp.int32)
    block_selection = (block_places[:, None] == block_owners[None, :]).astype(LOW)

    up_own = first_up.astype(LOW)
    small_own = jnp.concatenate(
        [
            part.reshape(-1)
            for part in (
                first_norm, attention_norm, convolution_norm, second_norm, final_norm,
                content_bias, position_bias, depthwise_kernel, batch_gain, batch_shift,
            )
        ]
    )
    small_own = after(small_own, up_own).astype(LOW)
    links = Links(4)
    up_spread = Spread(links, up_own)
    up_spread.go(ORDER)
    ups = up_spread.blocks
    down_own = after(first_down, ups[1]).astype(LOW)
    down_spread = Spread(links, down_own)
    down_spread.go(ORDER)
    downs = down_spread.blocks
    gates, mask = [downs[1], ups[5], ups[3]], dp_size // 2
    small_all = small_own[None]
    while mask:
        arrived = swap(small_all, "dp", mask)
        if gates:
            arrived = after(arrived, gates.pop())
        small_all = jnp.concatenate([small_all, arrived], axis=0)
        mask //= 2

    attention_own = jnp.concatenate(
        after(
            (query_weight, key_weight, value_weight, position_weight, output_weight), ups[3]
        ),
        axis=1,
    ).astype(LOW)
    attention_spread = Spread(links, attention_own)
    attention_spread.go(ORDER[:3], time=10)
    pointwise_in, pointwise_out, second_up, second_down = after(
        (pointwise_in, pointwise_out, second_up, second_down), ups[2]
    )
    convolution_own = jnp.concatenate(
        [pointwise_in.reshape(block, 2 * channels), pointwise_out], axis=1
    ).astype(LOW)
    second_own = jnp.concatenate([second_up, second_down], axis=1).astype(LOW)

    whole, first_half, second_half = (
        slice(0, hidden), slice(0, hidden), slice(hidden, 2 * hidden)
    )

    norms = small_all[:, : 5 * block].astype(FLOAT).reshape(dp_size, 5, block)
    norms = norms.transpose(1, 0, 2).reshape(5, 1, feature_count)
    first_gain, attention_gain, convolution_gain, second_gain, final_gain = norms
    plain_small = matmul(block_selection, small_all[:, 5 * block :])
    cut = bias_rows * head_count
    content_all = plain_small[:, :cut].reshape(head_size, head_count).T
    position_all = plain_small[:, cut : 2 * cut].reshape(head_size, head_count).T
    at = 2 * cut + local_channels * tap_count
    taps = plain_small[:, 2 * cut : at].reshape(channels, tap_count).T
    affine = jnp.stack(
        [
            plain_small[:, at : at + local_channels].reshape(channels),
            plain_small[:, at + local_channels :].reshape(channels),
        ]
    )

    arranged = matmul(
        jnp.concatenate(
            [
                lax.dynamic_slice_in_dim(
                    inputs, (mp_at ^ fixed_reversed(q, mp_size)) * row_block, row_block, axis=0
                )
                for q in range(mp_size)
            ],
            axis=0,
        ),
        selection,
    )
    own_out_grad = matmul(
        lax.dynamic_slice_in_dim(out_grad, mp_at * row_block, row_block, axis=0), selection
    ).astype(LOW)
    table_places = after(jnp.arange(2 * row_count, dtype=jnp.int32), ups[3])
    sin_table = position_table(table_places, row_count, feature_count)
    sin_table = matmul(sin_table, selection).astype(LOW)

    residual_zero = arranged[:row_block].astype(LOW)
    hat_a = standardize(arranged)[0]
    normed_a = (hat_a * first_gain).astype(LOW)
    hat_a = hat_a.astype(LOW)
    _, before_a, active_a, up_a, down_a, hi, next_part, own_part = ffn_call(
        ffn_forward_kernel, [normed_a], ups, downs, whole, whole, room=54
    )
    attention_spread.go((3, 5), hi, time=3)
    parts, sent = sum_rows(hi, next_part, own_part)
    attention_spread.go((6,), sent, time=10)
    attention_spread.go((7,), parts[2], time=10)
    attention_all = attention_spread.blocks
    convolution_spread = Spread(links, after(convolution_own, sent))
    convolution_spread.go(ORDER[:3], time=10)
    residual_one, own_b = step(parts, residual_zero, attention_gain, 0.5)
    second_spread = Spread(links, after(second_own, sent))

    (
        normed_b, mixed_rows, prob, content_rows, position_rows, keys, values, position,
        attention_weight, hi, next_part, own_part,
    ) = attention_forward(
        place, lengths, all_rows(own_b), attention_all, sin_table, content_all,
        position_all,
    )
    parts, sent = sum_rows(hi, next_part, own_part)
    convolution_spread.go((3, 5, 6), sent, time=10)
    convolution_spread.go((7,), sent, time=10)
    convolution_all = convolution_spread.blocks
    second_spread.go(ORDER[:3], time=10)
    residual_two, own_c = step(parts, residual_one, convolution_gain, 1.0)
    rows = all_rows(own_c)

    normed_c, lifted, convolution_weight, convolved, sums = conv_lift(
        place, lengths, taps, rows, convolution_all
    )
    second_spread.go(ORDER[3:5], sums, time=10)
    sums, _ = total_hops(sums, "dp")
    second_spread.go(ORDER[5:], sums, time=10)
    swished, hi, next_part, own_part = conv_out(
        place, lengths, affine, sums, convolved, [convolution_weight], mp_size,
        feature_count,
    )
    parts, sent = sum_rows(hi, next_part, own_part)
    residual_three, own_d = step(parts, residual_two, second_gain, 1.0)
    second_all = second_spread.blocks

    normed_d, before_d, active_d, up_d, down_d, hi, next_part, own_part = ffn_call(
        ffn_forward_kernel, all_rows(own_d), second_all, second_all, first_half,
        second_half, room=50,
    )
    parts, sent = sum_rows(hi, next_part, own_part)
    own_result, residual_grad, branch, final_gain_grad = turn(
        parts, residual_three, final_gain, own_out_grad
    )

    branch_rows, before_grad, hi, next_part, own_part = ffn_call(
        ffn_backward_kernel, all_rows(branch), [up_d], [down_d], whole, whole, before_d,
    )
    links = Links(3, apart=True)
    parts, sent = sum_rows(hi, next_part, own_part)
    second_down_sum = WeightSum((after(branch_rows, sent), active_d))
    second_down_sum.advance(links=links)
    residual_grad, branch, second_gain_grad = step_back(
        parts, residual_three, second_gain, residual_grad, 1.0
    )
    second_up_sum = WeightSum((after(normed_d, branch), before_grad))

    branch_rows, normal, back_sums = conv_back_sums(
        place, lengths, affine, sums, convolved, all_rows(branch), [convolution_weight]
    )
    back_sums, hops = total_hops(back_sums, "dp")
    second_down_sum.advance(hops[-2], links=links)
    second_up_sum.advance(hops[-1], links=links)
    lifted_grad, taps_grad, hi, next_part, own_part = conv_back(
        place, lengths, taps, affine, sums, back_sums, convolved, normal, lifted,
        [convolution_weight], mp_size, feature_count,
    )
    parts, sent = sum_rows(hi, next_part, own_part)
    convolution_sum = WeightSum(
        (normed_c, after(lifted_grad, sent)), (branch_rows, after(swished, sent))
    )
    convolution_sum.advance(links=links)
    residual_grad, branch, convolution_gain_grad = step_back(
        parts, residual_two, convolution_gain, residual_grad, 1.0
    )
    second_down_sum.advance(branch, links=links)
    first_row = dp_at * local_channels
    gain_piece = lax.dynamic_slice_in_dim(back_sums[1], first_row, local_channels)
    shift_piece = lax.dynamic_slice_in_dim(back_sums[0], first_row, local_channels)

    rows = all_rows(branch)
    rows[0] = after(rows[0], second_down_sum.upper)
    branch_rows, qkv_grad, position_grad, bias_grads, hi, next_part, own_part = attention_backward(
        place, rows, [attention_weight],
        (position, prob, content_rows, position_rows, keys, values), head_count,
    )
    parts, sent = sum_rows(hi, next_part, own_part)
    second_up_sum.advance(sent, links=links)
    residual_grad, branch, attention_gain_grad = step_back(
        parts, residual_one, attention_gain, residual_grad, 0.5
    )
    attention_sum = WeightSum(
        (normed_b, after(qkv_grad, sent)), (sin_table, after(position_grad, sent)),
        (branch_rows, after(mixed_rows, sent)),
    )
    attention_later = []
    attention_sum.advance(links=links, later=attention_later)
    convolution_sum.advance(branch, links=links)

    bias_grads, taps_grad = after((bias_grads, taps_grad), branch)
    plain_grads = jnp.concatenate(
        [
            bias_grads[:head_count].T.reshape(dp_size, cut),
            bias_grads[head_count:].T.reshape(dp_size, cut),
            taps_grad[:tap_count].T.reshape(dp_size, local_channels * tap_count),
        ],
        axis=1,
    )
    plain_grads = lax.dot_general(
        block_selection.astype(FLOAT), plain_grads, (((0,), (0,)), ((), ())),
        precision=lax.Precision.HIGHEST, preferred_element_type=FLOAT,
    )

    branch_rows, before_grad, hi, next_part, own_part, gain_grads = ffn_call(
        ffn_backward_kernel, all_rows(branch), [up_a], [down_a], whole, whole, before_a,
        (
            hat_a, attention_gain_grad, convolution_gain_grad, second_gain_grad, final_gain_grad
        ),
    )
    attention_later.append(hi)
    first_down_sum = WeightSum((branch_rows, active_a))
    first_up_sum = WeightSum((normed_a, before_grad))

    parts, sent = sum_rows(hi, next_part, own_part)
    first_down_sum.advance(later=(sent,))
    first_up_sum.advance(first_down_sum.upper, later=(sent,))
    convolution_sum.advance(first_down_sum.upper)
    second_up_sum.advance(first_down_sum.upper)
    attention_sum.advance()
    residual_grad, _, _ = step_back(
        after(parts, attention_sum.upper), residual_zero, first_gain, residual_grad, 1.0
    )
    inputs_rows = all_rows(
        times_transposed(residual_grad.astype(LOW), selection).astype(LOW)
    )
    result_rows = all_rows(
        times_transposed(after(own_result, parts[2]), selection).astype(LOW)
    )
    first_down_sum.advance(attention_sum.upper)

    attention_sum.advance(
        first_down_sum.upper, convolution_sum.sent, second_up_sum.sent, second_down_sum.sent
    )
    gain_grads, plain_grads = after((gain_grads, plain_grads), attention_sum.upper)
    mask, small_hops = 1, []
    while 4 * mask < dp_size:
        width, count = gain_grads.shape[1] // 2, plain_grads.shape[0] // 2
        small_hops.append(
            (swap(gain_grads[:, width:], "dp", mask), swap(plain_grads[count:], "dp", mask))
        )
        if 8 * mask < dp_size:
            gain_grads = gain_grads[:, :width] + small_hops[-1][0]
            plain_grads = plain_grads[:count] + small_hops[-1][1]
        mask *= 2

    first_down_sum.advance(attention_sum.upper)
    first_up_sum.advance(first_down_sum.upper, inputs_rows[3], result_rows[3])

    arrived = after(small_hops[-1], first_up_sum.upper)
    gain_grads = gain_grads[:, :width] + arrived[0]
    plain_grads = plain_grads[:count] + arrived[1]
    arrived = []
    masks = (dp_size // 2, dp_size // 4, 3 * dp_size // 4)
    for p, mask in enumerate(masks):
        columns = slice((p + 1) * block, (p + 2) * block)
        arrived.append(
            (
                swap(gain_grads[:, columns], "dp", mask),
                swap(plain_grads[p + 1 : p + 2], "dp", mask),
            )
        )
    gain_grads, plain_grads = gain_grads[:, :block], plain_grads[:1]

    last_hop = first_up_sum.sent
    first_up_sum.advance(attention_sum.sent, first_down_sum.sent)
    arrived = after(arrived, first_up_sum.upper)
    for gain_hop, plain_hop in arrived:
        gain_grads = gain_grads + gain_hop
        plain_grads = plain_grads + plain_hop
    for part in (
        second_down_sum, second_up_sum, convolution_sum, attention_sum, first_down_sum,
        first_up_sum,
    ):
        part.rest()

    second_down_grad, second_up_grad, convolution_in_grad, convolution_out_grad = finish(
        [second_down_sum, second_up_sum, convolution_sum],
        [hidden, hidden, 2 * channels, channels], last_hop,
    )
    attention_grads = finish([attention_sum], [heads] * 5, last_hop)
    first_down_grad = join([first_down_sum])

    result = select_rows(place, after(result_rows, first_up_sum.upper), LOW)
    inputs_grad = select_rows(place, after(inputs_rows, first_up_sum.upper), FLOAT)
    first_up_sum.kept = after(first_up_sum.kept, result, inputs_grad, first_down_grad)
    first_up_grad = join([first_up_sum])

    gain_grads, plain_grads = total_over(gain_grads, "mp"), plain_grads[0]

    return (
        result,
        inputs_grad,
        gain_grads[0],
        first_up_grad,
        first_down_grad,
        gain_grads[1],
        *attention_grads,
        plain_grads[:cut].reshape(bias_rows, head_count),
        plain_grads[cut : 2 * cut].reshape(bias_rows, head_count),
        gain_grads[2],
        convolution_in_grad.reshape(block, 2, channels),
        plain_grads[2 * cut :].reshape(local_channels, tap_count),
        gain_piece,
        shift_piece,
        convolution_out_grad,
        gain_grads[3],
        second_up_grad,
        second_down_grad,
        gain_grads[4],
    )


def solution(mesh):
    return jax.shard_map(
        per_device,
        mesh=mesh,
        in_specs=(
            P("dp", None),
            P("dp", None),
            P("dp", None),
            P("dp"),
            P("dp", "mp"),
            P("dp", "mp"),
            P("dp"),
            P("dp", "mp"),
            P("dp", "mp"),
            P("dp", "mp"),
            P("dp", "mp"),
            P("dp", "mp"),
            P("dp", "mp"),
            P("dp", "mp"),
            P("dp"),
            P("dp", None, "mp"),
            P(("mp", "dp"), None),
            P(("mp", "dp")),
            P(("mp", "dp")),
            P("dp", "mp"),
            P("dp"),
            P("dp", "mp"),
            P("dp", "mp"),
            P("dp"),
        ),
        out_specs=(
            P("dp", None),
            P("dp", None),
            P("dp"),
            P("dp", "mp"),
            P("dp", "mp"),
            P("dp"),
            P("dp", "mp"),
            P("dp", "mp"),
            P("dp", "mp"),
            P("dp", "mp"),
            P("dp", "mp"),
            P("dp", "mp"),
            P("dp", "mp"),
            P("dp"),
            P("dp", None, "mp"),
            P(("mp", "dp"), None),
            P(("mp", "dp")),
            P(("mp", "dp")),
            P("dp", "mp"),
            P("dp"),
            P("dp", "mp"),
            P("dp", "mp"),
            P("dp"),
        ),
        check_vma=False,
    )
```

```python
import functools
import math

import jax
import jax.numpy as jnp
from jax import lax
from jax.experimental import pallas as pl
from jax.experimental.pallas import tpu as pltpu
from jax.sharding import PartitionSpec as P

EPSILON = 1e-05
LOW = jnp.bfloat16
FLOAT = jnp.float32


def matmul(left_side, right_side):
    return jnp.dot(left_side, right_side, preferred_element_type=FLOAT)


def times_transposed(left_side, right_side):
    return lax.dot_general(
        left_side, right_side, (((1,), (1,)), ((), ())), preferred_element_type=FLOAT
    )


def outer_sum(left_side, right_side):
    return lax.dot_general(
        left_side, right_side, (((0,), (0,)), ((), ())), preferred_element_type=FLOAT
    )


def reversed_bits(places, size):
    outcome = places * 0
    mask, back = size // 2, 1
    while mask:
        outcome = outcome + ((places // back) % 2) * mask
        mask, back = mask // 2, back * 2
    return outcome


def swap(values, axis, mask):
    size = lax.axis_size(axis)
    return lax.ppermute(values, axis, [(i, i ^ mask) for i in range(size)])


def after(values, *tokens):
    return lax.optimization_barrier((values, tokens))[0] if tokens else values


class Links:
    def __init__(self, depth, apart=False):
        self.depth, self.apart, self.queues = depth, apart, {}

    def swap(self, values, mask, time=None):
        queue, depth = self.queues.setdefault(self.apart and mask == 1, []), self.depth
        if len(queue) >= depth:
            values = after(values, *queue[-2 * depth : len(queue) + 1 - depth])
        arrived = swap(values, "dp", mask)
        queue.append(arrived if time is None else held(arrived, time))
        return queue[-1]


ORDER = (4, 1, 2, 3, 5, 6, 7)


def pass_kernel(source_ref, target_ref):
    pass


def held(values, microseconds):
    return pl.pallas_call(
        pass_kernel,
        out_shape=jax.ShapeDtypeStruct(values.shape, values.dtype),
        in_specs=[pl.BlockSpec(memory_space=pl.ANY)],
        out_specs=pl.BlockSpec(memory_space=pl.ANY),
        input_output_aliases={0: 0},
        cost_estimate=pl.CostEstimate(
            flops=int(1.1e9 * microseconds), bytes_accessed=0, transcendentals=0
        ),
    )(values)


class Spread:
    def __init__(self, links, own):
        self.links, self.mask = links, lax.axis_size("dp") // 2
        while self.mask > 4:
            own = jnp.concatenate([own, links.swap(own, self.mask)], axis=0)
            self.mask //= 2
        self.blocks = [own] + [None] * (2 * self.mask - 1)

    def go(self, places, *tokens, time=None):
        for p in places:
            if p < len(self.blocks):
                top = 1 << (p.bit_length() - 1)
                self.blocks[p] = self.links.swap(
                    after(self.blocks[p - top], *tokens), self.mask // top,
                    time if p < 4 or time is None else 10,
                )


def spread(values, axis):
    mask = lax.axis_size(axis) // 2
    while mask:
        values = jnp.concatenate([values, swap(values, axis, mask)], axis=0)
        mask //= 2
    return values


def collect(values, axis, wire, mask=1):
    while mask < lax.axis_size(axis):
        half = values.shape[0] // 2
        values = values[:half] + swap(values[half:].astype(wire), axis, mask).astype(FLOAT)
        mask *= 2
    return values


def total_over(values, axis):
    mask = 1
    while mask < lax.axis_size(axis):
        values = values + swap(values, axis, mask)
        mask *= 2
    return values


def total_hops(values, axis):
    arrivals, mask = [], lax.axis_size(axis) // 2
    while mask:
        arrivals.append(swap(values, axis, mask))
        values = values + arrivals[-1]
        mask //= 2
    return values, arrivals


class WeightSum:
    def __init__(self, *pairs):
        self.pairs, self.mask = pairs, 0

    def advance(self, *tokens, links=None, later=()):
        if not self.mask:
            half = self.pairs[0][0].shape[1] // 2
            upper = [outer_sum(left[:, half:], right).astype(LOW) for left, right in self.pairs]
            self.later = later
            self.upper, self.mask = after(jnp.concatenate(upper, axis=1), *tokens), 1
        else:
            if self.mask == 1 << 1:
                lower = [
                    outer_sum(after(left, *self.later)[:, : left.shape[1] // 2], right)
                    for left, right in self.pairs
                ]
                self.kept = jnp.concatenate(lower, axis=1)
            total = self.kept + after(self.sent, *tokens).astype(FLOAT)
            half = total.shape[0] // 2
            self.upper, self.kept = total[half:].astype(LOW), total[:half]
        if links is None:
            self.sent = swap(self.upper, "dp", self.mask)
        else:
            self.sent = links.swap(self.upper, self.mask)
        self.mask *= 2

    def rest(self, *tokens):
        while self.mask < lax.axis_size("dp"):
            self.advance(*tokens)


def position_table(places, row_count, feature_count):
    rates = jnp.exp(
        jnp.arange(0, feature_count, 2).astype(FLOAT) * (-math.log(10000.0) / feature_count)
    )
    stride = 32
    count = places.shape[0] // stride
    coarse = (row_count - 1 - stride * places[:count]).astype(FLOAT)[:, None] * rates[None, :]
    fine = -places[:stride].astype(FLOAT)[:, None] * rates[None, :]
    coarse_sin, coarse_cos = jnp.sin(coarse)[:, None], jnp.cos(coarse)[:, None]
    fine_sin, fine_cos = jnp.sin(fine)[None], jnp.cos(fine)[None]
    sines = coarse_sin * fine_cos + coarse_cos * fine_sin
    cosines = coarse_cos * fine_cos - coarse_sin * fine_sin
    table = jnp.concatenate([sines, cosines], axis=2).astype(LOW)
    return table.reshape(places.shape[0], feature_count)


def fixed_reversed(place, size):
    outcome, mask = 0, size // 2
    while mask:
        outcome, place, mask = outcome + (place % 2) * mask, place // 2, mask // 2
    return outcome


def relative_window(position_ref, first, row_block, columns):
    row_count = position_ref.shape[0] // 2
    start = pl.multiple_of(row_count - row_block - first, row_block)
    return position_ref.at[pl.ds(start, row_count + row_block), columns]


def in_smem():
    return pl.BlockSpec(memory_space=pltpu.SMEM)


def in_vmem():
    return pl.BlockSpec(memory_space=pltpu.VMEM)


def in_hbm():
    return pl.BlockSpec(memory_space=pltpu.HBM)


def anywhere():
    return pl.BlockSpec(memory_space=pl.ANY)


def call(kernel, outs, scratch, flops, *operands, limit=6, room=50, saved=()):
    places = dict(smem=in_smem, vmem=in_vmem, any=anywhere, hbm=in_hbm)
    count, inner = len(operands), len(scratch)

    def saving(*refs):
        sources, targets, rest = (
            refs[:count], list(refs[count : count + len(outs)]), refs[count + len(outs) :]
        )
        kept, held_refs, semaphores = rest[:inner], rest[inner:-1], rest[-1]
        copies = [
            pltpu.make_async_copy(ref, targets[i], semaphores.at[n])
            for n, (i, ref) in enumerate(zip(saved, held_refs))
        ]
        for i, ref in zip(saved, held_refs):
            targets[i] = ref

        def save(*which):
            for n in which:
                copies[n].start()

        kernel(*sources, *targets, *kept, save=save)
        for copy in copies:
            copy.wait()

    extra = []
    if saved:
        extra = [pltpu.VMEM(*outs[i]) for i in saved] + [pltpu.SemaphoreType.DMA((len(saved),))]
    return pl.pallas_call(
        saving if saved else kernel,
        out_shape=tuple(jax.ShapeDtypeStruct(shape, kind) for shape, kind in outs),
        in_specs=[places[place]() for place, _ in operands],
        out_specs=tuple(in_hbm() if i in saved else in_vmem() for i in range(len(outs))),
        scratch_shapes=list(scratch) + extra,
        compiler_params=pltpu.CompilerParams(
            vmem_limit_bytes=(room if scratch else limit) * 2**20
        ),
        cost_estimate=pl.CostEstimate(flops=flops, bytes_accessed=0, transcendentals=0),
    )(*[array for _, array in operands])


class Copies:
    def __init__(self, semaphores):
        self.semaphores, self.count = semaphores, 0

    def start(self, source, target):
        copy = pltpu.make_async_copy(source, target, self.semaphores.at[self.count])
        copy.start()
        self.count += 1
        return copy

    def stack(self, sources, target, columns=None):
        copies, block = [], target.shape[0] // len(sources)
        for p, source in enumerate(sources):
            if columns is not None:
                source = source.at[:, columns]
            copies.append(self.start(source, target.at[pl.ds(p * block, block)]))
        return copies

    def weight(self, sources, target, columns):
        if len(sources) > 1:
            return self.stack(sources, target, columns)
        return [self.start(sources[0].at[:, columns], target)]


def wait(copies):
    for copy in copies:
        copy.wait()


TILE = 256


def write_parts(hi_ref, next_ref, own_ref, columns, product):
    half, own = hi_ref.shape[0], own_ref.shape[0]
    hi_ref[:, columns] = product[half:].astype(LOW)
    next_ref[:, columns] = product[own:half].astype(LOW)
    own_ref[:, columns] = product[:own]


def tiles(count):
    def loop(body):
        @pl.loop(0, count // TILE)
        def _(t):
            body(pl.ds(pl.multiple_of(t * TILE, TILE), TILE))

    return loop


def ffn_forward_kernel(*refs, pieces, weights, up_columns, down_columns, save):
    row_refs, refs = refs[:pieces], refs[pieces:]
    up_refs, refs = refs[:weights], refs[weights:]
    down_refs, refs = refs[:weights], refs[weights:]
    rows_ref, before_ref, active_ref, up, down, hi_ref, next_ref, own_ref, semaphores = refs
    copies = Copies(semaphores)
    rows_copies = copies.stack(row_refs, rows_ref)
    up_copies = copies.weight(up_refs, up, up_columns)
    down_copies = copies.weight(down_refs, down, down_columns)
    wait(rows_copies + up_copies)
    save(0, 3)

    @tiles(up.shape[1])
    def _(columns):
        before = matmul(rows_ref[...], up[:, columns])
        before_ref[:, columns] = before.astype(LOW)
        active_ref[:, columns] = (before * jax.nn.sigmoid(before)).astype(LOW)

    save(1, 2)
    wait(down_copies)
    save(4)

    @tiles(down.shape[0])
    def _(features):
        write_parts(
            hi_ref, next_ref, own_ref, features, times_transposed(active_ref[...], down[features, :])
        )


def ffn_backward_kernel(*refs, pieces, weights, up_columns, down_columns, gains, save):
    if gains:
        (hat_ref, *others), gain_grad_ref, refs = (
            refs[-9 - gains : -9], refs[-4], refs[: -9 - gains] + refs[-9:-4] + refs[-3:]
        )
        gain_grad_ref[...] = jnp.zeros_like(gain_grad_ref)
        for n, other in enumerate(others):
            gain_grad_ref[n + 1 : n + 2, :] = other[...]
    row_refs, refs = refs[:pieces], refs[pieces:]
    up_refs, refs = refs[:weights], refs[weights:]
    down_refs, refs = refs[:weights], refs[weights:]
    before_ref, rows_ref, grad_ref, hi_ref, next_ref, own_ref, up, down, semaphores = refs
    copies = Copies(semaphores)
    rows_copies = copies.stack(row_refs, rows_ref)
    down_copies = copies.weight(down_refs, down, down_columns)
    up_copies = copies.weight(up_refs, up, up_columns)
    wait(rows_copies + down_copies)
    save(0)

    @tiles(down.shape[1])
    def _(columns):
        before = before_ref[:, columns].astype(FLOAT)
        squashed = jax.nn.sigmoid(before)
        grad = matmul(rows_ref[...], down[:, columns])
        grad_ref[:, columns] = (grad * squashed * (1.0 + before * (1.0 - squashed))).astype(LOW)

    save(1)

    wait(up_copies)

    @tiles(up.shape[0])
    def _(features):
        product = times_transposed(grad_ref[...], up[features, :])
        write_parts(hi_ref, next_ref, own_ref, features, product)
        if gains:
            gain_grad_ref[0:1, features] = jnp.sum(
                product * hat_ref[:, features].astype(FLOAT), axis=0, keepdims=True
            )


def row_parts(rows, features):
    return [
        ((rows // 2, features), LOW), ((rows // 4, features), LOW), ((rows // 4, features), FLOAT)
    ]


def ffn_call(
    kernel, rows, ups, downs, up_columns, down_columns, before=None, hats=(), room=50
):
    row_count = len(rows) * rows[0].shape[0]
    features = rows[0].shape[1]
    hidden = up_columns.stop - up_columns.start
    outs = [((row_count, features), LOW)]
    outs += [((row_count, hidden), LOW)] * (2 if before is None else 1)
    weight = ((features, hidden), LOW)
    if before is None:
        outs += [weight] * 2
    count = len(rows) + 2 * len(ups)
    operands = [("any", array) for array in rows]
    operands += [("any" if len(ups) > 1 else "hbm", array) for array in list(ups) + list(downs)]
    if before is not None:
        operands.append(("vmem", before))
        kernel = functools.partial(kernel, gains=len(hats))
    outs += row_parts(row_count, features)
    if hats:
        operands += [("vmem", array) for array in hats]
        outs.append(((8, features), FLOAT))
    return call(
        functools.partial(
            kernel, pieces=len(rows), weights=len(ups), up_columns=up_columns,
            down_columns=down_columns,
        ),
        outs,
        [pltpu.VMEM(*weight)] * (0 if before is None else 2)
        + [pltpu.SemaphoreType.DMA((count,))],
        4 * row_count * features * hidden,
        *operands,
        saved=(0, 1, 2, 3, 4) if before is None else (0, 1), room=room,
    )


def segment_of(lengths_ref, places):
    bound, segment = 0, jnp.zeros(places.shape, jnp.int32)
    for s in range(lengths_ref.shape[1]):
        bound = bound + lengths_ref[0, s]
        segment = segment + (places >= bound).astype(jnp.int32)
    return segment


def block_firsts(place_ref, blocks, row_block):
    place = place_ref[0]
    return [
        pl.multiple_of((place ^ fixed_reversed(q, blocks)) * row_block, row_block)
        for q in range(blocks)
    ]


def attention_forward_kernel(*refs, pieces, weights, save):
    place_ref, lengths_ref, content_ref, shift_ref = refs[:4]
    refs = refs[4:]
    row_refs, refs = refs[:pieces], refs[pieces:]
    weight_refs, refs = refs[:weights], refs[weights:]
    (
        table_ref,
        rows_ref, mixed_ref, prob_ref, content_rows_ref, position_rows_ref, key_ref, value_ref,
        position_ref, weight, hi_ref, next_ref, own_ref,
        table, qkv, semaphores,
    ) = refs
    row_count, heads = mixed_ref.shape
    head_count, head_size = content_ref.shape
    row_block = row_count // pieces
    window = row_count + row_block
    copies = Copies(semaphores)
    rows_copies = copies.stack(row_refs, rows_ref)
    everything = slice(0, weight.shape[1])
    weight_copies_ = copies.weight(weight_refs, weight, everything)
    table_copy = copies.start(table_ref, table)
    firsts = block_firsts(place_ref, pieces, row_block)
    wait(rows_copies + weight_copies_)
    save(0, 8)

    @tiles(3 * heads)
    def _(columns):
        qkv[:, columns] = matmul(rows_ref[...], weight[:, columns])

    table_copy.wait()

    @tiles(table.shape[0])
    def _(places):
        position_ref[places, :] = matmul(
            table[places, :], weight[:, 3 * heads : 4 * heads]
        ).astype(LOW)

    for q in range(pieces):
        rows = pl.ds(q * row_block, row_block)
        key_ref[pl.ds(firsts[q], row_block), :] = qkv[rows, heads : 2 * heads].astype(LOW)
        value_ref[pl.ds(firsts[q], row_block), :] = qkv[rows, 2 * heads :].astype(LOW)

    save(5, 6, 7)

    along = lax.broadcasted_iota(jnp.int32, (1, row_count), 1)
    column_segment = segment_of(lengths_ref, along)
    for q in range(pieces):
        rows = pl.ds(q * row_block, row_block)
        down = lax.broadcasted_iota(jnp.int32, (row_block, 1), 0) + firsts[q]
        matching = segment_of(lengths_ref, down) == column_segment
        for h in range(head_count):
            columns = slice(h * head_size, (h + 1) * head_size)
            query = qkv[rows, columns]
            with_content = (query + content_ref[h : h + 1, :]).astype(LOW)
            with_position = (query + shift_ref[h : h + 1, :]).astype(LOW)
            content_rows_ref[rows, columns] = with_content
            position_rows_ref[rows, columns] = with_position
            direct = times_transposed(with_content, key_ref[:, columns])
            relative = relative_window(position_ref, firsts[q], row_block, columns)[...]
            broad = times_transposed(with_position, relative)
            broad = pltpu.roll(
                broad, window - (row_block - 1), axis=1, stride=1, stride_axis=0
            )
            scores = (direct + broad[:, :row_count]) * head_size ** (-0.5)
            scores = jnp.where(matching, scores, -1e30)
            exponent = jnp.exp(scores - jnp.max(scores, axis=1, keepdims=True))
            prob = (exponent / jnp.sum(exponent, axis=1, keepdims=True)).astype(LOW)
            prob_ref[h, rows, :] = prob
            mixed_ref[rows, columns] = matmul(prob, value_ref[:, columns]).astype(LOW)

    save(1, 2, 3, 4)

    @tiles(weight.shape[0])
    def _(features):
        write_parts(
            hi_ref, next_ref, own_ref, features,
            times_transposed(mixed_ref[...], weight[features, 4 * heads : 5 * heads]),
        )


def attention_forward(place, lengths, rows, weights, table, content_bias, position_bias):
    row_count, features = len(rows) * rows[0].shape[0], rows[0].shape[1]
    head_count, head_size = content_bias.shape
    heads = head_count * head_size
    row_array = ((row_count, heads), LOW)
    return call(
        functools.partial(attention_forward_kernel, pieces=len(rows), weights=len(weights)),
        [
            ((row_count, features), LOW), row_array,
            ((head_count, row_count, row_count), LOW),
            row_array, row_array, row_array, row_array,
            ((2 * row_count, heads), LOW), ((features, 5 * heads), LOW),
        ]
        + row_parts(row_count, features),
        [
            pltpu.VMEM(table.shape, LOW),
            pltpu.VMEM((row_count, 3 * heads), FLOAT),
            pltpu.SemaphoreType.DMA((len(rows) + len(weights) + 1,)),
        ],
        12 * row_count * features * heads + 9 * heads * row_count**2,
        ("smem", place), ("smem", lengths),
        ("vmem", content_bias), ("vmem", position_bias),
        *[("any", array) for array in list(rows) + list(weights)],
        ("hbm", table),
        saved=tuple(range(9)), room=54,
    )


def attention_backward_kernel(*refs, pieces, weights, head_count, save):
    place_ref, refs = refs[0], refs[1:]
    row_refs, refs = refs[:pieces], refs[pieces:]
    weight_refs, refs = refs[:weights], refs[weights:]
    (
        position_ref, prob_ref, content_rows_ref, position_rows_ref, key_ref, value_ref,
        rows_ref, qkv_grad_ref, position_grad_ref, bias_grad_ref, hi_ref, next_ref, own_ref,
        weight, mixed_grad_ref, key_sum, value_sum, position_sum, semaphores,
    ) = refs
    row_count, heads = mixed_grad_ref.shape
    head_size = heads // head_count
    row_block = row_count // pieces
    scale = head_size ** (-0.5)
    copies = Copies(semaphores)
    rows_copies = copies.stack(row_refs, rows_ref)
    everything = slice(0, weight.shape[1])
    weight_copies_ = copies.weight(weight_refs, weight, everything)
    firsts = block_firsts(place_ref, pieces, row_block)
    key_sum[...] = jnp.zeros_like(key_sum)
    value_sum[...] = jnp.zeros_like(value_sum)
    position_sum[...] = jnp.zeros_like(position_sum)
    turn = (
        lax.broadcasted_iota(jnp.int32, (row_block, row_block), 0)
        + lax.broadcasted_iota(jnp.int32, (row_block, row_block), 1)
        == row_block - 1
    ).astype(LOW)
    wait(rows_copies + weight_copies_)
    save(0)
    mixed_grad_ref[...] = matmul(rows_ref[...], weight[:, 4 * heads : 5 * heads]).astype(LOW)
    for h in range(head_count):
        columns = slice(h * head_size, (h + 1) * head_size)
        content_total = jnp.zeros((1, head_size), FLOAT)
        position_total = jnp.zeros((1, head_size), FLOAT)
        for q in range(pieces):
            rows = pl.ds(q * row_block, row_block)
            mixed_grad = mixed_grad_ref[rows, columns]
            prob = prob_ref[h, rows, :]
            prob_float = prob.astype(FLOAT)
            prob_grad = times_transposed(mixed_grad, value_ref[:, columns])
            inner = jnp.sum(prob_grad * prob_float, axis=1, keepdims=True)
            score_grad = (prob_float * (prob_grad - inner)).astype(LOW)
            value_sum[:, columns] += outer_sum(prob, mixed_grad)
            key_sum[:, columns] += outer_sum(score_grad, content_rows_ref[rows, columns])
            turned = matmul(turn, score_grad).astype(LOW)
            content_part = matmul(turned, key_ref[:, columns]) * scale
            broad = jnp.concatenate([turned, jnp.zeros((row_block, row_block), LOW)], axis=1)
            broad = pltpu.roll(broad, 0, axis=1, stride=1, stride_axis=0)
            relative = relative_window(position_ref, firsts[q], row_block, columns)[...]
            position_part = matmul(broad, relative) * scale
            turned_rows = matmul(turn, position_rows_ref[rows, columns]).astype(LOW)
            total_ref = relative_window(position_sum, firsts[q], row_block, columns)
            total_ref[...] += outer_sum(broad, turned_rows)
            query_grad = (content_part + position_part).astype(LOW)
            qkv_grad_ref[rows, columns] = matmul(turn, query_grad).astype(LOW)
            content_total += jnp.sum(content_part, axis=0, keepdims=True)
            position_total += jnp.sum(position_part, axis=0, keepdims=True)
        bias_grad_ref[h : h + 1, :] = content_total
        bias_grad_ref[head_count + h : head_count + h + 1, :] = position_total
    for q in range(pieces):
        rows, plain = pl.ds(q * row_block, row_block), pl.ds(firsts[q], row_block)
        qkv_grad_ref[rows, heads : 2 * heads] = (key_sum[plain, :] * scale).astype(LOW)
        qkv_grad_ref[rows, 2 * heads :] = value_sum[plain, :].astype(LOW)
    position_grad_ref[...] = (position_sum[...] * scale).astype(LOW)

    save(1, 2)

    @tiles(weight.shape[0])
    def _(features):
        write_parts(
            hi_ref, next_ref, own_ref, features,
            times_transposed(qkv_grad_ref[...], weight[features, : 3 * heads]),
        )


def attention_backward(place, rows, weights, stored, head_count):
    row_count, features = len(rows) * rows[0].shape[0], rows[0].shape[1]
    position = stored[0]
    heads = position.shape[1]
    return call(
        functools.partial(
            attention_backward_kernel, pieces=len(rows), weights=len(weights),
            head_count=head_count,
        ),
        [
            ((row_count, features), LOW),
            ((row_count, 3 * heads), LOW),
            (position.shape, LOW),
            ((2 * head_count, heads // head_count), FLOAT),
        ]
        + row_parts(row_count, features),
        [
            pltpu.VMEM((features, 5 * heads), LOW),
            pltpu.VMEM((row_count, heads), LOW),
            pltpu.VMEM((row_count, heads), FLOAT),
            pltpu.VMEM((row_count, heads), FLOAT),
            pltpu.VMEM(position.shape, FLOAT),
            pltpu.SemaphoreType.DMA((len(rows) + len(weights),)),
        ],
        8 * row_count * features * heads + 16 * heads * row_count**2,
        ("smem", place),
        *[("any", array) for array in rows],
        *[("any" if len(weights) > 1 else "hbm", array) for array in weights],
        *[("vmem", array) for array in stored],
        saved=(0, 1, 2),
    )


MARGIN = 8


def conv_matches(lengths_ref, row_count, taps):
    places = lax.broadcasted_iota(jnp.int32, (row_count, 1), 0)
    segment = segment_of(lengths_ref, places)
    valid = (segment < lengths_ref.shape[1]).astype(FLOAT)
    matches = []
    for t in range(taps):
        other = segment_of(lengths_ref, places + (t - taps // 2))
        matches.append((other == segment).astype(FLOAT))
    return valid, matches


def conv_lift_kernel(*refs, pieces, weights, save):
    place_ref, lengths_ref, taps_ref = refs[:3]
    refs = refs[3:]
    row_refs, refs = refs[:pieces], refs[pieces:]
    weight_refs, refs = refs[:weights], refs[weights:]
    rows_ref, lifted_ref, weight, convolved_ref, sums_ref, padded, semaphores = refs
    row_count, channels = convolved_ref.shape
    taps = taps_ref.shape[0]
    row_block = row_count // pieces
    copies = Copies(semaphores)
    rows_copies = copies.stack(row_refs, rows_ref)
    weight_copies_ = copies.weight(weight_refs, weight, slice(0, 3 * channels))
    firsts = block_firsts(place_ref, pieces, row_block)
    valid, matches = conv_matches(lengths_ref, row_count, taps)
    padded[:MARGIN, :] = jnp.zeros((MARGIN, channels), FLOAT)
    padded[MARGIN + row_count :, :] = jnp.zeros((MARGIN, channels), FLOAT)
    wait(rows_copies + weight_copies_)
    save(0, 2)
    lifted = matmul(rows_ref[...], weight[:, : 2 * channels])
    for q in range(pieces):
        lifted_ref[pl.ds(firsts[q], row_block), :] = lifted[q * row_block : (q + 1) * row_block]
    gated = lifted_ref[:, :channels] * jax.nn.sigmoid(lifted_ref[:, channels:]) * valid
    padded[MARGIN : MARGIN + row_count, :] = gated
    convolved = jnp.zeros((row_count, channels), FLOAT)
    for t in range(taps):
        first = MARGIN + t - taps // 2
        convolved += taps_ref[t : t + 1, :] * matches[t] * padded[first : first + row_count, :]
    convolved_ref[...] = convolved
    save(1)

    masked = convolved * valid
    sums_ref[...] = jnp.zeros_like(sums_ref)
    sums_ref[0:1, :] = jnp.sum(masked, axis=0, keepdims=True)
    sums_ref[1:2, :] = jnp.sum(masked * convolved, axis=0, keepdims=True)
    sums_ref[2:3, :] = jnp.zeros((1, channels), FLOAT) + jnp.sum(valid, axis=0, keepdims=True)


def conv_lift(place, lengths, taps, rows, weights):
    row_count, features = len(rows) * rows[0].shape[0], rows[0].shape[1]
    channels = taps.shape[1]
    return call(
        functools.partial(conv_lift_kernel, pieces=len(rows), weights=len(weights)),
        [
            ((row_count, features), LOW),
            ((row_count, 2 * channels), FLOAT),
            ((features, 3 * channels), LOW),
            ((row_count, channels), FLOAT),
            ((8, channels), FLOAT),
        ],
        [
            pltpu.VMEM((row_count + 2 * MARGIN, channels), FLOAT),
            pltpu.SemaphoreType.DMA((len(rows) + len(weights),)),
        ],
        4 * row_count * features * channels,
        ("smem", place), ("smem", lengths), ("vmem", taps),
        *[("any", array) for array in rows],
        *[("any" if len(weights) > 1 else "hbm", array) for array in weights],
        saved=(0, 1, 2), room=54,
    )


def batch_scales(sums_ref):
    count = sums_ref[2:3, :]
    average = sums_ref[0:1, :] / count
    return count, average, lax.rsqrt(sums_ref[1:2, :] / count - average * average + EPSILON)


def conv_out_kernel(*refs, pieces, weights, save):
    place_ref, lengths_ref, affine_ref, sums_ref, convolved_ref = refs[:5]
    refs = refs[5:]
    weight_refs, refs = refs[:weights], refs[weights:]
    swished_ref, hi_ref, next_ref, own_ref, weight, plain, semaphores = refs
    row_count, channels = convolved_ref.shape
    row_block = row_count // pieces
    copies = Copies(semaphores)
    weight_copies_ = copies.weight(
        weight_refs, weight, slice(2 * channels, 3 * channels)
    )
    firsts = block_firsts(place_ref, pieces, row_block)
    places = lax.broadcasted_iota(jnp.int32, (row_count, 1), 0)
    valid = (segment_of(lengths_ref, places) < lengths_ref.shape[1]).astype(FLOAT)
    _, average, inverse = batch_scales(sums_ref)
    hatted = (convolved_ref[...] - average) * inverse
    normalized = hatted * affine_ref[0:1, :] + affine_ref[1:2, :]
    plain[...] = (normalized * jax.nn.sigmoid(normalized) * valid).astype(LOW)
    for q in range(pieces):
        swished_ref[q * row_block : (q + 1) * row_block, :] = plain[
            pl.ds(firsts[q], row_block), :
        ]
    save(0)

    wait(weight_copies_)

    @tiles(weight.shape[0])
    def _(features):
        write_parts(
            hi_ref, next_ref, own_ref, features, times_transposed(swished_ref[...], weight[features, :])
        )


def conv_out(place, lengths, affine, sums, convolved, weights, pieces, features):
    row_count, channels = convolved.shape
    return call(
        functools.partial(conv_out_kernel, pieces=pieces, weights=len(weights)),
        [((row_count, channels), LOW)] + row_parts(row_count, features),
        [
            pltpu.VMEM((features, channels), LOW),
            pltpu.VMEM((row_count, channels), LOW),
            pltpu.SemaphoreType.DMA((len(weights),)),
        ],
        2 * row_count * features * channels,
        ("smem", place), ("smem", lengths),
        ("vmem", affine), ("vmem", sums), ("vmem", convolved),
        *[("any" if len(weights) > 1 else "hbm", array) for array in weights],
        saved=(0,), room=50,
    )


def conv_back_sums_kernel(*refs, pieces, weights, save):
    place_ref, lengths_ref, affine_ref, sums_ref, convolved_ref = refs[:5]
    refs = refs[5:]
    row_refs, refs = refs[:pieces], refs[pieces:]
    weight_refs, refs = refs[:weights], refs[weights:]
    rows_ref, normal_ref, back_ref, weight, plain, semaphores = refs
    row_count, channels = convolved_ref.shape
    row_block = row_count // pieces
    copies = Copies(semaphores)
    rows_copies = copies.stack(row_refs, rows_ref)
    weight_copies_ = copies.weight(
        weight_refs, weight, slice(2 * channels, 3 * channels)
    )
    firsts = block_firsts(place_ref, pieces, row_block)
    places = lax.broadcasted_iota(jnp.int32, (row_count, 1), 0)
    valid = (segment_of(lengths_ref, places) < lengths_ref.shape[1]).astype(FLOAT)
    _, average, inverse = batch_scales(sums_ref)
    hatted = (convolved_ref[...] - average) * inverse
    normalized = hatted * affine_ref[0:1, :] + affine_ref[1:2, :]
    squashed = jax.nn.sigmoid(normalized)
    wait(rows_copies + weight_copies_)
    product = matmul(rows_ref[...], weight[...])
    for q in range(pieces):
        plain[pl.ds(firsts[q], row_block), :] = product[q * row_block : (q + 1) * row_block]
    save(0)

    normal = plain[...] * valid * squashed * (1.0 + normalized * (1.0 - squashed))
    normal_ref[...] = normal
    back_ref[...] = jnp.zeros_like(back_ref)
    back_ref[0:1, :] = jnp.sum(normal, axis=0, keepdims=True)
    back_ref[1:2, :] = jnp.sum(normal * hatted, axis=0, keepdims=True)


def conv_back_sums(place, lengths, affine, sums, convolved, rows, weights):
    row_count, channels = convolved.shape
    features = rows[0].shape[1]
    return call(
        functools.partial(conv_back_sums_kernel, pieces=len(rows), weights=len(weights)),
        [
            ((row_count, features), LOW), ((row_count, channels), FLOAT), ((8, channels), FLOAT)
        ],
        [
            pltpu.VMEM((features, channels), LOW),
            pltpu.VMEM((row_count, channels), FLOAT),
            pltpu.SemaphoreType.DMA((len(rows) + len(weights),)),
        ],
        2 * row_count * features * channels,
        ("smem", place), ("smem", lengths),
        ("vmem", affine), ("vmem", sums), ("vmem", convolved),
        *[("any", array) for array in rows],
        *[("any" if len(weights) > 1 else "hbm", array) for array in weights],
        saved=(0,),
    )


def conv_back_kernel(*refs, pieces, weights, save):
    (
        place_ref, lengths_ref, taps_ref, affine_ref, sums_ref, back_ref,
        convolved_ref, normal_ref, lifted_ref,
    ) = refs[:9]
    refs = refs[9:]
    weight_refs, refs = refs[:weights], refs[weights:]
    lifted_grad_ref, taps_grad_ref, hi_ref, next_ref, own_ref, weight, padded, padded_grad, plain, semaphores = refs
    row_count, channels = convolved_ref.shape
    taps = taps_ref.shape[0]
    row_block = row_count // pieces
    copies = Copies(semaphores)
    weight_copies_ = copies.weight(weight_refs, weight, slice(0, 2 * channels))
    firsts = block_firsts(place_ref, pieces, row_block)
    valid, matches = conv_matches(lengths_ref, row_count, taps)
    count, average, inverse = batch_scales(sums_ref)
    gain = affine_ref[0:1, :]
    hatted = (convolved_ref[...] - average) * inverse
    conv_grad = inverse * (
        normal_ref[...] * gain
        - valid * gain * (back_ref[0:1, :] + hatted * back_ref[1:2, :]) / count
    )
    value = lifted_ref[:, :channels]
    gate = jax.nn.sigmoid(lifted_ref[:, channels:])
    for scratch in (padded, padded_grad):
        scratch[:MARGIN, :] = jnp.zeros((MARGIN, channels), FLOAT)
        scratch[MARGIN + row_count :, :] = jnp.zeros((MARGIN, channels), FLOAT)
    padded[MARGIN : MARGIN + row_count, :] = value * gate * valid
    padded_grad[MARGIN : MARGIN + row_count, :] = conv_grad
    taps_grad_ref[...] = jnp.zeros_like(taps_grad_ref)
    gated_grad = jnp.zeros((row_count, channels), FLOAT)
    for t in range(taps):
        offset = t - taps // 2
        read = padded[MARGIN + offset : MARGIN + offset + row_count, :]
        taps_grad_ref[t : t + 1, :] = jnp.sum(
            matches[t] * read * conv_grad, axis=0, keepdims=True
        )
        back = padded_grad[MARGIN - offset : MARGIN - offset + row_count, :]
        gated_grad += taps_ref[t : t + 1, :] * matches[taps - 1 - t] * back
    gated_grad = gated_grad * valid
    plain[:, :channels] = (gated_grad * gate).astype(LOW)
    plain[:, channels:] = (gated_grad * value * gate * (1.0 - gate)).astype(LOW)
    for q in range(pieces):
        lifted_grad_ref[q * row_block : (q + 1) * row_block, :] = plain[
            pl.ds(firsts[q], row_block), :
        ]
    save(0)

    wait(weight_copies_)

    @tiles(weight.shape[0])
    def _(features):
        write_parts(
            hi_ref, next_ref, own_ref, features,
            times_transposed(lifted_grad_ref[...], weight[features, :]),
        )


def conv_back(
    place, lengths, taps, affine, sums, back, convolved, normal, lifted, weights, pieces,
    features,
):
    row_count, channels = convolved.shape
    return call(
        functools.partial(conv_back_kernel, pieces=pieces, weights=len(weights)),
        [((row_count, 2 * channels), LOW), ((8, channels), FLOAT)] + row_parts(row_count, features),
        [
            pltpu.VMEM((features, 2 * channels), LOW),
            pltpu.VMEM((row_count + 2 * MARGIN, channels), FLOAT),
            pltpu.VMEM((row_count + 2 * MARGIN, channels), FLOAT),
            pltpu.VMEM((row_count, 2 * channels), LOW),
            pltpu.SemaphoreType.DMA((len(weights),)),
        ],
        4 * row_count * features * channels,
        ("smem", place), ("smem", lengths),
        *[
            ("vmem", array)
            for array in (taps, affine, sums, back, convolved, normal, lifted)
        ],
        *[("any" if len(weights) > 1 else "hbm", array) for array in weights],
        saved=(0,),
    )


def standardize(values):
    average = jnp.mean(values, axis=-1, keepdims=True)
    centred = values - average
    spread_of = jnp.mean(centred * centred, axis=-1, keepdims=True)
    scale = lax.rsqrt(spread_of + EPSILON)
    return centred * scale, scale


def norm_back(values, norm_gain, normed_grad):
    hat, scale = standardize(values)
    gained = normed_grad * norm_gain
    first = jnp.mean(gained, axis=-1, keepdims=True)
    second = jnp.mean(gained * hat, axis=-1, keepdims=True)
    grad = (gained - first - hat * second) * scale
    return grad, jnp.sum(normed_grad * hat, axis=0, keepdims=True)


def middle_kernel(next_ref, arrived_ref, sent_ref):
    first = next_ref.shape[0]
    sent_ref[...] = (
        next_ref[...].astype(FLOAT) + arrived_ref[first:, :].astype(FLOAT)
    ).astype(LOW)


def sum_rows(hi, next_part, own_part):
    arrived = swap(hi, "mp", 1)
    (sent,) = call(
        middle_kernel, [(next_part.shape, LOW)], [], next_part.size,
        ("vmem", next_part), ("vmem", arrived),
    )
    return (own_part, arrived, swap(sent, "mp", 2)), sent


def summed(own_ref, near_ref, far_ref):
    rows = own_ref.shape[0]
    return own_ref[...] + near_ref[:rows, :].astype(FLOAT) + far_ref[...].astype(FLOAT)


def all_rows(own):
    across = swap(own, "mp", 2)
    return [own, across, swap(own, "mp", 1), swap(across, "mp", 1)]


def step_kernel(
    own_ref, near_ref, far_ref, residual_ref, gain_ref, next_ref, normed_ref, *, factor
):
    residual = residual_ref[...].astype(FLOAT) + factor * summed(own_ref, near_ref, far_ref)
    next_ref[...] = residual
    normed_ref[...] = (standardize(residual)[0] * gain_ref[...]).astype(LOW)


def step(parts, residual, gain, factor):
    shape = parts[0].shape
    return call(
        functools.partial(step_kernel, factor=factor), [(shape, FLOAT), (shape, LOW)], [],
        8 * math.prod(shape),
        *[("vmem", array) for array in (*parts, residual, gain)],
    )


def turn_kernel(
    own_ref, near_ref, far_ref, residual_ref, gain_ref, out_grad_ref,
    result_ref, grad_ref, branch_ref, gain_grad_ref,
):
    residual = residual_ref[...] + 0.5 * summed(own_ref, near_ref, far_ref)
    gain = gain_ref[...]
    result_ref[...] = (standardize(residual)[0] * gain).astype(LOW)
    grad, gain_grad = norm_back(residual, gain, out_grad_ref[...].astype(FLOAT))
    grad_ref[...] = grad
    branch_ref[...] = (0.5 * grad).astype(LOW)
    gain_grad_ref[...] = gain_grad


def turn(parts, residual, gain, out_grad):
    shape = parts[0].shape
    return call(
        turn_kernel,
        [(shape, LOW), (shape, FLOAT), (shape, LOW), ((1, shape[1]), FLOAT)], [],
        16 * math.prod(shape),
        *[("vmem", array) for array in (*parts, residual, gain, out_grad)],
    )


def step_back_kernel(
    own_ref, near_ref, far_ref, residual_ref, gain_ref, grad_ref,
    next_ref, branch_ref, gain_grad_ref, *, factor,
):
    normed_grad = summed(own_ref, near_ref, far_ref)
    grad, gain_grad = norm_back(residual_ref[...].astype(FLOAT), gain_ref[...], normed_grad)
    grad = grad_ref[...] + grad
    next_ref[...] = grad
    branch_ref[...] = (factor * grad).astype(LOW)
    gain_grad_ref[...] = gain_grad


def step_back(parts, residual, gain, grad, factor):
    shape = parts[0].shape
    return call(
        functools.partial(step_back_kernel, factor=factor),
        [(shape, FLOAT), (shape, LOW), ((1, shape[1]), FLOAT)], [],
        16 * math.prod(shape),
        *[("vmem", array) for array in (*parts, residual, gain, grad)],
    )


def select_kernel(place_ref, *refs):
    pieces, target_ref = refs[:-1], refs[-1]
    row_block = pieces[0].shape[0]
    for piece, first in zip(pieces, block_firsts(place_ref, len(pieces), row_block)):
        target_ref[pl.ds(first, row_block), :] = piece[...].astype(target_ref.dtype)


def select_rows(place, pieces, kind):
    row_block, features = pieces[0].shape
    (outcome,) = call(
        select_kernel, [((len(pieces) * row_block, features), kind)], [], 0,
        ("smem", place), *[("vmem", piece) for piece in pieces], limit=16,
    )
    return outcome


def finish_kernel(*refs, counts):
    sources, targets = refs[: 2 * len(counts)], refs[2 * len(counts) :]
    at = 0
    for i, count in enumerate(counts):
        total = sources[2 * i][...] + sources[2 * i + 1][...].astype(FLOAT)
        first = 0
        for target in targets[at : at + count]:
            last = first + target.shape[1]
            target[...] = total[:, first:last]
            first = last
        at += count


def finish(sums, widths, *tokens):
    rows = sums[0].kept.shape[0]
    parts, counts, left = [], [], list(widths)
    for part in sums:
        parts += [("vmem", part.kept), ("vmem", after(part.sent, *tokens))]
        count, total = 0, 0
        while total < part.kept.shape[1]:
            total, count = total + left.pop(0), count + 1
        counts.append(count)
    return call(
        functools.partial(finish_kernel, counts=tuple(counts)),
        [((rows, width), FLOAT) for width in widths], [], 0, *parts,
    )


def join_kernel(*refs):
    target, first = refs[-1], 0
    for kept, arrived in zip(refs[0:-1:2], refs[1:-1:2]):
        last = first + kept.shape[1]
        target[:, first:last] = kept[...] + arrived[...].astype(FLOAT)
        first = last


def join(sums):
    rows, width = sums[0].kept.shape[0], sum(part.kept.shape[1] for part in sums)
    parts = []
    for part in sums:
        parts += [("vmem", part.kept), ("vmem", part.sent)]
    return call(join_kernel, [((rows, width), FLOAT)], [], 0, *parts)[0]


def per_device(
    inputs,
    lengths,
    out_grad,
    first_norm,
    first_up,
    first_down,
    attention_norm,
    query_weight,
    key_weight,
    value_weight,
    position_weight,
    output_weight,
    content_bias,
    position_bias,
    convolution_norm,
    pointwise_in,
    depthwise_kernel,
    batch_gain,
    batch_shift,
    pointwise_out,
    second_norm,
    second_up,
    second_down,
    final_norm,
):
    row_count, feature_count = inputs.shape
    dp_size, mp_size = lax.axis_size("dp"), lax.axis_size("mp")
    dp_at, mp_at = lax.axis_index("dp"), lax.axis_index("mp")
    block, hidden = first_up.shape
    row_block = row_count // mp_size
    bias_rows, head_count = content_bias.shape
    head_size = bias_rows * dp_size
    heads = head_count * head_size
    local_channels, tap_count = depthwise_kernel.shape
    channels = local_channels * dp_size
    place = mp_at.reshape(1).astype(jnp.int32)

    places = jnp.arange(feature_count, dtype=jnp.int32)
    owners = dp_at ^ reversed_bits(places // block, dp_size)
    source = owners * block + places % block
    selection = (places[:, None] == source[None, :]).astype(LOW)
    block_places = jnp.arange(dp_size, dtype=jnp.int32)
    block_owners = (dp_at ^ reversed_bits(block_places, dp_size)).astype(jnp.int32)
    block_selection = (block_places[:, None] == block_owners[None, :]).astype(LOW)

    up_own = first_up.astype(LOW)
    small_own = jnp.concatenate(
        [
            part.reshape(-1)
            for part in (
                first_norm, attention_norm, convolution_norm, second_norm, final_norm,
                content_bias, position_bias, depthwise_kernel, batch_gain, batch_shift,
            )
        ]
    )
    small_own = after(small_own, up_own).astype(LOW)
    links = Links(4)
    up_spread = Spread(links, up_own)
    up_spread.go(ORDER)
    ups = up_spread.blocks
    down_own = after(first_down, ups[1]).astype(LOW)
    down_spread = Spread(links, down_own)
    down_spread.go(ORDER)
    downs = down_spread.blocks
    gates, mask = [downs[1], ups[5], ups[3]], dp_size // 2
    small_all = small_own[None]
    while mask:
        arrived = swap(small_all, "dp", mask)
        if gates:
            arrived = after(arrived, gates.pop())
        small_all = jnp.concatenate([small_all, arrived], axis=0)
        mask //= 2

    attention_own = jnp.concatenate(
        after(
            (query_weight, key_weight, value_weight, position_weight, output_weight), ups[3]
        ),
        axis=1,
    ).astype(LOW)
    attention_spread = Spread(links, attention_own)
    attention_spread.go(ORDER[:3], time=10)
    pointwise_in, pointwise_out, second_up, second_down = after(
        (pointwise_in, pointwise_out, second_up, second_down), ups[2]
    )
    convolution_own = jnp.concatenate(
        [pointwise_in.reshape(block, 2 * channels), pointwise_out], axis=1
    ).astype(LOW)
    second_own = jnp.concatenate([second_up, second_down], axis=1).astype(LOW)

    whole, first_half, second_half = (
        slice(0, hidden), slice(0, hidden), slice(hidden, 2 * hidden)
    )

    norms = small_all[:, : 5 * block].astype(FLOAT).reshape(dp_size, 5, block)
    norms = norms.transpose(1, 0, 2).reshape(5, 1, feature_count)
    first_gain, attention_gain, convolution_gain, second_gain, final_gain = norms
    plain_small = matmul(block_selection, small_all[:, 5 * block :])
    cut = bias_rows * head_count
    content_all = plain_small[:, :cut].reshape(head_size, head_count).T
    position_all = plain_small[:, cut : 2 * cut].reshape(head_size, head_count).T
    at = 2 * cut + local_channels * tap_count
    taps = plain_small[:, 2 * cut : at].reshape(channels, tap_count).T
    affine = jnp.stack(
        [
            plain_small[:, at : at + local_channels].reshape(channels),
            plain_small[:, at + local_channels :].reshape(channels),
        ]
    )

    arranged = matmul(
        jnp.concatenate(
            [
                lax.dynamic_slice_in_dim(
                    inputs, (mp_at ^ fixed_reversed(q, mp_size)) * row_block, row_block, axis=0
                )
                for q in range(mp_size)
            ],
            axis=0,
        ),
        selection,
    )
    own_out_grad = matmul(
        lax.dynamic_slice_in_dim(out_grad, mp_at * row_block, row_block, axis=0), selection
    ).astype(LOW)
    table_places = after(jnp.arange(2 * row_count, dtype=jnp.int32), ups[3])
    sin_table = position_table(table_places, row_count, feature_count)
    sin_table = matmul(sin_table, selection).astype(LOW)

    residual_zero = arranged[:row_block].astype(LOW)
    hat_a = standardize(arranged)[0]
    normed_a = (hat_a * first_gain).astype(LOW)
    hat_a = hat_a.astype(LOW)
    _, before_a, active_a, up_a, down_a, hi, next_part, own_part = ffn_call(
        ffn_forward_kernel, [normed_a], ups, downs, whole, whole, room=54
    )
    attention_spread.go((3, 5), hi, time=3)
    parts, sent = sum_rows(hi, next_part, own_part)
    attention_spread.go((6,), sent, time=10)
    attention_spread.go((7,), parts[2], time=10)
    attention_all = attention_spread.blocks
    convolution_spread = Spread(links, after(convolution_own, sent))
    convolution_spread.go(ORDER[:3], time=10)
    residual_one, own_b = step(parts, residual_zero, attention_gain, 0.5)
    second_spread = Spread(links, after(second_own, sent))

    (
        normed_b, mixed_rows, prob, content_rows, position_rows, keys, values, position,
        attention_weight, hi, next_part, own_part,
    ) = attention_forward(
        place, lengths, all_rows(own_b), attention_all, sin_table, content_all,
        position_all,
    )
    parts, sent = sum_rows(hi, next_part, own_part)
    convolution_spread.go((3, 5, 6), sent, time=10)
    convolution_spread.go((7,), sent, time=10)
    convolution_all = convolution_spread.blocks
    second_spread.go(ORDER[:3], time=10)
    residual_two, own_c = step(parts, residual_one, convolution_gain, 1.0)
    rows = all_rows(own_c)

    normed_c, lifted, convolution_weight, convolved, sums = conv_lift(
        place, lengths, taps, rows, convolution_all
    )
    second_spread.go(ORDER[3:5], sums, time=10)
    sums, _ = total_hops(sums, "dp")
    second_spread.go(ORDER[5:], sums, time=10)
    swished, hi, next_part, own_part = conv_out(
        place, lengths, affine, sums, convolved, [convolution_weight], mp_size,
        feature_count,
    )
    parts, sent = sum_rows(hi, next_part, own_part)
    residual_three, own_d = step(parts, residual_two, second_gain, 1.0)
    second_all = second_spread.blocks

    normed_d, before_d, active_d, up_d, down_d, hi, next_part, own_part = ffn_call(
        ffn_forward_kernel, all_rows(own_d), second_all, second_all, first_half,
        second_half, room=50,
    )
    parts, sent = sum_rows(hi, next_part, own_part)
    own_result, residual_grad, branch, final_gain_grad = turn(
        parts, residual_three, final_gain, own_out_grad
    )

    branch_rows, before_grad, hi, next_part, own_part = ffn_call(
        ffn_backward_kernel, all_rows(branch), [up_d], [down_d], whole, whole, before_d,
    )
    links = Links(3, apart=True)
    parts, sent = sum_rows(hi, next_part, own_part)
    second_down_sum = WeightSum((after(branch_rows, sent), active_d))
    second_down_sum.advance(links=links)
    residual_grad, branch, second_gain_grad = step_back(
        parts, residual_three, second_gain, residual_grad, 1.0
    )
    second_up_sum = WeightSum((after(normed_d, branch), before_grad))

    branch_rows, normal, back_sums = conv_back_sums(
        place, lengths, affine, sums, convolved, all_rows(branch), [convolution_weight]
    )
    back_sums, hops = total_hops(back_sums, "dp")
    second_down_sum.advance(hops[-2], links=links)
    second_up_sum.advance(hops[-1], links=links)
    lifted_grad, taps_grad, hi, next_part, own_part = conv_back(
        place, lengths, taps, affine, sums, back_sums, convolved, normal, lifted,
        [convolution_weight], mp_size, feature_count,
    )
    parts, sent = sum_rows(hi, next_part, own_part)
    convolution_sum = WeightSum(
        (normed_c, after(lifted_grad, sent)), (branch_rows, after(swished, sent))
    )
    convolution_sum.advance(links=links)
    residual_grad, branch, convolution_gain_grad = step_back(
        parts, residual_two, convolution_gain, residual_grad, 1.0
    )
    second_down_sum.advance(branch, links=links)
    first_row = dp_at * local_channels
    gain_piece = lax.dynamic_slice_in_dim(back_sums[1], first_row, local_channels)
    shift_piece = lax.dynamic_slice_in_dim(back_sums[0], first_row, local_channels)

    rows = all_rows(branch)
    rows[0] = after(rows[0], second_down_sum.upper)
    branch_rows, qkv_grad, position_grad, bias_grads, hi, next_part, own_part = attention_backward(
        place, rows, [attention_weight],
        (position, prob, content_rows, position_rows, keys, values), head_count,
    )
    parts, sent = sum_rows(hi, next_part, own_part)
    second_up_sum.advance(sent, links=links)
    residual_grad, branch, attention_gain_grad = step_back(
        parts, residual_one, attention_gain, residual_grad, 0.5
    )
    attention_sum = WeightSum(
        (normed_b, after(qkv_grad, sent)), (sin_table, after(position_grad, sent)),
        (branch_rows, after(mixed_rows, sent)),
    )
    attention_later = []
    attention_sum.advance(links=links, later=attention_later)
    convolution_sum.advance(branch, links=links)

    bias_grads, taps_grad = after((bias_grads, taps_grad), branch)
    plain_grads = jnp.concatenate(
        [
            bias_grads[:head_count].T.reshape(dp_size, cut),
            bias_grads[head_count:].T.reshape(dp_size, cut),
            taps_grad[:tap_count].T.reshape(dp_size, local_channels * tap_count),
        ],
        axis=1,
    )
    plain_grads = lax.dot_general(
        block_selection.astype(FLOAT), plain_grads, (((0,), (0,)), ((), ())),
        precision=lax.Precision.HIGHEST, preferred_element_type=FLOAT,
    )

    branch_rows, before_grad, hi, next_part, own_part, gain_grads = ffn_call(
        ffn_backward_kernel, all_rows(branch), [up_a], [down_a], whole, whole, before_a,
        (
            hat_a, attention_gain_grad, convolution_gain_grad, second_gain_grad, final_gain_grad
        ),
    )
    attention_later.append(hi)
    first_down_sum = WeightSum((branch_rows, active_a))
    first_up_sum = WeightSum((normed_a, before_grad))

    parts, sent = sum_rows(hi, next_part, own_part)
    first_down_sum.advance(later=(sent,))
    first_up_sum.advance(first_down_sum.upper, later=(sent,))
    convolution_sum.advance(first_down_sum.upper)
    second_up_sum.advance(first_down_sum.upper)
    attention_sum.advance()
    residual_grad, _, _ = step_back(
        after(parts, attention_sum.upper), residual_zero, first_gain, residual_grad, 1.0
    )
    inputs_rows = all_rows(
        times_transposed(residual_grad.astype(LOW), selection).astype(LOW)
    )
    result_rows = all_rows(
        times_transposed(after(own_result, parts[2]), selection).astype(LOW)
    )
    first_down_sum.advance(attention_sum.upper)

    attention_sum.advance(
        first_down_sum.upper, convolution_sum.sent, second_up_sum.sent, second_down_sum.sent
    )
    gain_grads, plain_grads = after((gain_grads, plain_grads), attention_sum.upper)
    mask, small_hops = 1, []
    while 4 * mask < dp_size:
        width, count = gain_grads.shape[1] // 2, plain_grads.shape[0] // 2
        small_hops.append(
            (swap(gain_grads[:, width:], "dp", mask), swap(plain_grads[count:], "dp", mask))
        )
        if 8 * mask < dp_size:
            gain_grads = gain_grads[:, :width] + small_hops[-1][0]
            plain_grads = plain_grads[:count] + small_hops[-1][1]
        mask *= 2

    first_down_sum.advance(attention_sum.upper)
    first_up_sum.advance(first_down_sum.upper, inputs_rows[3], result_rows[3])

    arrived = after(small_hops[-1], first_up_sum.upper)
    gain_grads = gain_grads[:, :width] + arrived[0]
    plain_grads = plain_grads[:count] + arrived[1]
    arrived = []
    masks = (dp_size // 2, dp_size // 4, 3 * dp_size // 4)
    for p, mask in enumerate(masks):
        columns = slice((p + 1) * block, (p + 2) * block)
        arrived.append(
            (
                swap(gain_grads[:, columns], "dp", mask),
                swap(plain_grads[p + 1 : p + 2], "dp", mask),
            )
        )
    gain_grads, plain_grads = gain_grads[:, :block], plain_grads[:1]

    last_hop = first_up_sum.sent
    first_up_sum.advance(attention_sum.sent, first_down_sum.sent)
    arrived = after(arrived, first_up_sum.upper)
    for gain_hop, plain_hop in arrived:
        gain_grads = gain_grads + gain_hop
        plain_grads = plain_grads + plain_hop
    for part in (
        second_down_sum, second_up_sum, convolution_sum, attention_sum, first_down_sum,
        first_up_sum,
    ):
        part.rest()

    second_down_grad, second_up_grad, convolution_in_grad, convolution_out_grad = finish(
        [second_down_sum, second_up_sum, convolution_sum],
        [hidden, hidden, 2 * channels, channels], attention_sum.sent,
    )
    attention_grads = finish([attention_sum], [heads] * 5, last_hop)
    first_down_grad = join([first_down_sum])

    result = select_rows(place, after(result_rows, first_up_sum.upper), LOW)
    inputs_grad = select_rows(place, after(inputs_rows, first_up_sum.upper), FLOAT)
    first_up_sum.kept = after(first_up_sum.kept, result, inputs_grad, first_down_grad)
    first_up_grad = join([first_up_sum])

    gain_grads, plain_grads = total_over(gain_grads, "mp"), plain_grads[0]

    return (
        result,
        inputs_grad,
        gain_grads[0],
        first_up_grad,
        first_down_grad,
        gain_grads[1],
        *attention_grads,
        plain_grads[:cut].reshape(bias_rows, head_count),
        plain_grads[cut : 2 * cut].reshape(bias_rows, head_count),
        gain_grads[2],
        convolution_in_grad.reshape(block, 2, channels),
        plain_grads[2 * cut :].reshape(local_channels, tap_count),
        gain_piece,
        shift_piece,
        convolution_out_grad,
        gain_grads[3],
        second_up_grad,
        second_down_grad,
        gain_grads[4],
    )


def solution(mesh):
    return jax.shard_map(
        per_device,
        mesh=mesh,
        in_specs=(
            P("dp", None),
            P("dp", None),
            P("dp", None),
            P("dp"),
            P("dp", "mp"),
            P("dp", "mp"),
            P("dp"),
            P("dp", "mp"),
            P("dp", "mp"),
            P("dp", "mp"),
            P("dp", "mp"),
            P("dp", "mp"),
            P("dp", "mp"),
            P("dp", "mp"),
            P("dp"),
            P("dp", None, "mp"),
            P(("mp", "dp"), None),
            P(("mp", "dp")),
            P(("mp", "dp")),
            P("dp", "mp"),
            P("dp"),
            P("dp", "mp"),
            P("dp", "mp"),
            P("dp"),
        ),
        out_specs=(
            P("dp", None),
            P("dp", None),
            P("dp"),
            P("dp", "mp"),
            P("dp", "mp"),
            P("dp"),
            P("dp", "mp"),
            P("dp", "mp"),
            P("dp", "mp"),
            P("dp", "mp"),
            P("dp", "mp"),
            P("dp", "mp"),
            P("dp", "mp"),
            P("dp"),
            P("dp", None, "mp"),
            P(("mp", "dp"), None),
            P(("mp", "dp")),
            P(("mp", "dp")),
            P("dp", "mp"),
            P("dp"),
            P("dp", "mp"),
            P("dp", "mp"),
            P("dp"),
        ),
        check_vma=False,
    )
```
